256 devices in a mesh: expert: 8 (over z), vocab: 8 (over x, core), batch: 4 (over y).
Axes of the slice: x: 4, y: 4, z: 8, core: 2. Of those that a mesh axis runs over, the one named last changes fastest.
Arguments:
- resid: bfloat16 [4, 512, 6144], P('batch', ('expert', 'vocab')), may hold values from -6 to 6
- moe_gain: float32 [6144], replicated, may hold values from 0.25 to 2.5
- final_gain: float32 [6144], replicated, may hold values from 0.5 to 1.5
- router: bfloat16 [6144, 8], replicated, may hold values from -0.078125 to 0.078125
- w_gate: bfloat16 [8, 6144, 8192], P('expert', None, ('vocab', 'batch')), may hold values from -0.078125 to 0.078125
- w_up: bfloat16 [8, 6144, 8192], P('expert', None, ('vocab', 'batch')), may hold values from -0.078125 to 0.078125
- w_down: bfloat16 [8, 8192, 6144], P('expert', ('vocab', 'batch')), may hold values from -0.0625 to 0.0625
- lm_head: bfloat16 [16384, 6144], P(('expert', 'vocab')), may hold values from -6 to 6
- expert_ids: int32 [4, 512, 2], P('batch', ('expert', 'vocab')), may hold values from 0 to 7, all different within a row; in each aligned block of 8 rows (0 to 7, 8 to 15, ..., all dimensions but the last counted through in order) at most 3 rows name the same one
- target_ids: int32 [4, 512], P('batch'), may hold values from 0 to 16383
- choice_len: int32 [4, 16], P('batch'), may hold values from 1 to 64, 512 in all within a row
- choice_question: int32 [4, 16], P('batch'), may hold values from 0 to 3, as said below
Outputs:
- token_logprob: float32 [4, 512], P('batch', ('expert', 'vocab'))
- choice_prob: float32 [4, 16], P('batch')
The draws below stay inside these ranges and needn't reach their ends.
Inputs may be any that keep to these rules, and one draw needn't show every extreme that they name: `expert_ids`: A token's 2 experts differ; the rows of one device name each expert at most 3 times. `choice_len`: each group's lengths sum to 512. `choice_question`: in each group every question number appears exactly four times.
All inputs are finite; a program needn't handle non-finite values.
Results may differ from the reference program's by a relative error of at most 0.019.
Values may be sent and summed in bfloat16 or wider, within the bound.
No kernel may reach another device: no remote copies, remote signals or barrier semaphores. Data moves between devices by JAX's collectives and lax.ppermute only.
A program may use at most 128 MiB of HBM per device.

```python
import math
import jax
import jax.numpy as jnp
import numpy as np
from jax import lax

D = 6144
TOPK = 2
FF_WIN = 8192
VOC_WIN = 16384
TOK_DEV = 8
EXPERTS = 8
GROUP_TOK = 512
CHOICES = 16
MOSTLEN = 64
CAP = 3
N_EXPERT = 8
N_VOCAB = 8
N_BATCH = 4


def draw_resid(key, part):
    base_key = jax.random.fold_in(key, 707)
    values = jnp.clip(jax.random.normal(base_key, (N_BATCH * GROUP_TOK, D), jnp.float32), -6.0, 6.0)
    return values.reshape(N_BATCH, GROUP_TOK, D).astype(jnp.bfloat16)


def draw_lm_head(key, part):
    base_key = jax.random.fold_in(key, 101)
    scale = 3.0 / D ** 0.5
    table = jnp.clip(jax.random.normal(base_key, (VOC_WIN, D), jnp.float32), -6.0, 6.0) * scale
    return jnp.clip(table, -6.0, 6.0).astype(jnp.bfloat16)


def shuffled_row(row_key):
    return jax.random.permutation(row_key, CHOICES) // 4


def draw_choice_question(key, part):
    row_keys = jax.random.split(jax.random.fold_in(key, 404), N_BATCH)
    return jax.vmap(shuffled_row)(row_keys).astype(jnp.int32)


def plant(drawn, own_key, low, top_value):
    longest = drawn.shape.index(max(drawn.shape))
    spots = []
    for shift in (0, 1):
        where = [jax.random.randint(jax.random.fold_in(own_key, axis), (), 0, length) for axis, length in enumerate(drawn.shape)]
        where[longest] = (where[longest] + shift) % drawn.shape[longest]
        spots.append(tuple(where))
    return drawn.at[spots[0]].set(low).at[spots[1]].set(top_value)


def block_levels(own_key, dims, cuts, smallest, top_value):
    def one(dim, parts):
        heights = jax.random.uniform(jax.random.fold_in(jax.random.fold_in(own_key, 6), dim), (parts,), jnp.float32, smallest / len(cuts), top_value / len(cuts))
        return jnp.repeat(jnp.exp(heights), dims[dim] // parts).reshape((-1,) + (1,) * (len(dims) - dim - 1))

    level = one(*cuts[0])
    for cut in cuts[1:]:
        level = level * one(*cut)
    return level


def length_profile(amount, total, reach, slope):
    loads = [(1 << 20) // math.isqrt(grade ** slope) + 1 for grade in range(2, amount + 1)]
    surplus, given = total - reach - (amount - 1), [1] * (amount - 1)
    while surplus > 0:
        free = [i for i in range(amount - 1) if given[i] < reach]
        mass, left = sum([loads[i] for i in free]), surplus
        for i in free:
            extra = min(reach - given[i], max(1, left * loads[i] // mass), surplus)
            given[i] = given[i] + extra
            surplus = surplus - extra
    return np.array([reach] + given)


def ragged(key, count, total, bound, skew):
    if count == 2:
        one = jax.random.randint(key, (), max(1, total - bound), min(bound, total - 1) + 1)
        return jnp.stack([one, total - one])
    tallies = jnp.asarray(length_profile(count, total, bound, skew), jnp.int32)
    pairs = (count - 1) // 2
    donor, taker = tallies[1:1 + 2 * pairs:2], tallies[2:2 + 2 * pairs:2]
    margin = jnp.minimum(donor - 1, bound - taker)
    passed = jax.random.randint(jax.random.fold_in(key, 1), (pairs,), 0, 1 << 20) % (margin + 1)
    tallies = tallies.at[1:1 + 2 * pairs:2].set(donor - passed).at[2:2 + 2 * pairs:2].set(taker + passed)
    return tallies[jax.random.permutation(jax.random.fold_in(key, 2), count)]


def deal_out(key, own, number, rows, amount, top, reach, skew):
    sequence = jax.random.permutation(key, amount)
    crowded, ordinary = portions_of(amount, rows * top, reach, skew, True), portions_of(amount, rows * top, reach, skew, False)
    places = jnp.arange(amount)

    def named(sizes, rotation):
        used = int((sizes > 0).sum())
        fixed = max(1, used // 4)
        moved = fixed + (places - fixed + rotation * (used - fixed)) % max(1, amount - fixed)
        return jnp.zeros((amount,), jnp.int32).at[sequence[jnp.where(places < fixed, places, moved)]].set(jnp.asarray(sizes, jnp.int32))

    sizes = jnp.where(number % 4 == 0, named(crowded, number // 4), named(ordinary, number - number // 4 - 1))
    mixed = jax.random.permutation(jax.random.fold_in(own, 3), amount)
    source_of, sink = mixed[0:amount // 2 * 2:2], mixed[1:amount // 2 * 2:2]
    room = jnp.minimum(sizes[source_of] - 1, reach - sizes[sink]) // 2
    room = jnp.where((source_of == sequence[0]) | (sink == sequence[0]) | (sizes[sink] == 0), 0, jnp.maximum(room, 0))
    moved = jax.random.randint(jax.random.fold_in(own, 4), (amount // 2,), 0, 1 << 20) % (room + 1)
    sizes = sizes.at[source_of].add(-moved).at[sink].add(moved)
    items = jnp.searchsorted(jnp.cumsum(sizes), jnp.arange(rows * top), side="right").astype(jnp.int32)
    grid = items.reshape(top, rows).T
    grid = grid[jax.random.permutation(jax.random.fold_in(own, 1), rows)]
    rotation = jax.random.randint(jax.random.fold_in(own, 2), (rows, 1), 0, top)
    return jnp.take_along_axis(grid, (jnp.arange(top)[None, :] + rotation) % top, axis=1)


def portions_of(count, total, bound, lean, full):
    loads = [(1 << 20) // math.isqrt(standing ** lean) + 1 for standing in range(1, count + 1)]
    largest = bound if full else min(bound, max(-(-total // count), total * loads[0] // sum(loads)))
    least = 1 if total - largest >= count - 1 else 0
    holding, surplus = [largest] + [least] * (count - 1), total - largest - least * (count - 1)
    while surplus > 0:
        free = [i for i in range(1, count) if holding[i] < largest] or [i for i in range(1, count) if holding[i] < bound]
        mass, remaining = sum([loads[i] for i in free]), surplus
        for i in free:
            more = min(bound - holding[i], max(1, remaining * loads[i] // mass), surplus)
            holding[i] = holding[i] + more
            surplus = surplus - more
    return np.array(holding)


def noise(key, extent, spread, bound, cuts=(), held_as=jnp.bfloat16):
    values = jax.random.normal(key, extent, jnp.float32) * spread
    if len(cuts) > 0:
        values = block_levels(key, extent, cuts, -0.22, 0.18) * values
    return jnp.clip(values, min=-bound, max=bound).astype(held_as)


def setup_inputs(seed: int = 0) -> dict:
    splits = jax.random.split(jax.random.key(seed), 13)
    resid = draw_resid(jax.random.fold_in(splits[12], 71), 0)
    moe_gain = jnp.clip(jnp.exp(jax.random.uniform(splits[1], (D,), jnp.float32, math.log(0.25), math.log(2.5))), 0.25, 2.5)
    final_gain = jnp.clip(1.0 + 0.1 * jax.random.normal(splits[2], (D,), jnp.float32), 0.5, 1.5)
    router = noise(splits[3], (D, EXPERTS), D ** -0.5, 0.078125)
    w_gate = noise(splits[4], (EXPERTS, D, FF_WIN), D ** -0.5, 0.078125, ((0, 8), (2, 32)))
    w_up = noise(splits[5], (EXPERTS, D, FF_WIN), D ** -0.5, 0.078125, ((0, 8), (2, 32)))
    w_down = noise(splits[6], (EXPERTS, FF_WIN, D), FF_WIN ** -0.5, 0.0625, ((0, 8), (1, 32)))
    lm_head = draw_lm_head(jax.random.fold_in(splits[12], 71), 0)
    expert_ids_keys = jax.random.split(jax.random.fold_in(splits[8], 1), N_BATCH * GROUP_TOK // TOK_DEV)
    expert_ids_turns = jax.random.permutation(jax.random.fold_in(splits[8], 3), N_BATCH * GROUP_TOK // TOK_DEV)
    expert_ids = jax.vmap(lambda own, number: deal_out(jax.random.fold_in(splits[8], 2), own, number, TOK_DEV, EXPERTS, TOPK, CAP, 2))(expert_ids_keys, expert_ids_turns).reshape((N_BATCH, GROUP_TOK, TOPK))
    target_ids = plant(jax.random.randint(splits[9], (N_BATCH, GROUP_TOK), 0, VOC_WIN), jax.random.fold_in(splits[9], 1), 0, VOC_WIN - 1).astype(jnp.int32)
    choice_len = jax.vmap(lambda own: ragged(own, CHOICES, GROUP_TOK, MOSTLEN, 1))(jax.random.split(splits[10], N_BATCH)).reshape((N_BATCH, CHOICES)).astype(jnp.int32)
    choice_question = draw_choice_question(jax.random.fold_in(splits[12], 71), 0)
    return {"resid": resid, "moe_gain": moe_gain, "final_gain": final_gain, "router": router, "w_gate": w_gate, "w_up": w_up, "w_down": w_down, "lm_head": lm_head, "expert_ids": expert_ids, "target_ids": target_ids, "choice_len": choice_len, "choice_question": choice_question}


epsilon = 1e-05

def rms_scale(values, gain):
    mean_square = lax.optimization_barrier(jnp.mean(values * values, axis=-1, keepdims=True))
    return values * lax.rsqrt(mean_square + epsilon) * gain

def choice_member(lengths, positions):
    ends = jnp.cumsum(lengths, dtype=jnp.int32)
    starts = ends - lengths
    return (positions[None, :] >= starts[:, None]) & (positions[None, :] < ends[:, None])

def choice_softmax(choice_total, lengths, questions):
    average = choice_total / lengths.astype(jnp.float32)
    same_question = questions[:, None] == questions[None, :]
    question_top = lax.optimization_barrier(jnp.max(jnp.where(same_question, average[None, :], -jnp.inf), axis=1))
    raised = jnp.exp(average - question_top)
    denominator = lax.optimization_barrier(jnp.sum(jnp.where(same_question, raised[None, :], 0.0), axis=1))
    return raised / denominator

def reference(resid, moe_gain, final_gain, router, w_gate, w_up, w_down, lm_head, expert_ids, target_ids, choice_len, choice_question):
    groups, group_tokens, model_width = resid.shape
    stream = resid.reshape(-1, model_width).astype(jnp.float32)
    row_count = stream.shape[0]
    normed_in = rms_scale(stream, moe_gain).astype(jnp.bfloat16)
    router_logit = jnp.dot(normed_in, router, preferred_element_type=jnp.float32)
    route_ids = expert_ids.reshape(row_count, -1).astype(jnp.int32)
    picked = jnp.take_along_axis(router_logit, route_ids, axis=1)
    gate_weights = 1.0 / lax.optimization_barrier(jnp.sum(jnp.exp(picked[:, None, :] - picked[:, :, None]), axis=2))
    flat_ids = route_ids.reshape(-1)
    flat_gates = gate_weights.reshape(-1)
    token_of = jnp.arange(flat_ids.shape[0], dtype=jnp.int32) // route_ids.shape[1]
    slices = N_VOCAB * N_BATCH
    bound_rows = N_EXPERT * N_VOCAB * N_BATCH * CAP

    def one_expert(combined, expert):
        found = flat_ids == expert
        chosen_rows = jnp.nonzero(found, size=bound_rows, fill_value=0)[0].astype(jnp.int32)
        valid = jnp.arange(bound_rows, dtype=jnp.int32) < jnp.sum(found.astype(jnp.int32))
        tokens = token_of[chosen_rows]
        block_rows = normed_in[tokens]
        gate_part = jnp.dot(block_rows, w_gate[expert], preferred_element_type=jnp.float32)
        up_part = jnp.dot(block_rows, w_up[expert], preferred_element_type=jnp.float32)
        hidden = (jax.nn.silu(gate_part) * up_part).astype(jnp.bfloat16)
        hidden = hidden.reshape(bound_rows, slices, -1)
        down_parts = w_down[expert].reshape(slices, -1, model_width)

        def add_slice(running, slice_index):
            part = jnp.dot(hidden[:, slice_index], down_parts[slice_index], preferred_element_type=jnp.float32).astype(jnp.bfloat16)
            part = lax.optimization_barrier(part)
            return (running + part.astype(jnp.float32), None)
        running, _ = lax.scan(add_slice, jnp.zeros((bound_rows, model_width), jnp.float32), jnp.arange(slices, dtype=jnp.int32))
        expert_out = lax.optimization_barrier(running.astype(jnp.bfloat16)).astype(jnp.float32)
        weight = jnp.where(valid, flat_gates[chosen_rows], 0.0)
        return (combined.at[tokens].add(weight[:, None] * expert_out), None)
    combined, _ = lax.scan(one_expert, jnp.zeros((row_count, model_width), jnp.float32), jnp.arange(EXPERTS, dtype=jnp.int32))
    mixed_rows = stream + combined
    normed_out = rms_scale(mixed_rows, final_gain).astype(jnp.bfloat16)
    logits = lax.dot_general(normed_out, lm_head, (((1,), (1,)), ((), ())), preferred_element_type=jnp.float32)
    largest = lax.optimization_barrier(jnp.max(logits, axis=1))
    log_total = largest + jnp.log(lax.optimization_barrier(jnp.sum(jnp.exp(logits - largest[:, None]), axis=1)))
    target_logit = jnp.take_along_axis(logits, target_ids.reshape(-1, 1).astype(jnp.int32), axis=1)[:, 0]
    token_logprob = (target_logit - log_total).reshape(groups, group_tokens)
    positions = jnp.arange(group_tokens, dtype=jnp.int32)

    def group_probs(logprob_row, lengths, questions):
        member = choice_member(lengths, positions)
        choice_total = lax.optimization_barrier(jnp.sum(jnp.where(member, logprob_row[None, :], 0.0), axis=1))
        return choice_softmax(choice_total, lengths, questions)
    choice_prob = jax.vmap(group_probs)(token_logprob, choice_len, choice_question)
    return (token_logprob, choice_prob)
```

```python
import jax
import jax.numpy as jnp
from jax import lax
from jax.sharding import PartitionSpec as P

epsilon = 1e-05
bf16 = jnp.bfloat16
f32 = jnp.float32

NZ, NX, NC, NY = 8, 4, 2, 4
Z_ORDER = (0, -1, 1, -2, 2, -3, 3, 4)
X_ORDER = (0, -1, 1, 2)


def plane_perm(second, shift):
    pairs = []
    for x in range(NX):
        for c in range(NC):
            for y in range(NY):
                along_x = (c == 0) != second
                to_x = (x + shift) % NX if along_x else x
                to_y = y if along_x else (y + shift) % NY
                pairs.append(((x * NC + c) * NY + y, (to_x * NC + c) * NY + to_y))
    return pairs


def plane_shift(array, second, shift):
    return lax.ppermute(array, ("vocab", "batch"), plane_perm(second, shift))


def swap_cores(array):
    return lax.ppermute(array, "vocab", [(v, v ^ 1) for v in range(NX * NC)])


def x_shift(array, shift):
    return lax.ppermute(
        array,
        "vocab",
        [(v, ((v // NC + shift) % NX) * NC + v % NC) for v in range(NX * NC)],
    )


def z_shift(array, shift):
    return lax.ppermute(array, "expert", [(z, (z + shift) % NZ) for z in range(NZ)])


def gather_four(block, shift_by):
    return [block, shift_by(block, 1), shift_by(block, -1), shift_by(block, 2)]


def scatter_four(parts, shift_by):
    back = [shift_by(parts[1], -1), shift_by(parts[2], 1), shift_by(parts[3], 2)]
    return sum((piece.astype(f32) for piece in back), parts[0].astype(f32))


def copy_for_each(array, axis):
    peers = lax.axis_size(axis)
    return lax.all_to_all(
        jnp.broadcast_to(array[None], (peers, *array.shape)), axis, 0, 0, tiled=True
    )


def rms_scale(values, gain):
    mean_square = jnp.mean(values * values, axis=-1, keepdims=True)
    return values * lax.rsqrt(mean_square + epsilon) * gain


def route_gates(router_logit, route_ids):
    expert_count = router_logit.shape[1]
    matches = route_ids[:, :, None] == jnp.arange(expert_count, dtype=jnp.int32)[None, None, :]
    picked = jnp.sum(jnp.where(matches, router_logit[:, None, :], 0.0), axis=2)
    return 1.0 / jnp.sum(jnp.exp(picked[:, None, :] - picked[:, :, None]), axis=2)


def choice_member(lengths, positions):
    count = lengths.shape[0]
    upto = jnp.arange(count)[:, None] >= jnp.arange(count)[None, :]
    ends = jnp.sum(jnp.where(upto, lengths[None, :], 0), axis=1)
    starts = ends - lengths
    return (positions[None, :] >= starts[:, None]) & (positions[None, :] < ends[:, None])


def choice_softmax(choice_total, lengths, questions):
    average = choice_total / lengths.astype(f32)
    same_question = questions[:, None] == questions[None, :]
    question_top = jnp.max(jnp.where(same_question, average[None, :], -jnp.inf), axis=1)
    raised = jnp.exp(average - question_top)
    denominator = jnp.sum(jnp.where(same_question, raised[None, :], 0.0), axis=1)
    return raised / denominator


def on_device(
    resid,
    moe_gain,
    final_gain,
    router,
    w_gate,
    w_up,
    w_down,
    lm_head,
    expert_ids,
    target_ids,
    choice_len,
    choice_question,
):
    own_gate, own_up, own_down = w_gate[0], w_up[0], w_down[0]
    stream = resid[0].astype(f32)
    token_count, model_width = stream.shape

    other_gate = swap_cores(own_gate)
    other_up = swap_cores(own_up)
    other_down = swap_cores(own_down)
    other_head = swap_cores(lm_head)

    normed_in = rms_scale(stream, moe_gain).astype(bf16)
    router_logit = jnp.dot(normed_in, router, preferred_element_type=f32)
    route_ids = expert_ids[0]
    route_count = route_ids.shape[1]
    gate_weights = route_gates(router_logit, route_ids)
    bucket_size = 3
    flat_ids = route_ids.reshape(-1)
    picks = flat_ids.shape[0]
    before = jnp.arange(picks)[:, None] > jnp.arange(picks)[None, :]
    earlier = jnp.sum(
        (before & (flat_ids[:, None] == flat_ids[None, :])).astype(jnp.int32), axis=1
    )
    slot_index = flat_ids * bucket_size + earlier
    slot_match = (
        slot_index[:, None] == jnp.arange(NZ * bucket_size, dtype=jnp.int32)[None, :]
    ).astype(f32)
    slot_match = slot_match.reshape(token_count, route_count, -1)
    dispatch = jnp.sum(slot_match, axis=1).astype(bf16)
    combine_weights = jnp.sum(slot_match * gate_weights[:, :, None], axis=1)
    buckets = lax.dot_general(
        dispatch, normed_in, (((0,), (0,)), ((), ())), preferred_element_type=f32
    )
    buckets = buckets.astype(bf16).reshape(NZ, bucket_size, model_width)

    arrived = lax.all_to_all(buckets, "expert", split_axis=0, concat_axis=0, tiled=True).reshape(
        -1, model_width
    )
    column_rows = arrived.shape[0]

    def first(block, shift):
        return plane_shift(block, False, shift)

    def second(block, shift):
        return plane_shift(block, True, shift)

    line = jnp.concatenate(gather_four(arrived, first))
    rows = jnp.concatenate(gather_four(line, second))

    def expand(gate_cols, up_cols):
        gate_part = jnp.dot(rows, gate_cols, preferred_element_type=f32)
        up_part = jnp.dot(rows, up_cols, preferred_element_type=f32)
        return (jax.nn.silu(gate_part) * up_part).astype(bf16)

    hidden = jnp.concatenate([expand(own_gate, own_up), expand(other_gate, other_up)], axis=1)
    down = jnp.concatenate([own_down, other_down])
    parts = [
        jnp.dot(block, down, preferred_element_type=f32).astype(bf16)
        for block in jnp.split(hidden, 4)
    ]
    line_sum = scatter_four(parts, second).astype(bf16)
    expert_sum = scatter_four(jnp.split(line_sum, 4), first).astype(bf16)

    outgoing = expert_sum.reshape(NZ, bucket_size, model_width)
    returned = lax.all_to_all(outgoing, "expert", split_axis=0, concat_axis=0, tiled=True)
    returned_rows = returned.reshape(-1, model_width).astype(f32)
    mixed_rows = stream + jnp.sum(combine_weights[:, :, None] * returned_rows[None], axis=1)
    normed_out = rms_scale(mixed_rows, final_gain).astype(bf16)

    near = jnp.concatenate(gather_four(normed_out, x_shift))
    up_side, down_side = [near], [near]
    for _ in range(3):
        up_side.append(z_shift(up_side[-1], 1))
        down_side.append(z_shift(down_side[-1], -1))
    far = z_shift(up_side[-1], 1)
    blocks = [near]
    for step in range(1, 4):
        blocks += [up_side[step], down_side[step]]
    blocks.append(far)
    head_rows = jnp.concatenate(blocks)

    z_index = lax.axis_index("expert")
    v_index = lax.axis_index("vocab")
    x_index, c_index = v_index // NC, v_index % NC
    local = NZ * NX * token_count
    z_seen = (z_index + jnp.array(Z_ORDER, jnp.int32)) % NZ
    x_seen = (x_index + jnp.array(X_ORDER, jnp.int32)) % NX
    place = (
        (z_seen[:, None, None] * NX + x_seen[None, :, None]) * token_count
        + jnp.arange(token_count, dtype=jnp.int32)[None, None, :]
    ).reshape(-1)
    targets = target_ids[0]
    side_targets = lax.dynamic_slice_in_dim(
        targets.reshape(NZ * NX, NC, token_count), c_index, 1, 1
    ).reshape(-1)
    placed = place[:, None] == jnp.arange(local, dtype=jnp.int32)[None, :]
    seen_targets = jnp.sum(jnp.where(placed, side_targets[None, :], 0), axis=1)

    vocab_share = lm_head.shape[0]
    steps = jnp.arange(vocab_share, dtype=jnp.int32)
    own_base = (z_index * NX * NC + v_index) * vocab_share
    other_base = (z_index * NX * NC + (v_index ^ 1)) * vocab_share

    def head(rows_of, table, base):
        logits = lax.dot_general(
            rows_of, table, (((1,), (1,)), ((), ())), preferred_element_type=f32
        )
        top = jnp.max(logits, axis=1)
        total = jnp.sum(jnp.exp(logits - top[:, None]), axis=1)
        hit = jnp.sum(
            jnp.where(seen_targets[:, None] == (base + steps)[None, :], logits, 0.0), axis=1
        )
        return top, total, hit

    top_a, total_a, hit_a = head(head_rows, lm_head, own_base)
    top_b, total_b, hit_b = head(head_rows, other_head, other_base)
    top = jnp.maximum(top_a, top_b)
    total = total_a * jnp.exp(top_a - top) + total_b * jnp.exp(top_b - top)
    stats = jnp.stack([top, total, hit_a + hit_b])
    stats = jnp.sum(jnp.where(placed[None], stats[:, :, None], 0.0), axis=1)

    gathered = copy_for_each(stats, ("expert", "vocab")).reshape(NZ * NX, NC, 3, local)
    tops, totals, hits = gathered[:, :, 0], gathered[:, :, 1], gathered[:, :, 2]
    best = jnp.max(tops, axis=0)
    summed = jnp.sum(totals * jnp.exp(tops - best[None]), axis=0)
    logprob = jnp.sum(hits, axis=0) - (best + jnp.log(summed))
    group_logprob = logprob.reshape(NC, NZ * NX, token_count).transpose(1, 0, 2).reshape(-1)

    lengths = choice_len[0]
    questions = choice_question[0]
    positions = jnp.arange(group_logprob.shape[0], dtype=jnp.int32)
    choice_total = jnp.sum(
        jnp.where(choice_member(lengths, positions), group_logprob[None, :], 0.0), axis=1
    )
    own_first = (z_index * NX * NC + v_index) * token_count
    own_logprob = lax.dynamic_slice_in_dim(group_logprob, own_first, token_count, 0)
    choice_prob = choice_softmax(choice_total, lengths, questions)
    return (own_logprob.reshape(1, -1), choice_prob.reshape(1, -1))


def solution(mesh):
    return jax.shard_map(
        on_device,
        mesh=mesh,
        in_specs=(
            P("batch", ("expert", "vocab"), None),
            P(),
            P(),
            P(),
            P("expert", None, ("vocab", "batch")),
            P("expert", None, ("vocab", "batch")),
            P("expert", ("vocab", "batch"), None),
            P(("expert", "vocab"), None),
            P("batch", ("expert", "vocab"), None),
            P("batch", None),
            P("batch", None),
            P("batch", None),
        ),
        out_specs=(P("batch", ("expert", "vocab")), P("batch", None)),
        check_vma=False,
    )
```

```python
import jax
import jax.numpy as jnp
from jax import lax
from jax.sharding import PartitionSpec as P

epsilon = 1e-05
bf16 = jnp.bfloat16
f32 = jnp.float32

NZ, NX, NC, NY = 8, 4, 2, 4
SHIFT_ORDER = (0, -1, 1, 2)


def plane_perm(second, shift):
    pairs = []
    for x in range(NX):
        for c in range(NC):
            for y in range(NY):
                along_x = (c == 0) != second
                to_x = (x + shift) % NX if along_x else x
                to_y = y if along_x else (y + shift) % NY
                pairs.append(((x * NC + c) * NY + y, (to_x * NC + c) * NY + to_y))
    return pairs


def plane_shift(array, second, shift):
    return lax.ppermute(array, ("vocab", "batch"), plane_perm(second, shift))


def swap_cores(array):
    return lax.ppermute(array, "vocab", [(v, v ^ 1) for v in range(NX * NC)])


def y_shift(array, shift):
    return lax.ppermute(array, "batch", [(y, (y + shift) % NY) for y in range(NY)])


def gather_four(block, shift_by):
    return [block, shift_by(block, 1), shift_by(block, -1), shift_by(block, 2)]


def scatter_four(parts, shift_by):
    back = [shift_by(parts[1], -1), shift_by(parts[2], 1), shift_by(parts[3], 2)]
    return sum((piece.astype(f32) for piece in back), parts[0].astype(f32))


def tied(*arrays):
    return lax.optimization_barrier(arrays)


def copy_for_each(array, axis):
    peers = lax.axis_size(axis)
    return lax.all_to_all(
        jnp.broadcast_to(array[None], (peers, *array.shape)), axis, 0, 0, tiled=True
    )


def rms_scale(values, gain):
    mean_square = jnp.mean(values * values, axis=-1, keepdims=True)
    return values * lax.rsqrt(mean_square + epsilon) * gain


def route_gates(router_logit, route_ids):
    expert_count = router_logit.shape[1]
    matches = route_ids[:, :, None] == jnp.arange(expert_count, dtype=jnp.int32)[None, None, :]
    picked = jnp.sum(jnp.where(matches, router_logit[:, None, :], 0.0), axis=2)
    return 1.0 / jnp.sum(jnp.exp(picked[:, None, :] - picked[:, :, None]), axis=2)


def choice_member(lengths, positions):
    count = lengths.shape[0]
    upto = jnp.arange(count)[:, None] >= jnp.arange(count)[None, :]
    ends = jnp.sum(jnp.where(upto, lengths[None, :], 0), axis=1)
    starts = ends - lengths
    return (positions[None, :] >= starts[:, None]) & (positions[None, :] < ends[:, None])


def choice_softmax(choice_total, lengths, questions):
    average = choice_total / lengths.astype(f32)
    same_question = questions[:, None] == questions[None, :]
    question_top = jnp.max(jnp.where(same_question, average[None, :], -jnp.inf), axis=1)
    raised = jnp.exp(average - question_top)
    denominator = jnp.sum(jnp.where(same_question, raised[None, :], 0.0), axis=1)
    return raised / denominator


def on_device(
    resid,
    moe_gain,
    final_gain,
    router,
    w_gate,
    w_up,
    w_down,
    lm_head,
    expert_ids,
    target_ids,
    choice_len,
    choice_question,
):
    own_gate, own_up, own_down = w_gate[0], w_up[0], w_down[0]
    stream = resid[0].astype(f32)
    token_count, model_width = stream.shape
    z_index = lax.axis_index("expert")
    v_index = lax.axis_index("vocab")
    y_index = lax.axis_index("batch")
    x_index, c_index = v_index // NC, v_index % NC

    other_gate = swap_cores(own_gate)
    other_up = swap_cores(own_up)
    other_down = swap_cores(own_down)

    vocab_share = lm_head.shape[0]
    quarter = vocab_share // NY
    own_table = lax.all_gather(
        lax.dynamic_slice_in_dim(lm_head, y_index * quarter, quarter, 0),
        "expert",
        axis=0,
        tiled=True,
    )

    normed_in = rms_scale(stream, moe_gain).astype(bf16)
    router_logit = jnp.dot(normed_in, router, preferred_element_type=f32)
    route_ids = expert_ids[0]
    route_count = route_ids.shape[1]
    gate_weights = route_gates(router_logit, route_ids)
    bucket_size = 3
    flat_ids = route_ids.reshape(-1)
    picks = flat_ids.shape[0]
    before = jnp.arange(picks)[:, None] > jnp.arange(picks)[None, :]
    earlier = jnp.sum(
        (before & (flat_ids[:, None] == flat_ids[None, :])).astype(jnp.int32), axis=1
    )
    slot_index = flat_ids * bucket_size + earlier
    slot_match = (
        slot_index[:, None] == jnp.arange(NZ * bucket_size, dtype=jnp.int32)[None, :]
    ).astype(f32)
    slot_match = slot_match.reshape(token_count, route_count, -1)
    dispatch = jnp.sum(slot_match, axis=1).astype(bf16)
    combine_weights = jnp.sum(slot_match * gate_weights[:, :, None], axis=1)
    buckets = lax.dot_general(
        dispatch, normed_in, (((0,), (0,)), ((), ())), preferred_element_type=f32
    )
    buckets = buckets.astype(bf16).reshape(NZ, bucket_size, model_width)

    arrived = lax.all_to_all(buckets, "expert", split_axis=0, concat_axis=0, tiled=True).reshape(
        -1, model_width
    )
    arrived, other_gate, other_up, other_down = tied(arrived, other_gate, other_up, other_down)

    def first(block, shift):
        return plane_shift(block, False, shift)

    def second(block, shift):
        return plane_shift(block, True, shift)

    line = jnp.concatenate(gather_four(arrived, first))
    line_rows = line.shape[0]
    half = line_rows // 2
    from_before = second(line, 1)
    from_after = second(line, -1)
    far = jnp.concatenate([second(from_before[:half], 1), second(from_after[half:], -1)])
    near = jnp.concatenate([line, from_before, from_after])

    def expand(rows):
        def one(gate_cols, up_cols):
            gate_part = jnp.dot(rows, gate_cols, preferred_element_type=f32)
            up_part = jnp.dot(rows, up_cols, preferred_element_type=f32)
            return (jax.nn.silu(gate_part) * up_part).astype(bf16)

        return jnp.concatenate([one(own_gate, own_up), one(other_gate, other_up)], axis=1)

    near_hidden = expand(near)
    far_hidden = expand(far)
    down = jnp.concatenate([own_down, other_down])

    def contract(hidden):
        return jnp.dot(hidden, down, preferred_element_type=f32).astype(bf16)

    far_part = contract(far_hidden)
    to_before = second(far_part[:half], -1)
    to_after = second(far_part[half:], 1)
    own_part, before_part, after_part = [contract(h) for h in jnp.split(near_hidden, 3)]
    own_part, before_part, after_part, to_before, to_after = tied(
        own_part, before_part, after_part, to_before, to_after
    )
    before_part = before_part.at[:half].add(to_before)
    after_part = after_part.at[half:].add(to_after)
    line_sum = (
        own_part.astype(f32)
        + second(before_part, -1).astype(f32)
        + second(after_part, 1).astype(f32)
    ).astype(bf16)
    expert_sum = scatter_four(jnp.split(line_sum, 4), first).astype(bf16)

    outgoing = expert_sum.reshape(NZ, bucket_size, model_width)
    returned = lax.all_to_all(outgoing, "expert", split_axis=0, concat_axis=0, tiled=True)
    returned_rows = returned.reshape(-1, model_width).astype(f32)
    mixed_rows = stream + jnp.sum(combine_weights[:, :, None] * returned_rows[None], axis=1)
    normed_out = rms_scale(mixed_rows, final_gain).astype(bf16)

    head_line = jnp.concatenate(gather_four(normed_out, first))
    head_rows = jnp.concatenate(gather_four(head_line, second))

    other_table = swap_cores(own_table)
    sides = NX * NY
    local = sides * token_count
    order = jnp.array(SHIFT_ORDER, jnp.int32)
    x_order = jnp.where(c_index == 0, order[None, :], order[:, None])
    y_order = jnp.where(c_index == 0, order[:, None], order[None, :])
    x_seen = (x_index + x_order) % NX
    y_seen = (y_index + y_order) % NY
    token_step = jnp.arange(token_count, dtype=jnp.int32)
    seen_place = ((x_seen * NY + y_seen)[:, :, None] * token_count + token_step).reshape(-1)
    seen_x = (x_index + order) % NX
    side_targets = lax.dynamic_index_in_dim(
        lax.dynamic_index_in_dim(
            target_ids[0].reshape(NZ, NX, NC, token_count), z_index, 0, False
        ),
        c_index,
        1,
        False,
    )
    side_targets = jnp.sum(
        jnp.where(
            (seen_x[:, None] == jnp.arange(NX, dtype=jnp.int32)[None, :])[:, :, None],
            side_targets[None],
            0,
        ),
        axis=1,
    )
    near_targets = jnp.stack(gather_four(side_targets, y_shift))
    seen_targets = jnp.where(
        c_index == 0, near_targets, near_targets.transpose(1, 0, 2)
    ).reshape(-1)
    placed = seen_place[:, None] == jnp.arange(local, dtype=jnp.int32)[None, :]

    table_rows = NZ * quarter
    row_step = jnp.arange(table_rows, dtype=jnp.int32)

    def entries(v):
        return (
            ((row_step // quarter) * (NX * NC) + v) * vocab_share
            + y_index * quarter
            + row_step % quarter
        )

    def head(table, ids):
        logits = lax.dot_general(
            head_rows, table, (((1,), (1,)), ((), ())), preferred_element_type=f32
        )
        top = jnp.max(logits, axis=1)
        total = jnp.sum(jnp.exp(logits - top[:, None]), axis=1)
        hit = jnp.sum(jnp.where(seen_targets[:, None] == ids[None, :], logits, 0.0), axis=1)
        return top, total, hit

    top_a, total_a, hit_a = head(own_table, entries(v_index))
    top_b, total_b, hit_b = head(other_table, entries(v_index ^ 1))
    top = jnp.maximum(top_a, top_b)
    total = total_a * jnp.exp(top_a - top) + total_b * jnp.exp(top_b - top)
    stats = jnp.stack([top, total, hit_a + hit_b])
    stats = jnp.sum(jnp.where(placed[None], stats[:, :, None], 0.0), axis=1)

    gathered = copy_for_each(stats, ("vocab", "batch")).reshape(NX, NC, NY, 3, local)
    tops, totals, hits = gathered[:, :, :, 0], gathered[:, :, :, 1], gathered[:, :, :, 2]
    best = jnp.max(tops, axis=(0, 2))
    summed = jnp.sum(totals * jnp.exp(tops - best[None, :, None]), axis=(0, 2))
    plane_logprob = jnp.sum(hits, axis=(0, 2)) - (best + jnp.log(summed))
    plane_logprob = plane_logprob.reshape(NC, NX, NY, token_count)
    share = lax.dynamic_index_in_dim(plane_logprob, y_index, 2, False).transpose(1, 0, 2)
    group_logprob = copy_for_each(share.reshape(1, -1), "expert").reshape(-1)

    lengths = choice_len[0]
    questions = choice_question[0]
    positions = jnp.arange(group_logprob.shape[0], dtype=jnp.int32)
    choice_total = jnp.sum(
        jnp.where(choice_member(lengths, positions), group_logprob[None, :], 0.0), axis=1
    )
    own_first = (z_index * NX * NC + v_index) * token_count
    own_logprob = lax.dynamic_slice_in_dim(group_logprob, own_first, token_count, 0)
    choice_prob = choice_softmax(choice_total, lengths, questions)
    return (own_logprob.reshape(1, -1), choice_prob.reshape(1, -1))


def solution(mesh):
    return jax.shard_map(
        on_device,
        mesh=mesh,
        in_specs=(
            P("batch", ("expert", "vocab"), None),
            P(),
            P(),
            P(),
            P("expert", None, ("vocab", "batch")),
            P("expert", None, ("vocab", "batch")),
            P("expert", ("vocab", "batch"), None),
            P(("expert", "vocab"), None),
            P("batch", ("expert", "vocab"), None),
            P("batch", None),
            P("batch", None),
            P("batch", None),
        ),
        out_specs=(P("batch", ("expert", "vocab")), P("batch", None)),
        check_vma=False,
    )
```

```python
import functools

import jax
import jax.numpy as jnp
from jax import lax
from jax.experimental import pallas as pl
from jax.experimental.pallas import tpu as pltpu
from jax.sharding import PartitionSpec as P

epsilon = 1e-05
bf16 = jnp.bfloat16
f32 = jnp.float32
i32 = jnp.int32

NZ, NX, NC, NY = 8, 4, 2, 4
SLOTS = 3
VMEM_LIMIT = 48 * 2**20


def two_axis_perm(sizes, coords, axis_of, shift):
    pairs = []
    for index in range(sizes):
        place = coords(index)
        axis, step, size = axis_of(place)
        to = dict(place)
        to[axis] = (place[axis] + shift * step) % size
        pairs.append((index, coords(to)))
    return pairs


def plane_coords(index):
    if isinstance(index, dict):
        return (index["x"] * NC + index["c"]) * NY + index["y"]
    return {"x": index // (NC * NY), "c": index // NY % NC, "y": index % NY}


def head_coords(index):
    if isinstance(index, dict):
        return (index["z"] * NX + index["x"]) * NC + index["c"]
    return {"z": index // (NX * NC), "x": index // NC % NX, "c": index % NC}


def plane_shift(array, second, shift):
    def axis_of(place):
        return ("x", 1, NX) if (place["c"] == 0) != second else ("y", 1, NY)

    perm = two_axis_perm(NX * NC * NY, plane_coords, axis_of, shift)
    return lax.ppermute(array, ("vocab", "batch"), perm)


def head_shift(array, second, shift):
    def axis_of(place):
        return ("z", 2, NZ) if (place["c"] == 0) != second else ("x", 1, NX)

    perm = two_axis_perm(NZ * NX * NC, head_coords, axis_of, shift)
    return lax.ppermute(array, ("expert", "vocab"), perm)


def swap_cores(array):
    return lax.ppermute(array, "vocab", [(v, v ^ 1) for v in range(NX * NC)])


def swap_planes(array):
    return lax.ppermute(array, "expert", [(z, z ^ 1) for z in range(NZ)])


def gather_four(block, shift_by):
    return [block, shift_by(block, 1), shift_by(block, -1), shift_by(block, 2)]


def rel_step(rel):
    return jnp.where(rel == 1, -1, jnp.where(rel == 2, 1, jnp.where(rel == 3, 2, 0)))


def tied(*arrays):
    return lax.optimization_barrier(arrays)


def shape(dims, dtype):
    return jax.ShapeDtypeStruct(dims, dtype)


def iota(dims, axis):
    return lax.broadcasted_iota(i32, dims, axis)


def params():
    return pltpu.CompilerParams(vmem_limit_bytes=VMEM_LIMIT)


def cost(flops, moved):
    return pl.CostEstimate(flops=flops, bytes_accessed=moved, transcendentals=0)


def prelude_kernel(ids_ref, resid_ref, gain_ref, router_ref, buckets_ref, weights_ref):
    values = resid_ref[...].astype(f32)
    tokens = values.shape[0]
    mean_square = jnp.mean(values * values, axis=-1, keepdims=True)
    normed = (values * lax.rsqrt(mean_square + epsilon) * gain_ref[...]).astype(bf16)
    logits = lax.dot_general(
        normed, router_ref[...], (((1,), (1,)), ((), ())), preferred_element_type=f32
    )
    ids = ids_ref[...]
    id_a, id_b = ids[:, 0:1], ids[:, 1:2]
    earlier = (iota((tokens, tokens), 0) > iota((tokens, tokens), 1)).astype(f32)

    def slots(width):
        column = iota((tokens, NZ * width), 1)
        owner, slot = column // width, column % width
        match_a, match_b = id_a == owner, id_b == owner
        named = (match_a | match_b).astype(f32)
        rank = jnp.dot(earlier, named, preferred_element_type=f32)
        chosen = named * (rank == slot.astype(f32)).astype(f32)
        return chosen, match_a, match_b

    wide, _, _ = slots(8)
    chosen, match_a, match_b = slots(SLOTS)
    entry = iota(logits.shape, 1)
    pick_a = jnp.sum(jnp.where(id_a == entry, logits, 0.0), axis=1, keepdims=True)
    pick_b = jnp.sum(jnp.where(id_b == entry, logits, 0.0), axis=1, keepdims=True)
    gate_a = 1.0 / (1.0 + jnp.exp(pick_b - pick_a))
    gate_b = 1.0 / (jnp.exp(pick_a - pick_b) + 1.0)
    weights_ref[...] = chosen * (
        jnp.where(match_a, gate_a, 0.0) + jnp.where(match_b, gate_b, 0.0)
    )
    rows = lax.dot_general(
        wide.astype(bf16), normed, (((0,), (0,)), ((), ())), preferred_element_type=f32
    )
    for e in range(NZ):
        buckets_ref[e] = rows[8 * e : 8 * e + SLOTS].astype(bf16)


def prelude(ids, resid, gain, router):
    tokens, width = resid.shape
    return pl.pallas_call(
        prelude_kernel,
        out_shape=(
            shape((NZ, SLOTS, width), bf16),
            shape((tokens, NZ * SLOTS), f32),
        ),
        compiler_params=params(),
        cost_estimate=cost(2 * 64 * 8 * width, 8 * width),
    )(ids, resid, gain, router)


def stack_kernel(*refs, chunk):
    *parts, out_ref = refs
    width = out_ref.shape[1]

    @pl.loop(0, width // chunk)
    def _(step):
        columns = pl.ds(pl.multiple_of(step * chunk, chunk), chunk)
        pieces = []
        for part in parts:
            if len(part.shape) == 3:
                pieces += [part[e, :, columns].astype(f32) for e in range(part.shape[0])]
            else:
                pieces.append(part[:, columns].astype(f32))
        out_ref[:, columns] = jnp.concatenate(pieces).astype(bf16)


def stack(parts):
    width = parts[0].shape[-1]
    rows = sum(part.size // width for part in parts)
    return pl.pallas_call(
        functools.partial(stack_kernel, chunk=512),
        out_shape=shape((rows, width), bf16),
        compiler_params=params(),
        cost_estimate=cost(0, 4 * rows * width),
    )(*parts)


def expand_kernel(*refs, count):
    rows = [ref[...] for ref in refs[:count]]
    gate_a, up_a, gate_b, up_b, out_ref, total = refs[count:]
    step = pl.program_id(0)

    @pl.when(step == 0)
    def _():
        total[...] = jnp.zeros_like(total)

    block = rows[0] if count == 1 else jnp.concatenate(rows)
    for j, weight in enumerate((gate_a, up_a, gate_b, up_b)):
        total[j] += jnp.dot(block, weight[...], preferred_element_type=f32)

    @pl.when(step == pl.num_programs(0) - 1)
    def _():
        share = total.shape[2]
        for j in range(2):
            gate = total[2 * j]
            out_ref[:, j * share : (j + 1) * share] = (
                gate / (1.0 + jnp.exp(-gate)) * total[2 * j + 1]
            ).astype(bf16)


def expand(rows, weights):
    depth = 768
    count = len(rows)
    each, width = rows[0].shape
    share = weights[0].shape[1]
    return pl.pallas_call(
        functools.partial(expand_kernel, count=count),
        grid=(width // depth,),
        in_specs=[pl.BlockSpec((each, depth), lambda k: (0, k))] * count
        + [pl.BlockSpec((depth, share), lambda k: (k, 0))] * 4,
        out_specs=pl.BlockSpec((count * each, 2 * share), lambda k: (0, 0)),
        out_shape=shape((count * each, 2 * share), bf16),
        scratch_shapes=[pltpu.VMEM((4, count * each, share), f32)],
        compiler_params=params(),
        cost_estimate=cost(8 * count * each * width * share, 8 * width * share),
    )(*rows, *weights)


def contract(hidden, down_a, down_b):
    share = down_a.shape[0]
    return jnp.dot(hidden[:, :share], down_a, preferred_element_type=f32) + jnp.dot(
        hidden[:, share:], down_b, preferred_element_type=f32
    )


def far_kernel(hidden_ref, down_a, down_b, before_ref, after_ref):
    part = contract(hidden_ref[...], down_a[...], down_b[...]).astype(bf16)
    half = before_ref.shape[0]
    before_ref[...] = part[:half]
    after_ref[...] = part[half:]


def near_kernel(hidden_ref, down_a, down_b, got_before, got_after, own_ref, before_ref, after_ref):
    part = contract(hidden_ref[...], down_a[...], down_b[...])
    rows = own_ref.shape[0]
    half = rows // 2
    own_ref[...] = part[:rows].astype(bf16)
    before_ref[:half] = (part[rows : rows + half] + got_before[...].astype(f32)).astype(bf16)
    before_ref[half:] = part[rows + half : 2 * rows].astype(bf16)
    after_ref[:half] = part[2 * rows : 2 * rows + half].astype(bf16)
    after_ref[half:] = (part[2 * rows + half :] + got_after[...].astype(f32)).astype(bf16)


def down_call(kernel, hidden, downs, got, out_rows):
    tile = 1024
    share, width = downs[0].shape
    return pl.pallas_call(
        kernel,
        grid=(width // tile,),
        in_specs=[pl.BlockSpec(hidden.shape, lambda n: (0, 0))]
        + [pl.BlockSpec((share, tile), lambda n: (0, n))] * 2
        + [pl.BlockSpec((g.shape[0], tile), lambda n: (0, n)) for g in got],
        out_specs=[pl.BlockSpec((rows, tile), lambda n: (0, n)) for rows in out_rows],
        out_shape=[shape((rows, width), bf16) for rows in out_rows],
        compiler_params=params(),
        cost_estimate=cost(4 * hidden.shape[0] * share * width, 4 * share * width),
    )(hidden, *downs, *got)


def line_sum_kernel(own_ref, before_ref, after_ref, *outs):
    total = own_ref[...].astype(f32) + before_ref[...].astype(f32) + after_ref[...].astype(f32)
    rows = outs[0].shape[0]
    for j, out in enumerate(outs):
        out[...] = total[j * rows : (j + 1) * rows].astype(bf16)


def line_sum(parts):
    tile = 1536
    rows, width = parts[0].shape
    return pl.pallas_call(
        line_sum_kernel,
        grid=(width // tile,),
        in_specs=[pl.BlockSpec((rows, tile), lambda n: (0, n))] * 3,
        out_specs=[pl.BlockSpec((rows // 4, tile), lambda n: (0, n))] * 4,
        out_shape=[shape((rows // 4, width), bf16)] * 4,
        compiler_params=params(),
        cost_estimate=cost(3 * rows * width, 8 * rows * width),
    )(*parts)


def expert_sum_kernel(a, b, c, d, out_ref, *, chunk):
    @pl.loop(0, out_ref.shape[2] // chunk)
    def _(step):
        columns = pl.ds(pl.multiple_of(step * chunk, chunk), chunk)
        total = (
            a[:, columns].astype(f32)
            + b[:, columns].astype(f32)
            + c[:, columns].astype(f32)
            + d[:, columns].astype(f32)
        )
        for e in range(NZ):
            out_ref[e, :, columns] = total[SLOTS * e : SLOTS * e + SLOTS].astype(bf16)


def expert_sum(parts):
    width = parts[0].shape[1]
    return pl.pallas_call(
        functools.partial(expert_sum_kernel, chunk=512),
        out_shape=shape((NZ, SLOTS, width), bf16),
        compiler_params=params(),
        cost_estimate=cost(96 * width, 240 * width),
    )(*parts)


def combine_kernel(weights_ref, rows_ref, resid_ref, gain_ref, out_ref):
    mixed = resid_ref[...].astype(f32)
    weights = weights_ref[...]
    for e in range(NZ):
        rows = rows_ref[e].astype(f32)
        for s in range(SLOTS):
            slot = SLOTS * e + s
            mixed += weights[:, slot : slot + 1] * rows[s : s + 1]
    mean_square = jnp.mean(mixed * mixed, axis=-1, keepdims=True)
    out_ref[...] = (mixed * lax.rsqrt(mean_square + epsilon) * gain_ref[...]).astype(bf16)


def combine(weights, rows, resid, gain):
    return pl.pallas_call(
        combine_kernel,
        out_shape=shape(resid.shape, bf16),
        compiler_params=params(),
        cost_estimate=cost(48 * resid.size, 8 * resid.size),
    )(weights, rows, resid, gain)


def head_kernel(place_ref, targets_ref, r0, r1, r2, r3, t0, t1, t2, t3, out_ref, total):
    step = pl.program_id(0)

    @pl.when(step == 0)
    def _():
        total[...] = jnp.zeros_like(total)

    rows = jnp.concatenate([r0[...], r1[...], r2[...], r3[...]])
    share = t0.shape[0]
    for j, table in enumerate((t0, t1, t2, t3)):
        total[:, j * share : (j + 1) * share] += lax.dot_general(
            rows, table[...], (((1,), (1,)), ((), ())), preferred_element_type=f32
        )

    @pl.when(step == pl.num_programs(0) - 1)
    def _():
        z, x, c = place_ref[0], place_ref[1], place_ref[2]
        count = rows.shape[0]
        row = iota((count, 1), 0)
        outer, inner, token = rel_step(row // 32), rel_step(row // 8 % 4), row % 8
        z_half = (z // 2 + 4 + jnp.where(c == 0, inner, outer)) % 4
        x_seen = (x + 4 + jnp.where(c == 0, outer, inner)) % 4
        place = (z_half * NX + x_seen) * 8 + token
        position = ((2 * z_half + z % 2) * NX + x_seen) * (NC * 8) + c * 8 + token
        targets = targets_ref[...]
        wanted = jnp.sum(
            jnp.where(position == iota((count, targets.shape[1]), 1), targets, 0),
            axis=1,
            keepdims=True,
        )
        logits = total[...]
        entry = iota((1, 4 * share), 1)
        table, offset = entry // share, entry % share
        z_of = jnp.where(table < 2, z, z + 1 - 2 * (z % 2))
        c_of = jnp.where(table % 2 == 0, c, 1 - c)
        entry_id = ((z_of * NX + x) * NC + c_of) * share + offset
        top = jnp.max(logits, axis=1, keepdims=True)
        spread = jnp.sum(jnp.exp(logits - top), axis=1, keepdims=True)
        hit = jnp.sum(jnp.where(wanted == entry_id, logits, 0.0), axis=1, keepdims=True)
        here = place == iota((count, count), 1)
        figures = [
            jnp.sum(jnp.where(here, value, 0.0), axis=0, keepdims=True)
            for value in (top, spread, hit, hit)
        ]
        figures = jnp.concatenate(figures)
        for peer in range(out_ref.shape[0]):
            out_ref[peer] = figures


def head(place, targets, rows, tables):
    depth = 768
    width = rows[0].shape[1]
    share = tables[0].shape[0]
    count = sum(r.shape[0] for r in rows)
    whole = pl.BlockSpec(memory_space=pltpu.SMEM)
    return pl.pallas_call(
        head_kernel,
        grid=(width // depth,),
        in_specs=[whole, pl.BlockSpec(targets.shape, lambda k: (0, 0))]
        + [pl.BlockSpec((rows[0].shape[0], depth), lambda k: (0, k))] * 4
        + [pl.BlockSpec((share, depth), lambda k: (0, k))] * 4,
        out_specs=pl.BlockSpec((NZ * NX * NC, 4, count), lambda k: (0, 0, 0)),
        out_shape=shape((NZ * NX * NC, 4, count), f32),
        scratch_shapes=[pltpu.VMEM((count, 4 * share), f32)],
        compiler_params=params(),
        cost_estimate=cost(8 * count * share * width, 8 * share * width),
    )(place, targets, *rows, *tables)


def finish_kernel(place_ref, stats_ref, lengths_ref, questions_ref, logprob_ref, prob_ref):
    z, x, c = place_ref[0], place_ref[1], place_ref[2]
    count = lengths_ref.shape[1]
    local = stats_ref.shape[2]
    lengths = lengths_ref[...].astype(f32)
    questions = questions_ref[...].astype(f32)
    square = (count, count)
    same_place = iota(square, 0) == iota(square, 1)
    ends = jnp.sum(
        jnp.where(iota(square, 1) <= iota(square, 0), lengths, 0.0), axis=1, keepdims=True
    )

    def as_column(line):
        return jnp.sum(jnp.where(same_place, line, 0.0), axis=1, keepdims=True)

    def as_line(column):
        return jnp.sum(jnp.where(same_place, column, 0.0), axis=0, keepdims=True)

    length_column = as_column(lengths)
    starts = ends - length_column
    lane = iota((1, local), 1)
    choice_total = jnp.zeros((count, 1), f32)
    own = jnp.zeros((1, local), f32)
    for parity in range(2):
        for core in range(NC):
            senders = [
                (zz * NX + xx) * NC + core for zz in range(parity, NZ, 2) for xx in range(NX)
            ]
            figures = [stats_ref[j] for j in senders]
            best = functools.reduce(jnp.maximum, [f[0:1] for f in figures])
            summed = sum(f[1:2] * jnp.exp(f[0:1] - best) for f in figures)
            logprob = sum(f[2:3] for f in figures) - (best + jnp.log(summed))
            position = (
                (2 * (lane // 32) + parity) * (NX * NC * 8)
                + lane // 8 % 4 * (NC * 8)
                + core * 8
                + lane % 8
            ).astype(f32)
            member = (position >= starts) & (position < ends)
            choice_total += jnp.sum(jnp.where(member, logprob, 0.0), axis=1, keepdims=True)
            mine = (z % 2 == parity) & (c == core)
            own += jnp.where(mine, logprob, 0.0)
    tokens = logprob_ref.shape[1]
    first = (z // 2 * NX + x) * tokens
    column = jnp.sum(
        jnp.where(iota((tokens, local), 1) == first + iota((tokens, local), 0), own, 0.0),
        axis=1,
        keepdims=True,
    )
    eye = iota((tokens, tokens), 0) == iota((tokens, tokens), 1)
    logprob_ref[...] = jnp.sum(jnp.where(eye, column, 0.0), axis=0, keepdims=True)

    average = choice_total / length_column
    same_question = as_column(questions) == questions
    top = jnp.max(
        jnp.where(same_question, as_line(average), -jnp.inf), axis=1, keepdims=True
    )
    raised = jnp.exp(average - top)
    denominator = jnp.sum(
        jnp.where(same_question, as_line(raised), 0.0), axis=1, keepdims=True
    )
    prob_ref[...] = as_line(raised / denominator)


def finish(place, stats, lengths, questions, tokens):
    smem, vmem = (pl.BlockSpec(memory_space=space) for space in (pltpu.SMEM, pltpu.VMEM))
    return pl.pallas_call(
        finish_kernel,
        in_specs=[smem, vmem, vmem, vmem],
        out_shape=(shape((1, tokens), f32), shape(lengths.shape, f32)),
        compiler_params=params(),
    )(place, stats, lengths, questions)


def on_device(
    resid,
    moe_gain,
    final_gain,
    router,
    w_gate,
    w_up,
    w_down,
    lm_head,
    expert_ids,
    target_ids,
    choice_len,
    choice_question,
):
    own_gate, own_up, own_down = w_gate[0], w_up[0], w_down[0]
    z_index = lax.axis_index("expert")
    v_index = lax.axis_index("vocab")
    place = jnp.stack([z_index, v_index // NC, v_index % NC]).astype(i32)

    other_gate = swap_cores(own_gate)
    other_up = swap_cores(own_up)
    other_down = swap_cores(own_down)
    other_head = swap_cores(lm_head)

    buckets, combine_weights = prelude(
        expert_ids[0], resid[0], moe_gain.reshape(1, -1), router.T
    )
    arrived = lax.all_to_all(buckets, "expert", split_axis=0, concat_axis=0, tiled=True)
    arrived, other_gate, other_up, other_down, other_head, own_head = tied(
        arrived, other_gate, other_up, other_down, other_head, lm_head
    )
    pair_head = swap_planes(own_head)
    pair_other = swap_cores(pair_head)

    def first(block, shift):
        return plane_shift(block, False, shift)

    def second(block, shift):
        return plane_shift(block, True, shift)

    line = stack(gather_four(arrived, first))
    rows = line.shape[0]
    half = rows // 2
    from_before = second(line, 1)
    from_after = second(line, -1)
    far_before = second(from_before[:half], 1)
    far_after = second(from_after[half:], -1)
    weights = (own_gate, own_up, other_gate, other_up)
    downs = (own_down, other_down)
    near_hidden = expand([line, from_before, from_after], weights)
    far_hidden = expand([far_before, far_after], weights)

    to_before, to_after = down_call(far_kernel, far_hidden, downs, (), (half, half))
    got_before = second(to_before, -1)
    got_after = second(to_after, 1)
    own_part, before_part, after_part = down_call(
        near_kernel, near_hidden, downs, (got_before, got_after), (rows, rows, rows)
    )
    pieces = line_sum([own_part, second(before_part, -1), second(after_part, 1)])
    outgoing = expert_sum(
        [pieces[0], first(pieces[1], -1), first(pieces[2], 1), first(pieces[3], 2)]
    )

    returned = lax.all_to_all(outgoing, "expert", split_axis=0, concat_axis=0, tiled=True)
    normed_out = combine(combine_weights, returned, resid[0], final_gain.reshape(1, -1))

    head_line = stack(gather_four(normed_out, lambda b, s: head_shift(b, False, s)))
    head_rows = gather_four(head_line, lambda b, s: head_shift(b, True, s))
    stats = head(place, target_ids, head_rows, (lm_head, other_head, pair_head, pair_other))
    gathered = lax.all_to_all(stats, ("expert", "vocab"), 0, 0, tiled=True)
    return finish(place, gathered, choice_len, choice_question, resid.shape[1])


def solution(mesh):
    return jax.shard_map(
        on_device,
        mesh=mesh,
        in_specs=(
            P("batch", ("expert", "vocab"), None),
            P(),
            P(),
            P(),
            P("expert", None, ("vocab", "batch")),
            P("expert", None, ("vocab", "batch")),
            P("expert", ("vocab", "batch"), None),
            P(("expert", "vocab"), None),
            P("batch", ("expert", "vocab"), None),
            P("batch", None),
            P("batch", None),
            P("batch", None),
        ),
        out_specs=(P("batch", ("expert", "vocab")), P("batch", None)),
        check_vma=False,
    )
```

```python
import functools

import jax
import jax.numpy as jnp
from jax import lax
from jax.experimental import pallas as pl
from jax.experimental.pallas import tpu as pltpu
from jax.sharding import PartitionSpec as P

epsilon = 1e-05
bf16 = jnp.bfloat16
f32 = jnp.float32
i32 = jnp.int32

NZ, NX, NC, NY = 8, 4, 2, 4
SLOTS = 3
VMEM_LIMIT = 14 * 2**20


def two_axis_perm(sizes, coords, axis_of, shift):
    pairs = []
    for index in range(sizes):
        place = coords(index)
        axis, step, size = axis_of(place)
        to = dict(place)
        to[axis] = (place[axis] + shift * step) % size
        pairs.append((index, coords(to)))
    return pairs


def plane_coords(index):
    if isinstance(index, dict):
        return (index["x"] * NC + index["c"]) * NY + index["y"]
    return {"x": index // (NC * NY), "c": index // NY % NC, "y": index % NY}


def head_coords(index):
    if isinstance(index, dict):
        return (index["z"] * NX + index["x"]) * NC + index["c"]
    return {"z": index // (NX * NC), "x": index // NC % NX, "c": index % NC}


def plane_shift(array, second, shift):
    def axis_of(place):
        return ("x", 1, NX) if (place["c"] == 0) != second else ("y", 1, NY)

    perm = two_axis_perm(NX * NC * NY, plane_coords, axis_of, shift)
    return lax.ppermute(array, ("vocab", "batch"), perm)


def head_shift(array, second, shift):
    def axis_of(place):
        return ("z", 2, NZ) if (place["c"] == 0) != second else ("x", 1, NX)

    perm = two_axis_perm(NZ * NX * NC, head_coords, axis_of, shift)
    return lax.ppermute(array, ("expert", "vocab"), perm)


def swap_cores(array):
    return lax.ppermute(array, "vocab", [(v, v ^ 1) for v in range(NX * NC)])


def swap_planes(array):
    return lax.ppermute(array, "expert", [(z, z ^ 1) for z in range(NZ)])


def gather_four(block, shift_by):
    return [block, shift_by(block, 1), shift_by(block, -1), shift_by(block, 2)]


def rel_step(rel):
    return jnp.where(rel == 1, -1, jnp.where(rel == 2, 1, jnp.where(rel == 3, 2, 0)))


def tied(*arrays):
    return lax.optimization_barrier(arrays)


def shape(dims, dtype):
    return jax.ShapeDtypeStruct(dims, dtype)


def iota(dims, axis):
    return lax.broadcasted_iota(i32, dims, axis)


def params():
    return pltpu.CompilerParams(vmem_limit_bytes=VMEM_LIMIT)


def cost(flops, moved):
    return pl.CostEstimate(flops=flops, bytes_accessed=moved, transcendentals=0)


def prelude_kernel(ids_ref, resid_ref, gain_ref, router_ref, buckets_ref, weights_ref):
    values = resid_ref[...].astype(f32)
    tokens = values.shape[0]
    mean_square = jnp.mean(values * values, axis=-1, keepdims=True)
    normed = (values * lax.rsqrt(mean_square + epsilon) * gain_ref[...]).astype(bf16)
    logits = lax.dot_general(
        normed, router_ref[...], (((1,), (1,)), ((), ())), preferred_element_type=f32
    )
    ids = ids_ref[...]
    id_a, id_b = ids[:, 0:1], ids[:, 1:2]
    earlier = (iota((tokens, tokens), 0) > iota((tokens, tokens), 1)).astype(f32)

    def slots(width):
        column = iota((tokens, NZ * width), 1)
        owner, slot = column // width, column % width
        match_a, match_b = id_a == owner, id_b == owner
        named = (match_a | match_b).astype(f32)
        rank = jnp.dot(earlier, named, preferred_element_type=f32)
        chosen = named * (rank == slot.astype(f32)).astype(f32)
        return chosen, match_a, match_b

    wide, _, _ = slots(8)
    chosen, match_a, match_b = slots(SLOTS)
    entry = iota(logits.shape, 1)
    pick_a = jnp.sum(jnp.where(id_a == entry, logits, 0.0), axis=1, keepdims=True)
    pick_b = jnp.sum(jnp.where(id_b == entry, logits, 0.0), axis=1, keepdims=True)
    gate_a = 1.0 / (1.0 + jnp.exp(pick_b - pick_a))
    gate_b = 1.0 / (jnp.exp(pick_a - pick_b) + 1.0)
    weights_ref[...] = chosen * (
        jnp.where(match_a, gate_a, 0.0) + jnp.where(match_b, gate_b, 0.0)
    )
    rows = lax.dot_general(
        wide.astype(bf16), normed, (((0,), (0,)), ((), ())), preferred_element_type=f32
    )
    for e in range(NZ):
        buckets_ref[e] = rows[8 * e : 8 * e + SLOTS].astype(bf16)


def prelude(ids, resid, gain, router):
    tokens, width = resid.shape
    return pl.pallas_call(
        prelude_kernel,
        out_shape=(
            shape((NZ, SLOTS, width), bf16),
            shape((tokens, NZ * SLOTS), f32),
        ),
        compiler_params=params(),
        cost_estimate=cost(2 * 64 * 8 * width, 8 * width),
    )(ids, resid, gain, router)


def stack_kernel(*refs, chunk):
    *parts, out_ref = refs
    width = out_ref.shape[1]

    @pl.loop(0, width // chunk)
    def _(step):
        columns = pl.ds(pl.multiple_of(step * chunk, chunk), chunk)
        pieces = []
        for part in parts:
            if len(part.shape) == 3:
                pieces += [part[e, :, columns].astype(f32) for e in range(part.shape[0])]
            else:
                pieces.append(part[:, columns].astype(f32))
        out_ref[:, columns] = jnp.concatenate(pieces).astype(bf16)


def stack(parts):
    width = parts[0].shape[-1]
    rows = sum(part.size // width for part in parts)
    return pl.pallas_call(
        functools.partial(stack_kernel, chunk=512),
        out_shape=shape((rows, width), bf16),
        compiler_params=params(),
        cost_estimate=cost(0, 4 * rows * width),
    )(*parts)


def expand_kernel(*refs, count):
    rows = [ref[...] for ref in refs[:count]]
    gate_a, up_a, gate_b, up_b, out_ref, total = refs[count:]
    step = pl.program_id(0)

    @pl.when(step == 0)
    def _():
        total[...] = jnp.zeros_like(total)

    block = rows[0] if count == 1 else jnp.concatenate(rows)
    for j, weight in enumerate((gate_a, up_a, gate_b, up_b)):
        total[j] += jnp.dot(block, weight[...], preferred_element_type=f32)

    @pl.when(step == pl.num_programs(0) - 1)
    def _():
        share = total.shape[2]
        for j in range(2):
            gate = total[2 * j]
            out_ref[:, j * share : (j + 1) * share] = (
                gate / (1.0 + jnp.exp(-gate)) * total[2 * j + 1]
            ).astype(bf16)


def expand(rows, weights):
    depth = 768
    count = len(rows)
    each, width = rows[0].shape
    share = weights[0].shape[1]
    return pl.pallas_call(
        functools.partial(expand_kernel, count=count),
        grid=(width // depth,),
        in_specs=[pl.BlockSpec((each, depth), lambda k: (0, k))] * count
        + [pl.BlockSpec((depth, share), lambda k: (k, 0))] * 4,
        out_specs=pl.BlockSpec((count * each, 2 * share), lambda k: (0, 0)),
        out_shape=shape((count * each, 2 * share), bf16),
        scratch_shapes=[pltpu.VMEM((4, count * each, share), f32)],
        compiler_params=params(),
        cost_estimate=cost(8 * count * each * width * share, 8 * width * share),
    )(*rows, *weights)


def contract(hidden, down_a, down_b):
    share = down_a.shape[0]
    return jnp.dot(hidden[:, :share], down_a, preferred_element_type=f32) + jnp.dot(
        hidden[:, share:], down_b, preferred_element_type=f32
    )


def far_kernel(hidden_ref, down_a, down_b, before_ref, after_ref):
    part = contract(hidden_ref[...], down_a[...], down_b[...]).astype(bf16)
    half = before_ref.shape[0]
    before_ref[...] = part[:half]
    after_ref[...] = part[half:]


def near_kernel(hidden_ref, down_a, down_b, got_before, got_after, own_ref, before_ref, after_ref):
    part = contract(hidden_ref[...], down_a[...], down_b[...])
    rows = own_ref.shape[0]
    half = rows // 2
    own_ref[...] = part[:rows].astype(bf16)
    before_ref[:half] = (part[rows : rows + half] + got_before[...].astype(f32)).astype(bf16)
    before_ref[half:] = part[rows + half : 2 * rows].astype(bf16)
    after_ref[:half] = part[2 * rows : 2 * rows + half].astype(bf16)
    after_ref[half:] = (part[2 * rows + half :] + got_after[...].astype(f32)).astype(bf16)


def down_call(kernel, hidden, downs, got, out_rows):
    tile = 1024
    share, width = downs[0].shape
    return pl.pallas_call(
        kernel,
        grid=(width // tile,),
        in_specs=[pl.BlockSpec(hidden.shape, lambda n: (0, 0))]
        + [pl.BlockSpec((share, tile), lambda n: (0, n))] * 2
        + [pl.BlockSpec((g.shape[0], tile), lambda n: (0, n)) for g in got],
        out_specs=[pl.BlockSpec((rows, tile), lambda n: (0, n)) for rows in out_rows],
        out_shape=[shape((rows, width), bf16) for rows in out_rows],
        compiler_params=params(),
        cost_estimate=cost(4 * hidden.shape[0] * share * width, 4 * share * width),
    )(hidden, *downs, *got)


def line_sum_kernel(own_ref, before_ref, after_ref, *outs):
    total = own_ref[...].astype(f32) + before_ref[...].astype(f32) + after_ref[...].astype(f32)
    rows = outs[0].shape[0]
    for j, out in enumerate(outs):
        out[...] = total[j * rows : (j + 1) * rows].astype(bf16)


def line_sum(parts):
    tile = 1536
    rows, width = parts[0].shape
    return pl.pallas_call(
        line_sum_kernel,
        grid=(width // tile,),
        in_specs=[pl.BlockSpec((rows, tile), lambda n: (0, n))] * 3,
        out_specs=[pl.BlockSpec((rows // 4, tile), lambda n: (0, n))] * 4,
        out_shape=[shape((rows // 4, width), bf16)] * 4,
        compiler_params=params(),
        cost_estimate=cost(3 * rows * width, 8 * rows * width),
    )(*parts)


def expert_sum_kernel(a, b, c, d, out_ref, *, chunk):
    @pl.loop(0, out_ref.shape[2] // chunk)
    def _(step):
        columns = pl.ds(pl.multiple_of(step * chunk, chunk), chunk)
        total = (
            a[:, columns].astype(f32)
            + b[:, columns].astype(f32)
            + c[:, columns].astype(f32)
            + d[:, columns].astype(f32)
        )
        for e in range(NZ):
            out_ref[e, :, columns] = total[SLOTS * e : SLOTS * e + SLOTS].astype(bf16)


def expert_sum(parts):
    width = parts[0].shape[1]
    return pl.pallas_call(
        functools.partial(expert_sum_kernel, chunk=512),
        out_shape=shape((NZ, SLOTS, width), bf16),
        compiler_params=params(),
        cost_estimate=cost(96 * width, 240 * width),
    )(*parts)


def combine_kernel(weights_ref, rows_ref, resid_ref, gain_ref, out_ref):
    mixed = resid_ref[...].astype(f32)
    weights = weights_ref[...]
    for e in range(NZ):
        rows = rows_ref[e].astype(f32)
        for s in range(SLOTS):
            slot = SLOTS * e + s
            mixed += weights[:, slot : slot + 1] * rows[s : s + 1]
    mean_square = jnp.mean(mixed * mixed, axis=-1, keepdims=True)
    out_ref[...] = (mixed * lax.rsqrt(mean_square + epsilon) * gain_ref[...]).astype(bf16)


def combine(weights, rows, resid, gain):
    return pl.pallas_call(
        combine_kernel,
        out_shape=shape(resid.shape, bf16),
        compiler_params=params(),
        cost_estimate=cost(48 * resid.size, 8 * resid.size),
    )(weights, rows, resid, gain)


def head_kernel(place_ref, targets_ref, r0, r1, r2, r3, t0, t1, t2, t3, out_ref, total):
    step = pl.program_id(0)

    @pl.when(step == 0)
    def _():
        total[...] = jnp.zeros_like(total)

    rows = jnp.concatenate([r0[...], r1[...], r2[...], r3[...]])
    share = t0.shape[0]
    for j, table in enumerate((t0, t1, t2, t3)):
        total[:, j * share : (j + 1) * share] += lax.dot_general(
            rows, table[...], (((1,), (1,)), ((), ())), preferred_element_type=f32
        )

    @pl.when(step == pl.num_programs(0) - 1)
    def _():
        z, x, c = place_ref[0], place_ref[1], place_ref[2]
        count = rows.shape[0]
        row = iota((count, 1), 0)
        outer, inner, token = rel_step(row // 32), rel_step(row // 8 % 4), row % 8
        z_half = (z // 2 + 4 + jnp.where(c == 0, inner, outer)) % 4
        x_seen = (x + 4 + jnp.where(c == 0, outer, inner)) % 4
        place = (z_half * NX + x_seen) * 8 + token
        position = ((2 * z_half + z % 2) * NX + x_seen) * (NC * 8) + c * 8 + token
        targets = targets_ref[...]
        wanted = jnp.sum(
            jnp.where(position == iota((count, targets.shape[1]), 1), targets, 0),
            axis=1,
            keepdims=True,
        )
        logits = total[...]
        entry = iota((1, 4 * share), 1)
        table, offset = entry // share, entry % share
        z_of = jnp.where(table < 2, z, z + 1 - 2 * (z % 2))
        c_of = jnp.where(table % 2 == 0, c, 1 - c)
        entry_id = ((z_of * NX + x) * NC + c_of) * share + offset
        top = jnp.max(logits, axis=1, keepdims=True)
        spread = jnp.sum(jnp.exp(logits - top), axis=1, keepdims=True)
        hit = jnp.sum(jnp.where(wanted == entry_id, logits, 0.0), axis=1, keepdims=True)
        here = place == iota((count, count), 1)
        figures = [
            jnp.sum(jnp.where(here, value, 0.0), axis=0, keepdims=True)
            for value in (top, spread, hit, hit)
        ]
        figures = jnp.concatenate(figures)
        for peer in range(out_ref.shape[0]):
            out_ref[peer] = figures


def head(place, targets, rows, tables):
    depth = 768
    width = rows[0].shape[1]
    share = tables[0].shape[0]
    count = sum(r.shape[0] for r in rows)
    whole = pl.BlockSpec(memory_space=pltpu.SMEM)
    return pl.pallas_call(
        head_kernel,
        grid=(width // depth,),
        in_specs=[whole, pl.BlockSpec(targets.shape, lambda k: (0, 0))]
        + [pl.BlockSpec((rows[0].shape[0], depth), lambda k: (0, k))] * 4
        + [pl.BlockSpec((share, depth), lambda k: (0, k))] * 4,
        out_specs=pl.BlockSpec((NZ * NX * NC, 4, count), lambda k: (0, 0, 0)),
        out_shape=shape((NZ * NX * NC, 4, count), f32),
        scratch_shapes=[pltpu.VMEM((count, 4 * share), f32)],
        compiler_params=params(),
        cost_estimate=cost(8 * count * share * width, 8 * share * width),
    )(place, targets, *rows, *tables)


def finish_kernel(place_ref, stats_ref, lengths_ref, questions_ref, logprob_ref, prob_ref):
    z, x, c = place_ref[0], place_ref[1], place_ref[2]
    count = lengths_ref.shape[1]
    local = stats_ref.shape[2]
    lengths = lengths_ref[...].astype(f32)
    questions = questions_ref[...].astype(f32)
    square = (count, count)
    same_place = iota(square, 0) == iota(square, 1)
    ends = jnp.sum(
        jnp.where(iota(square, 1) <= iota(square, 0), lengths, 0.0), axis=1, keepdims=True
    )

    def as_column(line):
        return jnp.sum(jnp.where(same_place, line, 0.0), axis=1, keepdims=True)

    def as_line(column):
        return jnp.sum(jnp.where(same_place, column, 0.0), axis=0, keepdims=True)

    length_column = as_column(lengths)
    starts = ends - length_column
    lane = iota((1, local), 1)
    choice_total = jnp.zeros((count, 1), f32)
    own = jnp.zeros((1, local), f32)
    for parity in range(2):
        for core in range(NC):
            senders = [
                (zz * NX + xx) * NC + core for zz in range(parity, NZ, 2) for xx in range(NX)
            ]
            figures = [stats_ref[j] for j in senders]
            best = functools.reduce(jnp.maximum, [f[0:1] for f in figures])
            summed = sum(f[1:2] * jnp.exp(f[0:1] - best) for f in figures)
            logprob = sum(f[2:3] for f in figures) - (best + jnp.log(summed))
            position = (
                (2 * (lane // 32) + parity) * (NX * NC * 8)
                + lane // 8 % 4 * (NC * 8)
                + core * 8
                + lane % 8
            ).astype(f32)
            member = (position >= starts) & (position < ends)
            choice_total += jnp.sum(jnp.where(member, logprob, 0.0), axis=1, keepdims=True)
            mine = (z % 2 == parity) & (c == core)
            own += jnp.where(mine, logprob, 0.0)
    tokens = logprob_ref.shape[1]
    first = (z // 2 * NX + x) * tokens
    column = jnp.sum(
        jnp.where(iota((tokens, local), 1) == first + iota((tokens, local), 0), own, 0.0),
        axis=1,
        keepdims=True,
    )
    eye = iota((tokens, tokens), 0) == iota((tokens, tokens), 1)
    logprob_ref[...] = jnp.sum(jnp.where(eye, column, 0.0), axis=0, keepdims=True)

    average = choice_total / length_column
    same_question = as_column(questions) == questions
    top = jnp.max(
        jnp.where(same_question, as_line(average), -jnp.inf), axis=1, keepdims=True
    )
    raised = jnp.exp(average - top)
    denominator = jnp.sum(
        jnp.where(same_question, as_line(raised), 0.0), axis=1, keepdims=True
    )
    prob_ref[...] = as_line(raised / denominator)


def finish(place, stats, lengths, questions, tokens):
    smem, vmem = (pl.BlockSpec(memory_space=space) for space in (pltpu.SMEM, pltpu.VMEM))
    return pl.pallas_call(
        finish_kernel,
        in_specs=[smem, vmem, vmem, vmem],
        out_shape=(shape((1, tokens), f32), shape(lengths.shape, f32)),
        compiler_params=params(),
    )(place, stats, lengths, questions)


def on_device(
    resid,
    moe_gain,
    final_gain,
    router,
    w_gate,
    w_up,
    w_down,
    lm_head,
    expert_ids,
    target_ids,
    choice_len,
    choice_question,
):
    own_gate, own_up, own_down = w_gate[0], w_up[0], w_down[0]
    z_index = lax.axis_index("expert")
    v_index = lax.axis_index("vocab")
    place = jnp.stack([z_index, v_index // NC, v_index % NC]).astype(i32)

    other_gate = swap_cores(own_gate)
    other_up = swap_cores(own_up)
    other_down = swap_cores(own_down)
    other_head = swap_cores(lm_head)

    buckets, combine_weights = prelude(
        expert_ids[0], resid[0], moe_gain.reshape(1, -1), router.T
    )
    arrived = lax.all_to_all(buckets, "expert", split_axis=0, concat_axis=0, tiled=True)
    arrived, other_gate, other_up, other_down, other_head, own_head = tied(
        arrived, other_gate, other_up, other_down, other_head, lm_head
    )
    pair_head = swap_planes(own_head)

    def first(block, shift):
        return plane_shift(block, False, shift)

    def second(block, shift):
        return plane_shift(block, True, shift)

    line = stack(gather_four(arrived, first))
    rows = line.shape[0]
    half = rows // 2
    from_before = second(line, 1)
    from_after = second(line, -1)
    far_before = second(from_before[:half], 1)
    far_after = second(from_after[half:], -1)
    weights = (own_gate, own_up, other_gate, other_up)
    downs = (own_down, other_down)
    near_hidden = expand([line, from_before, from_after], weights)
    near_hidden, far_before, far_after = tied(near_hidden, far_before, far_after)
    far_hidden = expand([far_before, far_after], weights)

    to_before, to_after = down_call(far_kernel, far_hidden, downs, (), (half, half))
    got_before = second(to_before, -1)
    got_after = second(to_after, 1)
    own_part, before_part, after_part = down_call(
        near_kernel, near_hidden, downs, (got_before, got_after), (rows, rows, rows)
    )
    pieces = line_sum([own_part, second(before_part, -1), second(after_part, 1)])
    pair_head, *pieces = tied(pair_head, *pieces)
    pair_other = swap_cores(pair_head)
    outgoing = expert_sum(
        [pieces[0], first(pieces[1], -1), first(pieces[2], 1), first(pieces[3], 2)]
    )

    returned = lax.all_to_all(outgoing, "expert", split_axis=0, concat_axis=0, tiled=True)
    normed_out = combine(combine_weights, returned, resid[0], final_gain.reshape(1, -1))

    head_line = stack(gather_four(normed_out, lambda b, s: head_shift(b, False, s)))
    head_rows = gather_four(head_line, lambda b, s: head_shift(b, True, s))
    stats = head(place, target_ids, head_rows, (lm_head, other_head, pair_head, pair_other))
    gathered = lax.all_to_all(stats, ("expert", "vocab"), 0, 0, tiled=True)
    return finish(place, gathered, choice_len, choice_question, resid.shape[1])


def solution(mesh):
    return jax.shard_map(
        on_device,
        mesh=mesh,
        in_specs=(
            P("batch", ("expert", "vocab"), None),
            P(),
            P(),
            P(),
            P("expert", None, ("vocab", "batch")),
            P("expert", None, ("vocab", "batch")),
            P("expert", ("vocab", "batch"), None),
            P(("expert", "vocab"), None),
            P("batch", ("expert", "vocab"), None),
            P("batch", None),
            P("batch", None),
            P("batch", None),
        ),
        out_specs=(P("batch", ("expert", "vocab")), P("batch", None)),
        check_vma=False,
    )
```

```python
import functools

import jax
import jax.numpy as jnp
from jax import lax
from jax.experimental import pallas as pl
from jax.experimental.pallas import tpu as pltpu
from jax.sharding import PartitionSpec as P

epsilon = 1e-05
bf16 = jnp.bfloat16
f32 = jnp.float32
i32 = jnp.int32

NZ, NX, NC, NY = 8, 4, 2, 4
SLOTS = 3
VMEM_LIMIT = 16 * 2**20


def two_axis_perm(sizes, coords, axis_of, shift):
    pairs = []
    for index in range(sizes):
        place = coords(index)
        axis, step, size = axis_of(place)
        to = dict(place)
        to[axis] = (place[axis] + shift * step) % size
        pairs.append((index, coords(to)))
    return pairs


def plane_coords(index):
    if isinstance(index, dict):
        return (index["x"] * NC + index["c"]) * NY + index["y"]
    return {"x": index // (NC * NY), "c": index // NY % NC, "y": index % NY}


def head_coords(index):
    if isinstance(index, dict):
        return (index["z"] * NX + index["x"]) * NC + index["c"]
    return {"z": index // (NX * NC), "x": index // NC % NX, "c": index % NC}


def plane_shift(array, second, shift):
    def axis_of(place):
        return ("x", 1, NX) if (place["c"] == 0) != second else ("y", 1, NY)

    perm = two_axis_perm(NX * NC * NY, plane_coords, axis_of, shift)
    return lax.ppermute(array, ("vocab", "batch"), perm)


def head_shift(array, second, shift):
    def axis_of(place):
        return ("z", 2, NZ) if (place["c"] == 0) != second else ("x", 1, NX)

    perm = two_axis_perm(NZ * NX * NC, head_coords, axis_of, shift)
    return lax.ppermute(array, ("expert", "vocab"), perm)


def swap_cores(array):
    return lax.ppermute(array, "vocab", [(v, v ^ 1) for v in range(NX * NC)])


def swap_planes(array):
    return lax.ppermute(array, "expert", [(z, z ^ 1) for z in range(NZ)])


def gather_four(block, shift_by):
    return [block, shift_by(block, 1), shift_by(block, -1), shift_by(block, 2)]


def rel_step(rel):
    return jnp.where(rel == 1, -1, jnp.where(rel == 2, 1, jnp.where(rel == 3, 2, 0)))


def tied(*arrays):
    return lax.optimization_barrier(arrays)


def shape(dims, dtype):
    return jax.ShapeDtypeStruct(dims, dtype)


def iota(dims, axis):
    return lax.broadcasted_iota(i32, dims, axis)


def params():
    return pltpu.CompilerParams(vmem_limit_bytes=VMEM_LIMIT)


def cost(flops, moved):
    return pl.CostEstimate(flops=flops, bytes_accessed=moved, transcendentals=0)


def normed_rows(resid_ref, gain_ref):
    values = resid_ref[...].astype(f32)
    mean_square = jnp.mean(values * values, axis=-1, keepdims=True)
    return (values * lax.rsqrt(mean_square + epsilon) * gain_ref[...]).astype(bf16)


def slots(ids, width):
    tokens = ids.shape[0]
    earlier = (iota((tokens, tokens), 0) > iota((tokens, tokens), 1)).astype(f32)
    column = iota((tokens, NZ * width), 1)
    owner, slot = column // width, column % width
    match_a, match_b = ids[:, 0:1] == owner, ids[:, 1:2] == owner
    named = (match_a | match_b).astype(f32)
    rank = jnp.dot(earlier, named, preferred_element_type=f32)
    chosen = named * (rank == slot.astype(f32)).astype(f32)
    return chosen, match_a, match_b


def bucket_kernel(ids_ref, resid_ref, gain_ref, buckets_ref):
    chosen, _, _ = slots(ids_ref[...], 8)
    rows = lax.dot_general(
        chosen.astype(bf16),
        normed_rows(resid_ref, gain_ref),
        (((0,), (0,)), ((), ())),
        preferred_element_type=f32,
    )
    for e in range(NZ):
        buckets_ref[e] = rows[8 * e : 8 * e + SLOTS].astype(bf16)


def bucket_rows(ids, resid, gain):
    tokens, width = resid.shape
    return pl.pallas_call(
        bucket_kernel,
        out_shape=shape((NZ, SLOTS, width), bf16),
        compiler_params=params(),
        cost_estimate=cost(2 * 64 * tokens * width, 8 * width),
    )(ids, resid, gain)


def gate_kernel(ids_ref, resid_ref, gain_ref, router_ref, weights_ref):
    logits = lax.dot_general(
        normed_rows(resid_ref, gain_ref),
        router_ref[...],
        (((1,), (1,)), ((), ())),
        preferred_element_type=f32,
    )
    ids = ids_ref[...]
    chosen, match_a, match_b = slots(ids, SLOTS)
    entry = iota(logits.shape, 1)
    pick_a = jnp.sum(jnp.where(ids[:, 0:1] == entry, logits, 0.0), axis=1, keepdims=True)
    pick_b = jnp.sum(jnp.where(ids[:, 1:2] == entry, logits, 0.0), axis=1, keepdims=True)
    gate_a = 1.0 / (1.0 + jnp.exp(pick_b - pick_a))
    gate_b = 1.0 / (jnp.exp(pick_a - pick_b) + 1.0)
    weights_ref[...] = chosen * (
        jnp.where(match_a, gate_a, 0.0) + jnp.where(match_b, gate_b, 0.0)
    )


def slot_gates(ids, resid, gain, router):
    tokens, width = resid.shape
    return pl.pallas_call(
        gate_kernel,
        out_shape=shape((tokens, NZ * SLOTS), f32),
        compiler_params=params(),
        cost_estimate=cost(16 * tokens * width, 8 * width),
    )(ids, resid, gain, router)


def stack_kernel(*refs, chunk):
    *parts, out_ref = refs
    width = out_ref.shape[1]

    @pl.loop(0, width // chunk)
    def _(step):
        columns = pl.ds(pl.multiple_of(step * chunk, chunk), chunk)
        pieces = []
        for part in parts:
            if len(part.shape) == 3:
                pieces += [part[e, :, columns].astype(f32) for e in range(part.shape[0])]
            else:
                pieces.append(part[:, columns].astype(f32))
        out_ref[:, columns] = jnp.concatenate(pieces).astype(bf16)


def stack(parts):
    width = parts[0].shape[-1]
    rows = sum(part.size // width for part in parts)
    return pl.pallas_call(
        functools.partial(stack_kernel, chunk=512),
        out_shape=shape((rows, width), bf16),
        compiler_params=params(),
        cost_estimate=cost(0, 4 * rows * width),
    )(*parts)


def expand_kernel(*refs, count):
    rows = [ref[...] for ref in refs[:count]]
    gate_a, up_a, gate_b, up_b, out_ref, total = refs[count:]
    step = pl.program_id(0)

    @pl.when(step == 0)
    def _():
        total[...] = jnp.zeros_like(total)

    block = rows[0] if count == 1 else jnp.concatenate(rows)
    for j, weight in enumerate((gate_a, up_a, gate_b, up_b)):
        total[j] += jnp.dot(block, weight[...], preferred_element_type=f32)

    @pl.when(step == pl.num_programs(0) - 1)
    def _():
        share = total.shape[2]
        for j in range(2):
            gate = total[2 * j]
            out_ref[:, j * share : (j + 1) * share] = (
                gate / (1.0 + jnp.exp(-gate)) * total[2 * j + 1]
            ).astype(bf16)


def expand(rows, weights):
    depth = 1536
    count = len(rows)
    each, width = rows[0].shape
    share = weights[0].shape[1]
    return pl.pallas_call(
        functools.partial(expand_kernel, count=count),
        grid=(width // depth,),
        in_specs=[pl.BlockSpec((each, depth), lambda k: (0, k))] * count
        + [pl.BlockSpec((depth, share), lambda k: (k, 0))] * 4,
        out_specs=pl.BlockSpec((count * each, 2 * share), lambda k: (0, 0)),
        out_shape=shape((count * each, 2 * share), bf16),
        scratch_shapes=[pltpu.VMEM((4, count * each, share), f32)],
        compiler_params=params(),
        cost_estimate=cost(8 * count * each * width * share, 8 * width * share),
    )(*rows, *weights)


def contract(hidden, down_a, down_b):
    share = down_a.shape[0]
    return jnp.dot(hidden[:, :share], down_a, preferred_element_type=f32) + jnp.dot(
        hidden[:, share:], down_b, preferred_element_type=f32
    )


def far_kernel(hidden_ref, down_a, down_b, before_ref, after_ref):
    part = contract(hidden_ref[...], down_a[...], down_b[...]).astype(bf16)
    half = before_ref.shape[0]
    before_ref[...] = part[:half]
    after_ref[...] = part[half:]


def near_kernel(hidden_ref, down_a, down_b, got_before, got_after, own_ref, before_ref, after_ref):
    part = contract(hidden_ref[...], down_a[...], down_b[...])
    rows = own_ref.shape[0]
    half = rows // 2
    own_ref[...] = part[:rows].astype(bf16)
    before_ref[:half] = (part[rows : rows + half] + got_before[...].astype(f32)).astype(bf16)
    before_ref[half:] = part[rows + half : 2 * rows].astype(bf16)
    after_ref[:half] = part[2 * rows : 2 * rows + half].astype(bf16)
    after_ref[half:] = (part[2 * rows + half :] + got_after[...].astype(f32)).astype(bf16)


def down_call(kernel, hidden, downs, got, out_rows):
    tile = 1024
    share, width = downs[0].shape
    return pl.pallas_call(
        kernel,
        grid=(width // tile,),
        in_specs=[pl.BlockSpec(hidden.shape, lambda n: (0, 0))]
        + [pl.BlockSpec((share, tile), lambda n: (0, n))] * 2
        + [pl.BlockSpec((g.shape[0], tile), lambda n: (0, n)) for g in got],
        out_specs=[pl.BlockSpec((rows, tile), lambda n: (0, n)) for rows in out_rows],
        out_shape=[shape((rows, width), bf16) for rows in out_rows],
        compiler_params=params(),
        cost_estimate=cost(4 * hidden.shape[0] * share * width, 4 * share * width),
    )(hidden, *downs, *got)


def line_sum_kernel(own_ref, before_ref, after_ref, *outs):
    total = own_ref[...].astype(f32) + before_ref[...].astype(f32) + after_ref[...].astype(f32)
    rows = outs[0].shape[0]
    for j, out in enumerate(outs):
        out[...] = total[j * rows : (j + 1) * rows].astype(bf16)


def line_sum(parts):
    tile = 1536
    rows, width = parts[0].shape
    return pl.pallas_call(
        line_sum_kernel,
        grid=(width // tile,),
        in_specs=[pl.BlockSpec((rows, tile), lambda n: (0, n))] * 3,
        out_specs=[pl.BlockSpec((rows // 4, tile), lambda n: (0, n))] * 4,
        out_shape=[shape((rows // 4, width), bf16)] * 4,
        compiler_params=params(),
        cost_estimate=cost(3 * rows * width, 8 * rows * width),
    )(*parts)


def expert_sum_kernel(a, b, c, d, out_ref, *, chunk):
    @pl.loop(0, out_ref.shape[2] // chunk)
    def _(step):
        columns = pl.ds(pl.multiple_of(step * chunk, chunk), chunk)
        total = (
            a[:, columns].astype(f32)
            + b[:, columns].astype(f32)
            + c[:, columns].astype(f32)
            + d[:, columns].astype(f32)
        )
        for e in range(NZ):
            out_ref[e, :, columns] = total[SLOTS * e : SLOTS * e + SLOTS].astype(bf16)


def expert_sum(parts):
    width = parts[0].shape[1]
    return pl.pallas_call(
        functools.partial(expert_sum_kernel, chunk=512),
        out_shape=shape((NZ, SLOTS, width), bf16),
        compiler_params=params(),
        cost_estimate=cost(96 * width, 240 * width),
    )(*parts)


def combine_kernel(weights_ref, rows_ref, resid_ref, gain_ref, out_ref):
    mixed = resid_ref[...].astype(f32)
    weights = weights_ref[...]
    for e in range(NZ):
        rows = rows_ref[e].astype(f32)
        for s in range(SLOTS):
            slot = SLOTS * e + s
            mixed += weights[:, slot : slot + 1] * rows[s : s + 1]
    mean_square = jnp.mean(mixed * mixed, axis=-1, keepdims=True)
    out_ref[...] = (mixed * lax.rsqrt(mean_square + epsilon) * gain_ref[...]).astype(bf16)


def combine(weights, rows, resid, gain):
    return pl.pallas_call(
        combine_kernel,
        out_shape=shape(resid.shape, bf16),
        compiler_params=params(),
        cost_estimate=cost(48 * resid.size, 8 * resid.size),
    )(weights, rows, resid, gain)


def head_kernel(place_ref, targets_ref, r0, r1, r2, r3, t0, t1, t2, t3, out_ref, total):
    step = pl.program_id(0)

    @pl.when(step == 0)
    def _():
        total[...] = jnp.zeros_like(total)

    rows = jnp.concatenate([r0[...], r1[...], r2[...], r3[...]])
    share = t0.shape[0]
    for j, table in enumerate((t0, t1, t2, t3)):
        total[j * share : (j + 1) * share] += lax.dot_general(
            table[...], rows, (((1,), (1,)), ((), ())), preferred_element_type=f32
        )

    @pl.when(step == pl.num_programs(0) - 1)
    def _():
        z, x, c = place_ref[0], place_ref[1], place_ref[2]
        count = rows.shape[0]
        row = iota((count, 1), 0)
        outer, inner, token = rel_step(row // 32), rel_step(row // 8 % 4), row % 8
        z_half = (z // 2 + 4 + jnp.where(c == 0, inner, outer)) % 4
        x_seen = (x + 4 + jnp.where(c == 0, outer, inner)) % 4
        place = (z_half * NX + x_seen) * 8 + token
        position = ((2 * z_half + z % 2) * NX + x_seen) * (NC * 8) + c * 8 + token
        targets = targets_ref[...]
        wanted = jnp.sum(
            jnp.where(position == iota((count, targets.shape[1]), 1), targets, 0),
            axis=1,
            keepdims=True,
        )
        same = iota((count, count), 0) == iota((count, count), 1)
        here = place == iota((count, count), 1)
        wanted = jnp.sum(jnp.where(same, wanted, 0), axis=0, keepdims=True)
        logits = total[...]
        entry = iota((4 * share, 1), 0)
        table, offset = entry // share, entry % share
        z_of = jnp.where(table < 2, z, z + 1 - 2 * (z % 2))
        c_of = jnp.where(table % 2 == 0, c, 1 - c)
        entry_id = ((z_of * NX + x) * NC + c_of) * share + offset
        top = jnp.max(logits, axis=0, keepdims=True)
        spread = jnp.sum(jnp.exp(logits - top), axis=0, keepdims=True)
        hit = jnp.sum(jnp.where(wanted == entry_id, logits, 0.0), axis=0, keepdims=True)
        figures = []
        for value in (top + jnp.log(spread), hit):
            column = jnp.sum(jnp.where(same, value, 0.0), axis=1, keepdims=True)
            figures.append(jnp.sum(jnp.where(here, column, 0.0), axis=0, keepdims=True))
        figures = jnp.concatenate(figures)
        for peer in range(out_ref.shape[0]):
            out_ref[peer] = figures


def head(place, targets, rows, tables):
    depth = 1536
    width = rows[0].shape[1]
    share = tables[0].shape[0]
    count = sum(r.shape[0] for r in rows)
    whole = pl.BlockSpec(memory_space=pltpu.SMEM)
    return pl.pallas_call(
        head_kernel,
        grid=(width // depth,),
        in_specs=[whole, pl.BlockSpec(targets.shape, lambda k: (0, 0))]
        + [pl.BlockSpec((rows[0].shape[0], depth), lambda k: (0, k))] * 4
        + [pl.BlockSpec((share, depth), lambda k: (0, k))] * 4,
        out_specs=pl.BlockSpec((NZ * NX * NC, 2, count), lambda k: (0, 0, 0)),
        out_shape=shape((NZ * NX * NC, 2, count), f32),
        scratch_shapes=[pltpu.VMEM((4 * share, count), f32)],
        compiler_params=params(),
        cost_estimate=cost(8 * count * share * width, 8 * share * width),
    )(place, targets, *rows, *tables)


def hold_kernel(*refs, count):
    sources, kept, sems = refs[:count], refs[count : 2 * count], refs[2 * count]
    copies = [
        pltpu.make_async_copy(source, keep, sems.at[j])
        for j, (source, keep) in enumerate(zip(sources, kept))
    ]
    for copy in copies:
        copy.start()
    for copy in copies:
        copy.wait()


def hold(arrays):
    count = len(arrays)
    return pl.pallas_call(
        functools.partial(hold_kernel, count=count),
        in_specs=[pl.BlockSpec(memory_space=pl.ANY)] * count,
        out_specs=[pl.BlockSpec(memory_space=pltpu.VMEM)] * count,
        out_shape=[pltpu.VMEM(a.shape, a.dtype) for a in arrays],
        scratch_shapes=[pltpu.SemaphoreType.DMA((count,))],
        compiler_params=params(),
        cost_estimate=cost(0, sum(2 * a.size for a in arrays)),
    )(*arrays)


def finish_kernel(place_ref, stats_ref, lengths_ref, questions_ref, logprob_ref, prob_ref):
    z, x, c = place_ref[0], place_ref[1], place_ref[2]
    count = lengths_ref.shape[1]
    local = stats_ref.shape[2]
    lengths = lengths_ref[...].astype(f32)
    questions = questions_ref[...].astype(f32)
    square = (count, count)
    same_place = iota(square, 0) == iota(square, 1)
    ends = jnp.sum(
        jnp.where(iota(square, 1) <= iota(square, 0), lengths, 0.0), axis=1, keepdims=True
    )

    def as_column(line):
        return jnp.sum(jnp.where(same_place, line, 0.0), axis=1, keepdims=True)

    def as_line(column):
        return jnp.sum(jnp.where(same_place, column, 0.0), axis=0, keepdims=True)

    length_column = as_column(lengths)
    starts = ends - length_column
    lane = iota((1, local), 1)
    choice_total = jnp.zeros((count, 1), f32)
    own = jnp.zeros((1, local), f32)
    for parity in range(2):
        for core in range(NC):
            senders = [
                (zz * NX + xx) * NC + core for zz in range(parity, NZ, 2) for xx in range(NX)
            ]
            figures = [stats_ref[j] for j in senders]
            best = functools.reduce(jnp.maximum, [f[0:1] for f in figures])
            summed = sum(jnp.exp(f[0:1] - best) for f in figures)
            logprob = sum(f[1:2] for f in figures) - (best + jnp.log(summed))
            position = (
                (2 * (lane // 32) + parity) * (NX * NC * 8)
                + lane // 8 % 4 * (NC * 8)
                + core * 8
                + lane % 8
            ).astype(f32)
            member = (position >= starts) & (position < ends)
            choice_total += jnp.sum(jnp.where(member, logprob, 0.0), axis=1, keepdims=True)
            mine = (z % 2 == parity) & (c == core)
            own += jnp.where(mine, logprob, 0.0)
    tokens = logprob_ref.shape[1]
    first = (z // 2 * NX + x) * tokens
    column = jnp.sum(
        jnp.where(iota((tokens, local), 1) == first + iota((tokens, local), 0), own, 0.0),
        axis=1,
        keepdims=True,
    )
    eye = iota((tokens, tokens), 0) == iota((tokens, tokens), 1)
    logprob_ref[...] = jnp.sum(jnp.where(eye, column, 0.0), axis=0, keepdims=True)

    average = choice_total / length_column
    same_question = as_column(questions) == questions
    top = jnp.max(
        jnp.where(same_question, as_line(average), -jnp.inf), axis=1, keepdims=True
    )
    raised = jnp.exp(average - top)
    denominator = jnp.sum(
        jnp.where(same_question, as_line(raised), 0.0), axis=1, keepdims=True
    )
    prob_ref[...] = as_line(raised / denominator)


def finish(place, stats, lengths, questions, tokens):
    smem, vmem = (pl.BlockSpec(memory_space=space) for space in (pltpu.SMEM, pltpu.VMEM))
    return pl.pallas_call(
        finish_kernel,
        in_specs=[smem, vmem, vmem, vmem],
        out_shape=(shape((1, tokens), f32), shape(lengths.shape, f32)),
        compiler_params=params(),
    )(place, stats, lengths, questions)


def on_device(
    resid,
    moe_gain,
    final_gain,
    router,
    w_gate,
    w_up,
    w_down,
    lm_head,
    expert_ids,
    target_ids,
    choice_len,
    choice_question,
):
    own_gate, own_up, own_down = w_gate[0], w_up[0], w_down[0]
    z_index = lax.axis_index("expert")
    v_index = lax.axis_index("vocab")
    place = jnp.stack([z_index, v_index // NC, v_index % NC]).astype(i32)

    other_gate = swap_cores(own_gate)
    other_up = swap_cores(own_up)
    other_down = swap_cores(own_down)
    other_head = swap_cores(lm_head)

    buckets = bucket_rows(expert_ids[0], resid[0], moe_gain.reshape(1, -1))
    arrived = lax.all_to_all(buckets, "expert", split_axis=0, concat_axis=0, tiled=True)
    arrived, other_gate, other_up, other_down, other_head, own_head, router = tied(
        arrived, other_gate, other_up, other_down, other_head, lm_head, router
    )
    combine_weights = slot_gates(expert_ids[0], resid[0], moe_gain.reshape(1, -1), router.T)
    pair_head = swap_planes(own_head)

    def first(block, shift):
        return plane_shift(block, False, shift)

    def second(block, shift):
        return plane_shift(block, True, shift)

    line = stack(gather_four(arrived, first))
    rows = line.shape[0]
    half = rows // 2
    from_before = second(line, 1)
    from_after = second(line, -1)
    weights = hold(tied(line, own_gate, own_up, other_gate, other_up)[1:])
    from_before, from_after, combine_weights, *weights = tied(
        from_before, from_after, combine_weights, *weights
    )
    far_before = second(from_before[:half], 1)
    far_after = second(from_after[half:], -1)
    downs = (own_down, other_down)
    near_hidden = expand([line, from_before, from_after], weights)
    near_hidden, far_before, far_after = tied(near_hidden, far_before, far_after)
    far_hidden = expand([far_before, far_after], weights)

    to_before, to_after = down_call(far_kernel, far_hidden, downs, (), (half, half))
    got_before = second(to_before, -1)
    got_after = second(to_after, 1)
    own_part, before_part, after_part = down_call(
        near_kernel, near_hidden, downs, (got_before, got_after), (rows, rows, rows)
    )
    pieces = line_sum([own_part, second(before_part, -1), second(after_part, 1)])
    back = (first(pieces[1], -1), first(pieces[2], 1), first(pieces[3], 2))
    *back, pair_head = tied(*back, pair_head)
    pair_other = swap_cores(pair_head)
    outgoing = expert_sum([pieces[0], *back])

    returned = lax.all_to_all(outgoing, "expert", split_axis=0, concat_axis=0, tiled=True)
    normed_out = combine(combine_weights, returned, resid[0], final_gain.reshape(1, -1))

    head_line = stack(gather_four(normed_out, lambda b, s: head_shift(b, False, s)))
    head_rows = gather_four(head_line, lambda b, s: head_shift(b, True, s))
    stats = head(place, target_ids, head_rows, hold([lm_head, other_head, pair_head, pair_other]))
    gathered = lax.all_to_all(stats, ("expert", "vocab"), 0, 0, tiled=True)
    return finish(place, gathered, choice_len, choice_question, resid.shape[1])


def solution(mesh):
    return jax.shard_map(
        on_device,
        mesh=mesh,
        in_specs=(
            P("batch", ("expert", "vocab"), None),
            P(),
            P(),
            P(),
            P("expert", None, ("vocab", "batch")),
            P("expert", None, ("vocab", "batch")),
            P("expert", ("vocab", "batch"), None),
            P(("expert", "vocab"), None),
            P("batch", ("expert", "vocab"), None),
            P("batch", None),
            P("batch", None),
            P("batch", None),
        ),
        out_specs=(P("batch", ("expert", "vocab")), P("batch", None)),
        check_vma=False,
    )
```

```python
import functools

import jax
import jax.numpy as jnp
from jax import lax
from jax.experimental import pallas as pl
from jax.experimental.pallas import tpu as pltpu
from jax.sharding import PartitionSpec as P

epsilon = 1e-05
bf16 = jnp.bfloat16
f32 = jnp.float32
i32 = jnp.int32

NZ, NX, NC, NY = 8, 4, 2, 4
SLOTS = 3
VMEM_LIMIT = 16 * 2**20


def two_axis_perm(sizes, coords, axis_of, shift):
    pairs = []
    for index in range(sizes):
        place = coords(index)
        axis, step, size = axis_of(place)
        to = dict(place)
        to[axis] = (place[axis] + shift * step) % size
        pairs.append((index, coords(to)))
    return pairs


def plane_coords(index):
    if isinstance(index, dict):
        return (index["x"] * NC + index["c"]) * NY + index["y"]
    return {"x": index // (NC * NY), "c": index // NY % NC, "y": index % NY}


def head_coords(index):
    if isinstance(index, dict):
        return (index["z"] * NX + index["x"]) * NC + index["c"]
    return {"z": index // (NX * NC), "x": index // NC % NX, "c": index % NC}


def plane_shift(array, second, shift):
    def axis_of(place):
        return ("x", 1, NX) if (place["c"] == 0) != second else ("y", 1, NY)

    perm = two_axis_perm(NX * NC * NY, plane_coords, axis_of, shift)
    return lax.ppermute(array, ("vocab", "batch"), perm)


def head_shift(array, second, shift):
    def axis_of(place):
        return ("z", 2, NZ) if (place["c"] == 0) != second else ("x", 1, NX)

    perm = two_axis_perm(NZ * NX * NC, head_coords, axis_of, shift)
    return lax.ppermute(array, ("expert", "vocab"), perm)


def swap_cores(array):
    return lax.ppermute(array, "vocab", [(v, v ^ 1) for v in range(NX * NC)])


def z_shift(array, shift):
    return lax.ppermute(array, "expert", [(z, (z + shift) % NZ) for z in range(NZ)])


def gather_four(block, shift_by):
    return [block, shift_by(block, 1), shift_by(block, -1), shift_by(block, 2)]


def rel_step(rel):
    return jnp.where(rel == 1, -1, jnp.where(rel == 2, 1, jnp.where(rel == 3, 2, 0)))


def tied(*arrays):
    return lax.optimization_barrier(arrays)


def shape(dims, dtype):
    return jax.ShapeDtypeStruct(dims, dtype)


def iota(dims, axis):
    return lax.broadcasted_iota(i32, dims, axis)


def params():
    return pltpu.CompilerParams(vmem_limit_bytes=VMEM_LIMIT)


def cost(flops, moved):
    return pl.CostEstimate(flops=flops, bytes_accessed=moved, transcendentals=0)


def normed_rows(resid_ref, gain_ref):
    values = resid_ref[...].astype(f32)
    mean_square = jnp.mean(values * values, axis=-1, keepdims=True)
    return (values * lax.rsqrt(mean_square + epsilon) * gain_ref[...]).astype(bf16)


def slots(ids, width):
    tokens = ids.shape[0]
    earlier = (iota((tokens, tokens), 0) > iota((tokens, tokens), 1)).astype(f32)
    column = iota((tokens, NZ * width), 1)
    owner, slot = column // width, column % width
    match_a, match_b = ids[:, 0:1] == owner, ids[:, 1:2] == owner
    named = (match_a | match_b).astype(f32)
    rank = jnp.dot(earlier, named, preferred_element_type=f32)
    chosen = named * (rank == slot.astype(f32)).astype(f32)
    return chosen, match_a, match_b


def bucket_kernel(ids_ref, resid_ref, gain_ref, buckets_ref):
    chosen, _, _ = slots(ids_ref[...], 8)
    rows = lax.dot_general(
        chosen.astype(bf16),
        normed_rows(resid_ref, gain_ref),
        (((0,), (0,)), ((), ())),
        preferred_element_type=f32,
    )
    for e in range(NZ):
        buckets_ref[e] = rows[8 * e : 8 * e + SLOTS].astype(bf16)


def bucket_rows(ids, resid, gain):
    tokens, width = resid.shape
    return pl.pallas_call(
        bucket_kernel,
        out_shape=shape((NZ, SLOTS, width), bf16),
        compiler_params=params(),
        cost_estimate=cost(2 * 64 * tokens * width, 8 * width),
    )(ids, resid, gain)


def gate_kernel(ids_ref, resid_ref, gain_ref, router_ref, weights_ref):
    logits = lax.dot_general(
        normed_rows(resid_ref, gain_ref),
        router_ref[...],
        (((1,), (1,)), ((), ())),
        preferred_element_type=f32,
    )
    ids = ids_ref[...]
    chosen, match_a, match_b = slots(ids, SLOTS)
    entry = iota(logits.shape, 1)
    pick_a = jnp.sum(jnp.where(ids[:, 0:1] == entry, logits, 0.0), axis=1, keepdims=True)
    pick_b = jnp.sum(jnp.where(ids[:, 1:2] == entry, logits, 0.0), axis=1, keepdims=True)
    gate_a = 1.0 / (1.0 + jnp.exp(pick_b - pick_a))
    gate_b = 1.0 / (jnp.exp(pick_a - pick_b) + 1.0)
    weights_ref[...] = chosen * (
        jnp.where(match_a, gate_a, 0.0) + jnp.where(match_b, gate_b, 0.0)
    )


def slot_gates(ids, resid, gain, router):
    tokens, width = resid.shape
    return pl.pallas_call(
        gate_kernel,
        out_shape=shape((tokens, NZ * SLOTS), f32),
        compiler_params=params(),
        cost_estimate=cost(16 * tokens * width, 8 * width),
    )(ids, resid, gain, router)


def stack_kernel(*refs, chunk):
    *parts, out_ref = refs
    width = out_ref.shape[1]

    @pl.loop(0, width // chunk)
    def _(step):
        columns = pl.ds(pl.multiple_of(step * chunk, chunk), chunk)
        pieces = []
        for part in parts:
            if len(part.shape) == 3:
                pieces += [part[e, :, columns].astype(f32) for e in range(part.shape[0])]
            else:
                pieces.append(part[:, columns].astype(f32))
        out_ref[:, columns] = jnp.concatenate(pieces).astype(bf16)


def stack(parts):
    width = parts[0].shape[-1]
    rows = sum(part.size // width for part in parts)
    return pl.pallas_call(
        functools.partial(stack_kernel, chunk=512),
        out_shape=shape((rows, width), bf16),
        compiler_params=params(),
        cost_estimate=cost(0, 4 * rows * width),
    )(*parts)


def expand_kernel(*refs, count):
    rows = [ref[...] for ref in refs[:count]]
    gate_a, up_a, gate_b, up_b, out_ref, total = refs[count:]
    step = pl.program_id(0)

    @pl.when(step == 0)
    def _():
        total[...] = jnp.zeros_like(total)

    block = rows[0] if count == 1 else jnp.concatenate(rows)
    for j, weight in enumerate((gate_a, up_a, gate_b, up_b)):
        total[j] += jnp.dot(block, weight[...], preferred_element_type=f32)

    @pl.when(step == pl.num_programs(0) - 1)
    def _():
        share = total.shape[2]
        for j in range(2):
            gate = total[2 * j]
            out_ref[:, j * share : (j + 1) * share] = (
                gate / (1.0 + jnp.exp(-gate)) * total[2 * j + 1]
            ).astype(bf16)


def expand(rows, weights):
    depth = 1536
    count = len(rows)
    each, width = rows[0].shape
    share = weights[0].shape[1]
    return pl.pallas_call(
        functools.partial(expand_kernel, count=count),
        grid=(width // depth,),
        in_specs=[pl.BlockSpec((each, depth), lambda k: (0, k))] * count
        + [pl.BlockSpec((depth, share), lambda k: (k, 0))] * 4,
        out_specs=pl.BlockSpec((count * each, 2 * share), lambda k: (0, 0)),
        out_shape=shape((count * each, 2 * share), bf16),
        scratch_shapes=[pltpu.VMEM((4, count * each, share), f32)],
        compiler_params=params(),
        cost_estimate=cost(8 * count * each * width * share, 8 * width * share),
    )(*rows, *weights)


def contract(hidden, down_a, down_b):
    share = down_a.shape[0]
    return jnp.dot(hidden[:, :share], down_a, preferred_element_type=f32) + jnp.dot(
        hidden[:, share:], down_b, preferred_element_type=f32
    )


def far_kernel(hidden_ref, down_a, down_b, before_ref, after_ref):
    part = contract(hidden_ref[...], down_a[...], down_b[...]).astype(bf16)
    half = before_ref.shape[0]
    before_ref[...] = part[:half]
    after_ref[...] = part[half:]


def near_kernel(hidden_ref, down_a, down_b, got_before, got_after, before_ref, after_ref):
    rows = before_ref.shape[0]
    half = rows // 2
    part = contract(hidden_ref[rows:], down_a[...], down_b[...])
    before_ref[:half] = (part[:half] + got_before[...].astype(f32)).astype(bf16)
    before_ref[half:] = part[half:rows].astype(bf16)
    after_ref[:half] = part[rows : rows + half].astype(bf16)
    after_ref[half:] = (part[rows + half :] + got_after[...].astype(f32)).astype(bf16)


def own_kernel(hidden_ref, down_a, down_b, own_ref):
    rows = own_ref.shape[0]
    own_ref[...] = contract(hidden_ref[:rows], down_a[...], down_b[...]).astype(bf16)


def down_call(kernel, hidden, downs, got, out_rows):
    tile = 1024
    share, width = downs[0].shape
    return pl.pallas_call(
        kernel,
        grid=(width // tile,),
        in_specs=[pl.BlockSpec(hidden.shape, lambda n: (0, 0))]
        + [pl.BlockSpec((share, tile), lambda n: (0, n))] * 2
        + [pl.BlockSpec((g.shape[0], tile), lambda n: (0, n)) for g in got],
        out_specs=[pl.BlockSpec((rows, tile), lambda n: (0, n)) for rows in out_rows],
        out_shape=[shape((rows, width), bf16) for rows in out_rows],
        compiler_params=params(),
        cost_estimate=cost(4 * hidden.shape[0] * share * width, 4 * share * width),
    )(hidden, *downs, *got)


def line_sum_kernel(own_ref, before_ref, after_ref, *outs):
    total = own_ref[...].astype(f32) + before_ref[...].astype(f32) + after_ref[...].astype(f32)
    rows = outs[0].shape[0]
    for j, out in enumerate(outs):
        out[...] = total[j * rows : (j + 1) * rows].astype(bf16)


def line_sum(parts):
    tile = 1536
    rows, width = parts[0].shape
    return pl.pallas_call(
        line_sum_kernel,
        grid=(width // tile,),
        in_specs=[pl.BlockSpec((rows, tile), lambda n: (0, n))] * 3,
        out_specs=[pl.BlockSpec((rows // 4, tile), lambda n: (0, n))] * 4,
        out_shape=[shape((rows // 4, width), bf16)] * 4,
        compiler_params=params(),
        cost_estimate=cost(3 * rows * width, 8 * rows * width),
    )(*parts)


def expert_sum_kernel(a, b, c, d, out_ref, *, chunk):
    @pl.loop(0, out_ref.shape[2] // chunk)
    def _(step):
        columns = pl.ds(pl.multiple_of(step * chunk, chunk), chunk)
        total = (
            a[:, columns].astype(f32)
            + b[:, columns].astype(f32)
            + c[:, columns].astype(f32)
            + d[:, columns].astype(f32)
        )
        for e in range(NZ):
            out_ref[e, :, columns] = total[SLOTS * e : SLOTS * e + SLOTS].astype(bf16)


def expert_sum(parts):
    width = parts[0].shape[1]
    return pl.pallas_call(
        functools.partial(expert_sum_kernel, chunk=512),
        out_shape=shape((NZ, SLOTS, width), bf16),
        compiler_params=params(),
        cost_estimate=cost(96 * width, 240 * width),
    )(*parts)


def combine_kernel(weights_ref, rows_ref, resid_ref, gain_ref, out_ref):
    mixed = resid_ref[...].astype(f32)
    weights = weights_ref[...]
    for e in range(NZ):
        rows = rows_ref[e].astype(f32)
        for s in range(SLOTS):
            slot = SLOTS * e + s
            mixed += weights[:, slot : slot + 1] * rows[s : s + 1]
    mean_square = jnp.mean(mixed * mixed, axis=-1, keepdims=True)
    out_ref[...] = (mixed * lax.rsqrt(mean_square + epsilon) * gain_ref[...]).astype(bf16)


def combine(weights, rows, resid, gain):
    return pl.pallas_call(
        combine_kernel,
        out_shape=shape(resid.shape, bf16),
        compiler_params=params(),
        cost_estimate=cost(48 * resid.size, 8 * resid.size),
    )(weights, rows, resid, gain)


def head_kernel(place_ref, targets_ref, r0, r1, r2, r3, *refs):
    *tables, out_ref, total = refs
    step = pl.program_id(0)

    @pl.when(step == 0)
    def _():
        total[...] = jnp.zeros_like(total)

    rows = jnp.concatenate([r0[...], r1[...], r2[...], r3[...]])
    share = tables[0].shape[0]
    at = 0
    for table in tables:
        total[at : at + table.shape[0]] += lax.dot_general(
            table[...], rows, (((1,), (1,)), ((), ())), preferred_element_type=f32
        )
        at += table.shape[0]

    @pl.when(step == pl.num_programs(0) - 1)
    def _():
        z, x, c = place_ref[0], place_ref[1], place_ref[2]
        count = rows.shape[0]
        row = iota((count, 1), 0)
        outer, inner, token = rel_step(row // 32), rel_step(row // 8 % 4), row % 8
        z_half = (z // 2 + 4 + jnp.where(c == 0, inner, outer)) % 4
        x_seen = (x + 4 + jnp.where(c == 0, outer, inner)) % 4
        place = (z_half * NX + x_seen) * 8 + token
        position = ((2 * z_half + z % 2) * NX + x_seen) * (NC * 8) + c * 8 + token
        targets = targets_ref[...]
        wanted = jnp.sum(
            jnp.where(position == iota((count, targets.shape[1]), 1), targets, 0),
            axis=1,
            keepdims=True,
        )
        same = iota((count, count), 0) == iota((count, count), 1)
        here = place == iota((count, count), 1)
        wanted = jnp.sum(jnp.where(same, wanted, 0), axis=0, keepdims=True)
        logits = total[...]
        half = share // 2
        entry = iota((4 * share, 1), 0)
        part = entry // half
        shared, upper = part >= 4, part >= 6
        z_of = jnp.where(shared, (z + NZ + jnp.where(upper, 1, -1)) % NZ, z)
        other = jnp.where(shared, part % 2, jnp.where(part >= 2, 1, 0))
        c_of = c + other * (1 - 2 * c)
        offset = jnp.where(
            shared, entry % half + jnp.where(upper, half, 0), entry % share
        )
        entry_id = ((z_of * NX + x) * NC + c_of) * share + offset
        top = jnp.max(logits, axis=0, keepdims=True)
        spread = jnp.sum(jnp.exp(logits - top), axis=0, keepdims=True)
        hit = jnp.sum(jnp.where(wanted == entry_id, logits, 0.0), axis=0, keepdims=True)
        figures = []
        for value in (top + jnp.log(spread), hit):
            column = jnp.sum(jnp.where(same, value, 0.0), axis=1, keepdims=True)
            figures.append(jnp.sum(jnp.where(here, column, 0.0), axis=0, keepdims=True))
        figures = jnp.concatenate(figures)
        for peer in range(out_ref.shape[0]):
            out_ref[peer] = figures


def head(place, targets, rows, tables):
    depth = 1536
    width = rows[0].shape[1]
    share = tables[0].shape[0]
    count = sum(r.shape[0] for r in rows)
    whole = pl.BlockSpec(memory_space=pltpu.SMEM)
    return pl.pallas_call(
        head_kernel,
        grid=(width // depth,),
        in_specs=[whole, pl.BlockSpec(targets.shape, lambda k: (0, 0))]
        + [pl.BlockSpec((rows[0].shape[0], depth), lambda k: (0, k))] * 4
        + [pl.BlockSpec((t.shape[0], depth), lambda k: (0, k)) for t in tables],
        out_specs=pl.BlockSpec((NZ * NX * NC, 2, count), lambda k: (0, 0, 0)),
        out_shape=shape((NZ * NX * NC, 2, count), f32),
        scratch_shapes=[pltpu.VMEM((4 * share, count), f32)],
        compiler_params=params(),
        cost_estimate=cost(8 * count * share * width, 8 * share * width),
    )(place, targets, *rows, *tables)


def hold_kernel(*refs, count):
    sources, kept, sems = refs[:count], refs[count : 2 * count], refs[2 * count]
    copies = [
        pltpu.make_async_copy(source, keep, sems.at[j])
        for j, (source, keep) in enumerate(zip(sources, kept))
    ]
    for copy in copies:
        copy.start()
    for copy in copies:
        copy.wait()


def hold(arrays):
    count = len(arrays)
    return pl.pallas_call(
        functools.partial(hold_kernel, count=count),
        in_specs=[pl.BlockSpec(memory_space=pl.ANY)] * count,
        out_specs=[pl.BlockSpec(memory_space=pltpu.VMEM)] * count,
        out_shape=[pltpu.VMEM(a.shape, a.dtype) for a in arrays],
        scratch_shapes=[pltpu.SemaphoreType.DMA((count,))],
        compiler_params=params(),
        cost_estimate=cost(0, sum(2 * a.size for a in arrays)),
    )(*arrays)


def finish_kernel(place_ref, stats_ref, lengths_ref, questions_ref, logprob_ref, prob_ref):
    z, x, c = place_ref[0], place_ref[1], place_ref[2]
    count = lengths_ref.shape[1]
    local = stats_ref.shape[2]
    lengths = lengths_ref[...].astype(f32)
    questions = questions_ref[...].astype(f32)
    square = (count, count)
    same_place = iota(square, 0) == iota(square, 1)
    ends = jnp.sum(
        jnp.where(iota(square, 1) <= iota(square, 0), lengths, 0.0), axis=1, keepdims=True
    )

    def as_column(line):
        return jnp.sum(jnp.where(same_place, line, 0.0), axis=1, keepdims=True)

    def as_line(column):
        return jnp.sum(jnp.where(same_place, column, 0.0), axis=0, keepdims=True)

    length_column = as_column(lengths)
    starts = ends - length_column
    lane = iota((1, local), 1)
    choice_total = jnp.zeros((count, 1), f32)
    own = jnp.zeros((1, local), f32)
    for parity in range(2):
        for core in range(NC):
            senders = [
                (zz * NX + xx) * NC + core for zz in range(parity, NZ, 2) for xx in range(NX)
            ]
            figures = [stats_ref[j] for j in senders]
            best = functools.reduce(jnp.maximum, [f[0:1] for f in figures])
            summed = sum(jnp.exp(f[0:1] - best) for f in figures)
            logprob = sum(f[1:2] for f in figures) - (best + jnp.log(summed))
            position = (
                (2 * (lane // 32) + parity) * (NX * NC * 8)
                + lane // 8 % 4 * (NC * 8)
                + core * 8
                + lane % 8
            ).astype(f32)
            member = (position >= starts) & (position < ends)
            choice_total += jnp.sum(jnp.where(member, logprob, 0.0), axis=1, keepdims=True)
            mine = (z % 2 == parity) & (c == core)
            own += jnp.where(mine, logprob, 0.0)
    tokens = logprob_ref.shape[1]
    first = (z // 2 * NX + x) * tokens
    column = jnp.sum(
        jnp.where(iota((tokens, local), 1) == first + iota((tokens, local), 0), own, 0.0),
        axis=1,
        keepdims=True,
    )
    eye = iota((tokens, tokens), 0) == iota((tokens, tokens), 1)
    logprob_ref[...] = jnp.sum(jnp.where(eye, column, 0.0), axis=0, keepdims=True)

    average = choice_total / length_column
    same_question = as_column(questions) == questions
    top = jnp.max(
        jnp.where(same_question, as_line(average), -jnp.inf), axis=1, keepdims=True
    )
    raised = jnp.exp(average - top)
    denominator = jnp.sum(
        jnp.where(same_question, as_line(raised), 0.0), axis=1, keepdims=True
    )
    prob_ref[...] = as_line(raised / denominator)


def finish(place, stats, lengths, questions, tokens):
    smem, vmem = (pl.BlockSpec(memory_space=space) for space in (pltpu.SMEM, pltpu.VMEM))
    return pl.pallas_call(
        finish_kernel,
        in_specs=[smem, vmem, vmem, vmem],
        out_shape=(shape((1, tokens), f32), shape(lengths.shape, f32)),
        compiler_params=params(),
    )(place, stats, lengths, questions)


def on_device(
    resid,
    moe_gain,
    final_gain,
    router,
    w_gate,
    w_up,
    w_down,
    lm_head,
    expert_ids,
    target_ids,
    choice_len,
    choice_question,
):
    own_gate, own_up, own_down = w_gate[0], w_up[0], w_down[0]
    z_index = lax.axis_index("expert")
    v_index = lax.axis_index("vocab")
    place = jnp.stack([z_index, v_index // NC, v_index % NC]).astype(i32)

    other_gate = swap_cores(own_gate)
    other_up = swap_cores(own_up)
    other_down = swap_cores(own_down)
    other_head = swap_cores(lm_head)

    buckets = bucket_rows(expert_ids[0], resid[0], moe_gain.reshape(1, -1))
    arrived = lax.all_to_all(buckets, "expert", split_axis=0, concat_axis=0, tiled=True)
    arrived, other_gate, other_up, other_down, other_head, own_head, router = tied(
        arrived, other_gate, other_up, other_down, other_head, lm_head, router
    )
    combine_weights = slot_gates(expert_ids[0], resid[0], moe_gain.reshape(1, -1), router.T)
    head_half = own_head.shape[0] // 2
    low_head = z_shift(own_head[:head_half], 1)
    high_head = z_shift(own_head[head_half:], -1)

    def first(block, shift):
        return plane_shift(block, False, shift)

    def second(block, shift):
        return plane_shift(block, True, shift)

    line = stack(gather_four(arrived, first))
    rows = line.shape[0]
    half = rows // 2
    from_before = second(line, 1)
    from_after = second(line, -1)
    weights = hold(tied(line, own_gate, own_up, other_gate, other_up)[1:])
    from_before, from_after, combine_weights, *weights = tied(
        from_before, from_after, combine_weights, *weights
    )
    far_before = second(from_before[:half], 1)
    far_after = second(from_after[half:], -1)
    downs = (own_down, other_down)
    near_hidden = expand([line, from_before, from_after], weights)
    near_hidden, far_before, far_after = tied(near_hidden, far_before, far_after)
    far_hidden = expand([far_before, far_after], weights)

    to_before, to_after = down_call(far_kernel, far_hidden, downs, (), (half, half))
    got_before = second(to_before, -1)
    got_after = second(to_after, 1)
    got_before, low_head, high_head = tied(got_before, low_head, high_head)
    before_part, after_part = down_call(
        near_kernel, near_hidden, downs, (got_before, got_after), (rows, rows)
    )
    (own_part,) = down_call(own_kernel, near_hidden, downs, (), (rows,))
    own_part, low_head, high_head = tied(own_part, low_head, high_head)
    low_other = swap_cores(low_head)
    high_other = swap_cores(high_head)
    pieces = line_sum([own_part, second(before_part, -1), second(after_part, 1)])
    back = (first(pieces[1], -1), first(pieces[2], 1), first(pieces[3], 2))
    outgoing = expert_sum([pieces[0], *back])

    returned = lax.all_to_all(outgoing, "expert", split_axis=0, concat_axis=0, tiled=True)
    normed_out = combine(combine_weights, returned, resid[0], final_gain.reshape(1, -1))

    head_line = stack(gather_four(normed_out, lambda b, s: head_shift(b, False, s)))
    head_rows = gather_four(head_line, lambda b, s: head_shift(b, True, s))
    stats = head(place, target_ids, head_rows, hold([lm_head, other_head, low_head, low_other, high_head, high_other]))
    gathered = lax.all_to_all(stats, ("expert", "vocab"), 0, 0, tiled=True)
    return finish(place, gathered, choice_len, choice_question, resid.shape[1])


def solution(mesh):
    return jax.shard_map(
        on_device,
        mesh=mesh,
        in_specs=(
            P("batch", ("expert", "vocab"), None),
            P(),
            P(),
            P(),
            P("expert", None, ("vocab", "batch")),
            P("expert", None, ("vocab", "batch")),
            P("expert", ("vocab", "batch"), None),
            P(("expert", "vocab"), None),
            P("batch", ("expert", "vocab"), None),
            P("batch", None),
            P("batch", None),
            P("batch", None),
        ),
        out_specs=(P("batch", ("expert", "vocab")), P("batch", None)),
        check_vma=False,
    )
```

```python
import functools

import jax
import jax.numpy as jnp
from jax import lax
from jax.experimental import pallas as pl
from jax.experimental.pallas import tpu as pltpu
from jax.sharding import PartitionSpec as P

epsilon = 1e-05
bf16 = jnp.bfloat16
f32 = jnp.float32
i32 = jnp.int32

NZ, NX, NC, NY = 8, 4, 2, 4
SLOTS = 3
VMEM_LIMIT = 16 * 2**20


def two_axis_perm(sizes, coords, axis_of, shift):
    pairs = []
    for index in range(sizes):
        place = coords(index)
        axis, step, size = axis_of(place)
        to = dict(place)
        to[axis] = (place[axis] + shift * step) % size
        pairs.append((index, coords(to)))
    return pairs


def plane_coords(index):
    if isinstance(index, dict):
        return (index["x"] * NC + index["c"]) * NY + index["y"]
    return {"x": index // (NC * NY), "c": index // NY % NC, "y": index % NY}


def head_coords(index):
    if isinstance(index, dict):
        return (index["z"] * NX + index["x"]) * NC + index["c"]
    return {"z": index // (NX * NC), "x": index // NC % NX, "c": index % NC}


def plane_shift(array, second, shift):
    def axis_of(place):
        return ("x", 1, NX) if (place["c"] == 0) != second else ("y", 1, NY)

    perm = two_axis_perm(NX * NC * NY, plane_coords, axis_of, shift)
    return lax.ppermute(array, ("vocab", "batch"), perm)


def head_shift(array, second, shift):
    def axis_of(place):
        return ("x", 1, NX) if second else ("z", 2, NZ)

    perm = two_axis_perm(NZ * NX * NC, head_coords, axis_of, shift)
    return lax.ppermute(array, ("expert", "vocab"), perm)


def swap_cores(array):
    return lax.ppermute(array, "vocab", [(v, v ^ 1) for v in range(NX * NC)])


def z_shift(array, shift):
    return lax.ppermute(array, "expert", [(z, (z + shift) % NZ) for z in range(NZ)])


def gather_four(block, shift_by):
    return [block, shift_by(block, 1), shift_by(block, -1), shift_by(block, 2)]


def rel_step(rel):
    return jnp.where(rel == 1, -1, jnp.where(rel == 2, 1, jnp.where(rel == 3, 2, 0)))


def tied(*arrays):
    return lax.optimization_barrier(arrays)


def shape(dims, dtype):
    return jax.ShapeDtypeStruct(dims, dtype)


def iota(dims, axis):
    return lax.broadcasted_iota(i32, dims, axis)


def params():
    return pltpu.CompilerParams(vmem_limit_bytes=VMEM_LIMIT)


def cost(flops, moved):
    return pl.CostEstimate(flops=flops, bytes_accessed=moved, transcendentals=0)


def normed_rows(resid_ref, gain_ref):
    values = resid_ref[...].astype(f32)
    mean_square = jnp.mean(values * values, axis=-1, keepdims=True)
    return (values * lax.rsqrt(mean_square + epsilon) * gain_ref[...]).astype(bf16)


def slots(ids, width):
    tokens = ids.shape[0]
    earlier = (iota((tokens, tokens), 0) > iota((tokens, tokens), 1)).astype(f32)
    column = iota((tokens, NZ * width), 1)
    owner, slot = column // width, column % width
    match_a, match_b = ids[:, 0:1] == owner, ids[:, 1:2] == owner
    named = (match_a | match_b).astype(f32)
    rank = jnp.dot(earlier, named, preferred_element_type=f32)
    chosen = named * (rank == slot.astype(f32)).astype(f32)
    return chosen, match_a, match_b


def bucket_kernel(ids_ref, resid_ref, gain_ref, buckets_ref):
    chosen, _, _ = slots(ids_ref[...], 8)
    rows = lax.dot_general(
        chosen.astype(bf16),
        normed_rows(resid_ref, gain_ref),
        (((0,), (0,)), ((), ())),
        preferred_element_type=f32,
    )
    for e in range(NZ):
        buckets_ref[e] = rows[8 * e : 8 * e + SLOTS].astype(bf16)


def bucket_rows(ids, resid, gain):
    tokens, width = resid.shape
    return pl.pallas_call(
        bucket_kernel,
        out_shape=shape((NZ, SLOTS, width), bf16),
        compiler_params=params(),
        cost_estimate=cost(2 * 64 * tokens * width, 8 * width),
    )(ids, resid, gain)


def gate_kernel(ids_ref, resid_ref, gain_ref, router_ref, weights_ref):
    logits = lax.dot_general(
        normed_rows(resid_ref, gain_ref),
        router_ref[...],
        (((1,), (1,)), ((), ())),
        preferred_element_type=f32,
    )
    ids = ids_ref[...]
    chosen, match_a, match_b = slots(ids, SLOTS)
    entry = iota(logits.shape, 1)
    pick_a = jnp.sum(jnp.where(ids[:, 0:1] == entry, logits, 0.0), axis=1, keepdims=True)
    pick_b = jnp.sum(jnp.where(ids[:, 1:2] == entry, logits, 0.0), axis=1, keepdims=True)
    gate_a = 1.0 / (1.0 + jnp.exp(pick_b - pick_a))
    gate_b = 1.0 / (jnp.exp(pick_a - pick_b) + 1.0)
    weights_ref[...] = chosen * (
        jnp.where(match_a, gate_a, 0.0) + jnp.where(match_b, gate_b, 0.0)
    )


def slot_gates(ids, resid, gain, router):
    tokens, width = resid.shape
    return pl.pallas_call(
        gate_kernel,
        out_shape=shape((tokens, NZ * SLOTS), f32),
        compiler_params=params(),
        cost_estimate=cost(16 * tokens * width, 8 * width),
    )(ids, resid, gain, router)


def stack_kernel(*refs, chunk):
    *parts, out_ref = refs
    width = out_ref.shape[1]

    @pl.loop(0, width // chunk)
    def _(step):
        columns = pl.ds(pl.multiple_of(step * chunk, chunk), chunk)
        pieces = []
        for part in parts:
            if len(part.shape) == 3:
                pieces += [part[e, :, columns].astype(f32) for e in range(part.shape[0])]
            else:
                pieces.append(part[:, columns].astype(f32))
        out_ref[:, columns] = jnp.concatenate(pieces).astype(bf16)


def stack(parts):
    width = parts[0].shape[-1]
    rows = sum(part.size // width for part in parts)
    return pl.pallas_call(
        functools.partial(stack_kernel, chunk=512),
        out_shape=shape((rows, width), bf16),
        compiler_params=params(),
        cost_estimate=cost(0, 4 * rows * width),
    )(*parts)


def expand_kernel(*refs, count):
    rows = [ref[...] for ref in refs[:count]]
    gate_a, up_a, gate_b, up_b, out_ref, total = refs[count:]
    step = pl.program_id(0)

    @pl.when(step == 0)
    def _():
        total[...] = jnp.zeros_like(total)

    block = rows[0] if count == 1 else jnp.concatenate(rows)
    for j, weight in enumerate((gate_a, up_a, gate_b, up_b)):
        total[j] += jnp.dot(block, weight[...], preferred_element_type=f32)

    @pl.when(step == pl.num_programs(0) - 1)
    def _():
        share = total.shape[2]
        for j in range(2):
            gate = total[2 * j]
            out_ref[:, j * share : (j + 1) * share] = (
                gate / (1.0 + jnp.exp(-gate)) * total[2 * j + 1]
            ).astype(bf16)


def expand(rows, weights):
    depth = 1536
    count = len(rows)
    each, width = rows[0].shape
    share = weights[0].shape[1]
    return pl.pallas_call(
        functools.partial(expand_kernel, count=count),
        grid=(width // depth,),
        in_specs=[pl.BlockSpec((each, depth), lambda k: (0, k))] * count
        + [pl.BlockSpec((depth, share), lambda k: (k, 0))] * 4,
        out_specs=pl.BlockSpec((count * each, 2 * share), lambda k: (0, 0)),
        out_shape=shape((count * each, 2 * share), bf16),
        scratch_shapes=[pltpu.VMEM((4, count * each, share), f32)],
        compiler_params=params(),
        cost_estimate=cost(8 * count * each * width * share, 8 * width * share),
    )(*rows, *weights)


def contract(hidden, down_a, down_b):
    share = down_a.shape[0]
    return jnp.dot(hidden[:, :share], down_a, preferred_element_type=f32) + jnp.dot(
        hidden[:, share:], down_b, preferred_element_type=f32
    )


def far_kernel(hidden_ref, down_a, down_b, before_ref, after_ref):
    part = contract(hidden_ref[...], down_a[...], down_b[...]).astype(bf16)
    half = before_ref.shape[0]
    before_ref[...] = part[:half]
    after_ref[...] = part[half:]


def near_kernel(hidden_ref, down_a, down_b, got_before, got_after, before_ref, after_ref):
    rows = before_ref.shape[0]
    half = rows // 2
    part = contract(hidden_ref[rows:], down_a[...], down_b[...])
    before_ref[:half] = (part[:half] + got_before[...].astype(f32)).astype(bf16)
    before_ref[half:] = part[half:rows].astype(bf16)
    after_ref[:half] = part[rows : rows + half].astype(bf16)
    after_ref[half:] = (part[rows + half :] + got_after[...].astype(f32)).astype(bf16)


def own_kernel(hidden_ref, down_a, down_b, own_ref):
    rows = own_ref.shape[0]
    own_ref[...] = contract(hidden_ref[:rows], down_a[...], down_b[...]).astype(bf16)


def down_call(kernel, hidden, downs, got, out_rows):
    tile = 1024
    share, width = downs[0].shape
    return pl.pallas_call(
        kernel,
        grid=(width // tile,),
        in_specs=[pl.BlockSpec(hidden.shape, lambda n: (0, 0))]
        + [pl.BlockSpec((share, tile), lambda n: (0, n))] * 2
        + [pl.BlockSpec((g.shape[0], tile), lambda n: (0, n)) for g in got],
        out_specs=[pl.BlockSpec((rows, tile), lambda n: (0, n)) for rows in out_rows],
        out_shape=[shape((rows, width), bf16) for rows in out_rows],
        compiler_params=params(),
        cost_estimate=cost(4 * hidden.shape[0] * share * width, 4 * share * width),
    )(hidden, *downs, *got)


def line_sum_kernel(own_ref, before_ref, after_ref, *outs):
    total = own_ref[...].astype(f32) + before_ref[...].astype(f32) + after_ref[...].astype(f32)
    rows = outs[0].shape[0]
    for j, out in enumerate(outs):
        out[...] = total[j * rows : (j + 1) * rows].astype(bf16)


def line_sum(parts):
    tile = 1536
    rows, width = parts[0].shape
    return pl.pallas_call(
        line_sum_kernel,
        grid=(width // tile,),
        in_specs=[pl.BlockSpec((rows, tile), lambda n: (0, n))] * 3,
        out_specs=[pl.BlockSpec((rows // 4, tile), lambda n: (0, n))] * 4,
        out_shape=[shape((rows // 4, width), bf16)] * 4,
        compiler_params=params(),
        cost_estimate=cost(3 * rows * width, 8 * rows * width),
    )(*parts)


def expert_sum_kernel(a, b, c, d, out_ref, *, chunk):
    @pl.loop(0, out_ref.shape[2] // chunk)
    def _(step):
        columns = pl.ds(pl.multiple_of(step * chunk, chunk), chunk)
        total = (
            a[:, columns].astype(f32)
            + b[:, columns].astype(f32)
            + c[:, columns].astype(f32)
            + d[:, columns].astype(f32)
        )
        for e in range(NZ):
            out_ref[e, :, columns] = total[SLOTS * e : SLOTS * e + SLOTS].astype(bf16)


def expert_sum(parts):
    width = parts[0].shape[1]
    return pl.pallas_call(
        functools.partial(expert_sum_kernel, chunk=512),
        out_shape=shape((NZ, SLOTS, width), bf16),
        compiler_params=params(),
        cost_estimate=cost(96 * width, 240 * width),
    )(*parts)


def combine_kernel(weights_ref, rows_ref, resid_ref, gain_ref, out_ref):
    mixed = resid_ref[...].astype(f32)
    weights = weights_ref[...]
    for e in range(NZ):
        rows = rows_ref[e].astype(f32)
        for s in range(SLOTS):
            slot = SLOTS * e + s
            mixed += weights[:, slot : slot + 1] * rows[s : s + 1]
    mean_square = jnp.mean(mixed * mixed, axis=-1, keepdims=True)
    out_ref[...] = (mixed * lax.rsqrt(mean_square + epsilon) * gain_ref[...]).astype(bf16)


def combine(weights, rows, resid, gain):
    return pl.pallas_call(
        combine_kernel,
        out_shape=shape(resid.shape, bf16),
        compiler_params=params(),
        cost_estimate=cost(48 * resid.size, 8 * resid.size),
    )(weights, rows, resid, gain)


def head_kernel(place_ref, targets_ref, r0, r1, r2, r3, *refs):
    *tables, out_ref, total = refs
    step = pl.program_id(0)

    @pl.when(step == 0)
    def _():
        total[...] = jnp.zeros_like(total)

    rows = jnp.concatenate([r0[...], r1[...], r2[...], r3[...]])
    share = tables[0].shape[0]
    at = 0
    for table in tables:
        total[at : at + table.shape[0]] += lax.dot_general(
            table[...], rows, (((1,), (1,)), ((), ())), preferred_element_type=f32
        )
        at += table.shape[0]

    @pl.when(step == pl.num_programs(0) - 1)
    def _():
        z, x, c = place_ref[0], place_ref[1], place_ref[2]
        count = rows.shape[0]
        row = iota((count, 1), 0)
        outer, inner, token = rel_step(row // 32), rel_step(row // 8 % 4), row % 8
        z_half = (z // 2 + 4 + inner) % 4
        x_seen = (x + 4 + outer) % 4
        place = (z_half * NX + x_seen) * 8 + token
        position = ((2 * z_half + z % 2) * NX + x_seen) * (NC * 8) + c * 8 + token
        targets = targets_ref[...]
        wanted = jnp.sum(
            jnp.where(position == iota((count, targets.shape[1]), 1), targets, 0),
            axis=1,
            keepdims=True,
        )
        same = iota((count, count), 0) == iota((count, count), 1)
        here = place == iota((count, count), 1)
        wanted = jnp.sum(jnp.where(same, wanted, 0), axis=0, keepdims=True)
        logits = total[...]
        half = share // 2
        entry = iota((4 * share, 1), 0)
        part = entry // half
        shared, upper = part >= 4, part >= 6
        z_of = jnp.where(shared, (z + NZ + jnp.where(upper, 1, -1)) % NZ, z)
        other = jnp.where(shared, part % 2, jnp.where(part >= 2, 1, 0))
        c_of = c + other * (1 - 2 * c)
        offset = jnp.where(
            shared, entry % half + jnp.where(upper, half, 0), entry % share
        )
        entry_id = ((z_of * NX + x) * NC + c_of) * share + offset
        top = jnp.max(logits, axis=0, keepdims=True)
        spread = jnp.sum(jnp.exp(logits - top), axis=0, keepdims=True)
        hit = jnp.sum(jnp.where(wanted == entry_id, logits, 0.0), axis=0, keepdims=True)
        figures = []
        for value in (top + jnp.log(spread), hit):
            column = jnp.sum(jnp.where(same, value, 0.0), axis=1, keepdims=True)
            figures.append(jnp.sum(jnp.where(here, column, 0.0), axis=0, keepdims=True))
        figures = jnp.concatenate(figures)
        for peer in range(out_ref.shape[0]):
            out_ref[peer] = figures


def head(place, targets, rows, tables):
    depth = 1536
    width = rows[0].shape[1]
    share = tables[0].shape[0]
    count = sum(r.shape[0] for r in rows)
    whole = pl.BlockSpec(memory_space=pltpu.SMEM)
    return pl.pallas_call(
        head_kernel,
        grid=(width // depth,),
        in_specs=[whole, pl.BlockSpec(targets.shape, lambda k: (0, 0))]
        + [pl.BlockSpec((rows[0].shape[0], depth), lambda k: (0, k))] * 4
        + [pl.BlockSpec((t.shape[0], depth), lambda k: (0, k)) for t in tables],
        out_specs=pl.BlockSpec((NZ * NX * NC, 2, count), lambda k: (0, 0, 0)),
        out_shape=shape((NZ * NX * NC, 2, count), f32),
        scratch_shapes=[pltpu.VMEM((4 * share, count), f32)],
        compiler_params=params(),
        cost_estimate=cost(8 * count * share * width, 8 * share * width),
    )(place, targets, *rows, *tables)


def hold_kernel(*refs, count):
    sources, kept, sems = refs[:count], refs[count : 2 * count], refs[2 * count]
    copies = [
        pltpu.make_async_copy(source, keep, sems.at[j])
        for j, (source, keep) in enumerate(zip(sources, kept))
    ]
    for copy in copies:
        copy.start()
    for copy in copies:
        copy.wait()


def hold(arrays):
    count = len(arrays)
    return pl.pallas_call(
        functools.partial(hold_kernel, count=count),
        in_specs=[pl.BlockSpec(memory_space=pl.ANY)] * count,
        out_specs=[pl.BlockSpec(memory_space=pltpu.VMEM)] * count,
        out_shape=[pltpu.VMEM(a.shape, a.dtype) for a in arrays],
        scratch_shapes=[pltpu.SemaphoreType.DMA((count,))],
        compiler_params=params(),
        cost_estimate=cost(0, sum(2 * a.size for a in arrays)),
    )(*arrays)


def finish_kernel(place_ref, stats_ref, lengths_ref, questions_ref, logprob_ref, prob_ref):
    z, x, c = place_ref[0], place_ref[1], place_ref[2]
    count = lengths_ref.shape[1]
    local = stats_ref.shape[2]
    lengths = lengths_ref[...].astype(f32)
    questions = questions_ref[...].astype(f32)
    square = (count, count)
    same_place = iota(square, 0) == iota(square, 1)
    ends = jnp.sum(
        jnp.where(iota(square, 1) <= iota(square, 0), lengths, 0.0), axis=1, keepdims=True
    )

    def as_column(line):
        return jnp.sum(jnp.where(same_place, line, 0.0), axis=1, keepdims=True)

    def as_line(column):
        return jnp.sum(jnp.where(same_place, column, 0.0), axis=0, keepdims=True)

    length_column = as_column(lengths)
    starts = ends - length_column
    lane = iota((1, local), 1)
    choice_total = jnp.zeros((count, 1), f32)
    own = jnp.zeros((1, local), f32)
    for parity in range(2):
        for core in range(NC):
            senders = [
                (zz * NX + xx) * NC + core for zz in range(parity, NZ, 2) for xx in range(NX)
            ]
            figures = [stats_ref[j] for j in senders]
            best = functools.reduce(jnp.maximum, [f[0:1] for f in figures])
            summed = sum(jnp.exp(f[0:1] - best) for f in figures)
            logprob = sum(f[1:2] for f in figures) - (best + jnp.log(summed))
            position = (
                (2 * (lane // 32) + parity) * (NX * NC * 8)
                + lane // 8 % 4 * (NC * 8)
                + core * 8
                + lane % 8
            ).astype(f32)
            member = (position >= starts) & (position < ends)
            choice_total += jnp.sum(jnp.where(member, logprob, 0.0), axis=1, keepdims=True)
            mine = (z % 2 == parity) & (c == core)
            own += jnp.where(mine, logprob, 0.0)
    tokens = logprob_ref.shape[1]
    first = (z // 2 * NX + x) * tokens
    column = jnp.sum(
        jnp.where(iota((tokens, local), 1) == first + iota((tokens, local), 0), own, 0.0),
        axis=1,
        keepdims=True,
    )
    eye = iota((tokens, tokens), 0) == iota((tokens, tokens), 1)
    logprob_ref[...] = jnp.sum(jnp.where(eye, column, 0.0), axis=0, keepdims=True)

    average = choice_total / length_column
    same_question = as_column(questions) == questions
    top = jnp.max(
        jnp.where(same_question, as_line(average), -jnp.inf), axis=1, keepdims=True
    )
    raised = jnp.exp(average - top)
    denominator = jnp.sum(
        jnp.where(same_question, as_line(raised), 0.0), axis=1, keepdims=True
    )
    prob_ref[...] = as_line(raised / denominator)


def finish(place, stats, lengths, questions, tokens):
    smem, vmem = (pl.BlockSpec(memory_space=space) for space in (pltpu.SMEM, pltpu.VMEM))
    return pl.pallas_call(
        finish_kernel,
        in_specs=[smem, vmem, vmem, vmem],
        out_shape=(shape((1, tokens), f32), shape(lengths.shape, f32)),
        compiler_params=params(),
    )(place, stats, lengths, questions)


def on_device(
    resid,
    moe_gain,
    final_gain,
    router,
    w_gate,
    w_up,
    w_down,
    lm_head,
    expert_ids,
    target_ids,
    choice_len,
    choice_question,
):
    own_gate, own_up, own_down = w_gate[0], w_up[0], w_down[0]
    z_index = lax.axis_index("expert")
    v_index = lax.axis_index("vocab")
    place = jnp.stack([z_index, v_index // NC, v_index % NC]).astype(i32)

    other_gate = swap_cores(own_gate)
    other_up = swap_cores(own_up)
    other_down = swap_cores(own_down)
    other_head = swap_cores(lm_head)

    buckets = bucket_rows(expert_ids[0], resid[0], moe_gain.reshape(1, -1))
    arrived = lax.all_to_all(buckets, "expert", split_axis=0, concat_axis=0, tiled=True)
    arrived, other_gate, other_up, other_down, other_head, own_head, router = tied(
        arrived, other_gate, other_up, other_down, other_head, lm_head, router
    )
    combine_weights = slot_gates(expert_ids[0], resid[0], moe_gain.reshape(1, -1), router.T)
    head_half = own_head.shape[0] // 2
    low_head = z_shift(own_head[:head_half], 1)
    high_head = z_shift(own_head[head_half:], -1)

    def first(block, shift):
        return plane_shift(block, False, shift)

    def second(block, shift):
        return plane_shift(block, True, shift)

    line = stack(gather_four(arrived, first))
    rows = line.shape[0]
    half = rows // 2
    from_before = second(line, 1)
    from_after = second(line, -1)
    weights = hold(tied(line, own_gate, own_up, other_gate, other_up)[1:])
    from_before, from_after, combine_weights, *weights = tied(
        from_before, from_after, combine_weights, *weights
    )
    far_before = second(from_before[:half], 1)
    far_after = second(from_after[half:], -1)
    downs = (own_down, other_down)
    near_hidden = expand([line, from_before, from_after], weights)
    near_hidden, far_before, far_after = tied(near_hidden, far_before, far_after)
    far_hidden = expand([far_before, far_after], weights)

    to_before, to_after = down_call(far_kernel, far_hidden, downs, (), (half, half))
    got_before = second(to_before, -1)
    got_after = second(to_after, 1)
    got_before, low_head, high_head = tied(got_before, low_head, high_head)
    before_part, after_part = down_call(
        near_kernel, near_hidden, downs, (got_before, got_after), (rows, rows)
    )
    (own_part,) = down_call(own_kernel, near_hidden, downs, (), (rows,))
    own_part, low_head, high_head = tied(own_part, low_head, high_head)
    low_other = swap_cores(low_head)
    high_other = swap_cores(high_head)
    pieces = line_sum([own_part, second(before_part, -1), second(after_part, 1)])
    back = (first(pieces[1], -1), first(pieces[2], 1), first(pieces[3], 2))
    outgoing = expert_sum([pieces[0], *back])

    returned = lax.all_to_all(outgoing, "expert", split_axis=0, concat_axis=0, tiled=True)
    normed_out = combine(combine_weights, returned, resid[0], final_gain.reshape(1, -1))

    head_line = stack(gather_four(normed_out, lambda b, s: head_shift(b, False, s)))
    head_rows = gather_four(head_line, lambda b, s: head_shift(b, True, s))
    stats = head(place, target_ids, head_rows, hold([lm_head, other_head, low_head, low_other, high_head, high_other]))
    gathered = lax.all_to_all(stats, ("expert", "vocab"), 0, 0, tiled=True)
    return finish(place, gathered, choice_len, choice_question, resid.shape[1])


def solution(mesh):
    return jax.shard_map(
        on_device,
        mesh=mesh,
        in_specs=(
            P("batch", ("expert", "vocab"), None),
            P(),
            P(),
            P(),
            P("expert", None, ("vocab", "batch")),
            P("expert", None, ("vocab", "batch")),
            P("expert", ("vocab", "batch"), None),
            P(("expert", "vocab"), None),
            P("batch", ("expert", "vocab"), None),
            P("batch", None),
            P("batch", None),
            P("batch", None),
        ),
        out_specs=(P("batch", ("expert", "vocab")), P("batch", None)),
        check_vma=False,
    )
```

```python
import functools

import jax
import jax.numpy as jnp
from jax import lax
from jax.experimental import pallas as pl
from jax.experimental.pallas import tpu as pltpu
from jax.sharding import PartitionSpec as P

epsilon = 1e-05
bf16 = jnp.bfloat16
f32 = jnp.float32
i32 = jnp.int32

NZ, NX, NC, NY = 8, 4, 2, 4
SLOTS = 3
VMEM_LIMIT = 16 * 2**20


def two_axis_perm(sizes, coords, axis_of, shift):
    pairs = []
    for index in range(sizes):
        place = coords(index)
        axis, step, size = axis_of(place)
        to = dict(place)
        to[axis] = (place[axis] + shift * step) % size
        pairs.append((index, coords(to)))
    return pairs


def plane_coords(index):
    if isinstance(index, dict):
        return (index["x"] * NC + index["c"]) * NY + index["y"]
    return {"x": index // (NC * NY), "c": index // NY % NC, "y": index % NY}


def head_coords(index):
    if isinstance(index, dict):
        return (index["z"] * NX + index["x"]) * NC + index["c"]
    return {"z": index // (NX * NC), "x": index // NC % NX, "c": index % NC}


def plane_shift(array, second, shift):
    def axis_of(place):
        return ("x", 1, NX) if (place["c"] == 0) != second else ("y", 1, NY)

    perm = two_axis_perm(NX * NC * NY, plane_coords, axis_of, shift)
    return lax.ppermute(array, ("vocab", "batch"), perm)


def head_shift(array, second, shift):
    def axis_of(place):
        return ("x", 1, NX) if second else ("z", 2, NZ)

    perm = two_axis_perm(NZ * NX * NC, head_coords, axis_of, shift)
    return lax.ppermute(array, ("expert", "vocab"), perm)


def swap_cores(array):
    return lax.ppermute(array, "vocab", [(v, v ^ 1) for v in range(NX * NC)])


def z_shift(array, shift):
    return lax.ppermute(array, "expert", [(z, (z + shift) % NZ) for z in range(NZ)])


def gather_four(block, shift_by):
    return [block, shift_by(block, 1), shift_by(block, -1), shift_by(block, 2)]


def rel_step(rel):
    return jnp.where(rel == 1, -1, jnp.where(rel == 2, 1, jnp.where(rel == 3, 2, 0)))


def tied(*arrays):
    return lax.optimization_barrier(arrays)


def shape(dims, dtype):
    return jax.ShapeDtypeStruct(dims, dtype)


def iota(dims, axis):
    return lax.broadcasted_iota(i32, dims, axis)


def params():
    return pltpu.CompilerParams(vmem_limit_bytes=VMEM_LIMIT)


def cost(flops, moved):
    return pl.CostEstimate(flops=flops, bytes_accessed=moved, transcendentals=0)


def normed_rows(resid_ref, gain_ref):
    values = resid_ref[...].astype(f32)
    mean_square = jnp.mean(values * values, axis=-1, keepdims=True)
    return (values * lax.rsqrt(mean_square + epsilon) * gain_ref[...]).astype(bf16)


def slots(ids, width):
    tokens = ids.shape[0]
    earlier = (iota((tokens, tokens), 0) > iota((tokens, tokens), 1)).astype(f32)
    column = iota((tokens, NZ * width), 1)
    owner, slot = column // width, column % width
    match_a, match_b = ids[:, 0:1] == owner, ids[:, 1:2] == owner
    named = (match_a | match_b).astype(f32)
    rank = jnp.dot(earlier, named, preferred_element_type=f32)
    chosen = named * (rank == slot.astype(f32)).astype(f32)
    return chosen, match_a, match_b


def bucket_kernel(ids_ref, resid_ref, gain_ref, buckets_ref):
    chosen, _, _ = slots(ids_ref[...], 8)
    rows = lax.dot_general(
        chosen.astype(bf16),
        normed_rows(resid_ref, gain_ref),
        (((0,), (0,)), ((), ())),
        preferred_element_type=f32,
    )
    for e in range(NZ):
        buckets_ref[e] = rows[8 * e : 8 * e + SLOTS].astype(bf16)


def bucket_rows(ids, resid, gain):
    tokens, width = resid.shape
    return pl.pallas_call(
        bucket_kernel,
        out_shape=shape((NZ, SLOTS, width), bf16),
        compiler_params=params(),
        cost_estimate=cost(2 * 64 * tokens * width, 8 * width),
    )(ids, resid, gain)


def gate_kernel(ids_ref, resid_ref, gain_ref, router_ref, weights_ref):
    logits = lax.dot_general(
        normed_rows(resid_ref, gain_ref),
        router_ref[...],
        (((1,), (1,)), ((), ())),
        preferred_element_type=f32,
    )
    ids = ids_ref[...]
    chosen, match_a, match_b = slots(ids, SLOTS)
    entry = iota(logits.shape, 1)
    pick_a = jnp.sum(jnp.where(ids[:, 0:1] == entry, logits, 0.0), axis=1, keepdims=True)
    pick_b = jnp.sum(jnp.where(ids[:, 1:2] == entry, logits, 0.0), axis=1, keepdims=True)
    gate_a = 1.0 / (1.0 + jnp.exp(pick_b - pick_a))
    gate_b = 1.0 / (jnp.exp(pick_a - pick_b) + 1.0)
    weights_ref[...] = chosen * (
        jnp.where(match_a, gate_a, 0.0) + jnp.where(match_b, gate_b, 0.0)
    )


def slot_gates(ids, resid, gain, router):
    tokens, width = resid.shape
    return pl.pallas_call(
        gate_kernel,
        out_shape=shape((tokens, NZ * SLOTS), f32),
        compiler_params=params(),
        cost_estimate=cost(16 * tokens * width, 8 * width),
    )(ids, resid, gain, router)


def stack_kernel(*refs, chunk):
    *parts, out_ref = refs
    width = out_ref.shape[1]

    @pl.loop(0, width // chunk)
    def _(step):
        columns = pl.ds(pl.multiple_of(step * chunk, chunk), chunk)
        pieces = []
        for part in parts:
            if len(part.shape) == 3:
                pieces += [part[e, :, columns].astype(f32) for e in range(part.shape[0])]
            else:
                pieces.append(part[:, columns].astype(f32))
        out_ref[:, columns] = jnp.concatenate(pieces).astype(bf16)


def stack(parts):
    width = parts[0].shape[-1]
    rows = sum(part.size // width for part in parts)
    return pl.pallas_call(
        functools.partial(stack_kernel, chunk=512),
        out_shape=shape((rows, width), bf16),
        compiler_params=params(),
        cost_estimate=cost(0, 4 * rows * width),
    )(*parts)


def expand_kernel(*refs, count):
    rows = [ref[...] for ref in refs[:count]]
    gate_a, up_a, gate_b, up_b, out_ref, total = refs[count:]
    step = pl.program_id(0)

    @pl.when(step == 0)
    def _():
        total[...] = jnp.zeros_like(total)

    block = rows[0] if count == 1 else jnp.concatenate(rows)
    for j, weight in enumerate((gate_a, up_a, gate_b, up_b)):
        total[j] += jnp.dot(block, weight[...], preferred_element_type=f32)

    @pl.when(step == pl.num_programs(0) - 1)
    def _():
        share = total.shape[2]
        for j in range(2):
            gate = total[2 * j]
            out_ref[:, j * share : (j + 1) * share] = (
                gate / (1.0 + jnp.exp(-gate)) * total[2 * j + 1]
            ).astype(bf16)


def expand(rows, weights):
    depth = 1536
    count = len(rows)
    each, width = rows[0].shape
    share = weights[0].shape[1]
    return pl.pallas_call(
        functools.partial(expand_kernel, count=count),
        grid=(width // depth,),
        in_specs=[pl.BlockSpec((each, depth), lambda k: (0, k))] * count
        + [pl.BlockSpec((depth, share), lambda k: (k, 0))] * 4,
        out_specs=pl.BlockSpec((count * each, 2 * share), lambda k: (0, 0)),
        out_shape=shape((count * each, 2 * share), bf16),
        scratch_shapes=[pltpu.VMEM((4, count * each, share), f32)],
        compiler_params=params(),
        cost_estimate=cost(8 * count * each * width * share, 8 * width * share),
    )(*rows, *weights)


def contract(hidden, down_a, down_b):
    share = down_a.shape[0]
    return jnp.dot(hidden[:, :share], down_a, preferred_element_type=f32) + jnp.dot(
        hidden[:, share:], down_b, preferred_element_type=f32
    )


def rows_from(near_ref, far_ref, places):
    near, far = near_ref[...].astype(f32), far_ref[...].astype(f32)
    block = far.shape[0]
    each = block // 4
    pieces = []
    for place in places:
        at = place * each
        pieces += [near[q * block + at : q * block + at + each] for q in range(3)]
        pieces.append(far[at : at + each])
    return jnp.concatenate(pieces).astype(bf16)


def far_kernel(near_ref, far_ref, down_a, down_b, before_ref, after_ref):
    part = contract(rows_from(near_ref, far_ref, (3,)), down_a[...], down_b[...]).astype(bf16)
    half = before_ref.shape[0]
    before_ref[...] = part[:half]
    after_ref[...] = part[half:]


def near_kernel(
    near_ref, far_ref, down_a, down_b, got_before, got_after, before_ref, after_ref
):
    rows = before_ref.shape[0]
    half = rows // 2
    part = contract(rows_from(near_ref, far_ref, (1, 2)), down_a[...], down_b[...])
    before_ref[:half] = (part[:half] + got_before[...].astype(f32)).astype(bf16)
    before_ref[half:] = part[half:rows].astype(bf16)
    after_ref[:half] = part[rows : rows + half].astype(bf16)
    after_ref[half:] = (part[rows + half :] + got_after[...].astype(f32)).astype(bf16)


def own_kernel(near_ref, far_ref, down_a, down_b, own_ref):
    own_ref[...] = contract(
        rows_from(near_ref, far_ref, (0,)), down_a[...], down_b[...]
    ).astype(bf16)


def down_call(kernel, hidden, downs, got, out_rows):
    tile = 1536
    share, width = downs[0].shape
    total = sum(out_rows)
    return pl.pallas_call(
        kernel,
        grid=(width // tile,),
        in_specs=[pl.BlockSpec(h.shape, lambda n: (0, 0)) for h in hidden]
        + [pl.BlockSpec((share, tile), lambda n: (0, n))] * 2
        + [pl.BlockSpec((g.shape[0], tile), lambda n: (0, n)) for g in got],
        out_specs=[pl.BlockSpec((rows, tile), lambda n: (0, n)) for rows in out_rows],
        out_shape=[shape((rows, width), bf16) for rows in out_rows],
        compiler_params=params(),
        cost_estimate=cost(4 * total * share * width, 4 * share * width),
    )(*hidden, *downs, *got)


def line_sum_kernel(own_ref, before_ref, after_ref, *outs):
    total = own_ref[...].astype(f32) + before_ref[...].astype(f32) + after_ref[...].astype(f32)
    rows = outs[0].shape[0]
    for j, out in enumerate(outs):
        out[...] = total[j * rows : (j + 1) * rows].astype(bf16)


def line_sum(parts):
    tile = 1536
    rows, width = parts[0].shape
    return pl.pallas_call(
        line_sum_kernel,
        grid=(width // tile,),
        in_specs=[pl.BlockSpec((rows, tile), lambda n: (0, n))] * 3,
        out_specs=[pl.BlockSpec((rows // 4, tile), lambda n: (0, n))] * 4,
        out_shape=[shape((rows // 4, width), bf16)] * 4,
        compiler_params=params(),
        cost_estimate=cost(3 * rows * width, 8 * rows * width),
    )(*parts)


def expert_sum_kernel(a, b, c, d, out_ref, *, chunk):
    @pl.loop(0, out_ref.shape[2] // chunk)
    def _(step):
        columns = pl.ds(pl.multiple_of(step * chunk, chunk), chunk)
        total = (
            a[:, columns].astype(f32)
            + b[:, columns].astype(f32)
            + c[:, columns].astype(f32)
            + d[:, columns].astype(f32)
        )
        for e in range(NZ):
            out_ref[e, :, columns] = total[SLOTS * e : SLOTS * e + SLOTS].astype(bf16)


def expert_sum(parts):
    width = parts[0].shape[1]
    return pl.pallas_call(
        functools.partial(expert_sum_kernel, chunk=512),
        out_shape=shape((NZ, SLOTS, width), bf16),
        compiler_params=params(),
        cost_estimate=cost(96 * width, 240 * width),
    )(*parts)


def combine_kernel(weights_ref, rows_ref, resid_ref, gain_ref, out_ref):
    mixed = resid_ref[...].astype(f32)
    weights = weights_ref[...]
    for e in range(NZ):
        rows = rows_ref[e].astype(f32)
        for s in range(SLOTS):
            slot = SLOTS * e + s
            mixed += weights[:, slot : slot + 1] * rows[s : s + 1]
    mean_square = jnp.mean(mixed * mixed, axis=-1, keepdims=True)
    out_ref[...] = (mixed * lax.rsqrt(mean_square + epsilon) * gain_ref[...]).astype(bf16)


def combine(weights, rows, resid, gain):
    return pl.pallas_call(
        combine_kernel,
        out_shape=shape(resid.shape, bf16),
        compiler_params=params(),
        cost_estimate=cost(48 * resid.size, 8 * resid.size),
    )(weights, rows, resid, gain)


def head_kernel(place_ref, targets_ref, r0, r1, r2, r3, *refs):
    *tables, out_ref, total = refs
    step = pl.program_id(0)

    @pl.when(step == 0)
    def _():
        total[...] = jnp.zeros_like(total)

    rows = jnp.concatenate([r0[...], r1[...], r2[...], r3[...]])
    share = tables[0].shape[0]
    at = 0
    for table in tables:
        total[at : at + table.shape[0]] += lax.dot_general(
            table[...], rows, (((1,), (1,)), ((), ())), preferred_element_type=f32
        )
        at += table.shape[0]

    @pl.when(step == pl.num_programs(0) - 1)
    def _():
        z, x, c = place_ref[0], place_ref[1], place_ref[2]
        count = rows.shape[0]
        row = iota((count, 1), 0)
        outer, inner, token = rel_step(row // 32), rel_step(row // 8 % 4), row % 8
        z_half = (z // 2 + 4 + inner) % 4
        x_seen = (x + 4 + outer) % 4
        place = (z_half * NX + x_seen) * 8 + token
        position = ((2 * z_half + z % 2) * NX + x_seen) * (NC * 8) + c * 8 + token
        targets = targets_ref[...]
        wanted = jnp.sum(
            jnp.where(position == iota((count, targets.shape[1]), 1), targets, 0),
            axis=1,
            keepdims=True,
        )
        same = iota((count, count), 0) == iota((count, count), 1)
        here = place == iota((count, count), 1)
        wanted = jnp.sum(jnp.where(same, wanted, 0), axis=0, keepdims=True)
        logits = total[...]
        half = share // 2
        entry = iota((4 * share, 1), 0)
        part = entry // half
        shared, upper = part >= 4, part >= 6
        z_of = jnp.where(shared, (z + NZ + jnp.where(upper, 1, -1)) % NZ, z)
        other = jnp.where(shared, part % 2, jnp.where(part >= 2, 1, 0))
        c_of = c + other * (1 - 2 * c)
        offset = jnp.where(
            shared, entry % half + jnp.where(upper, half, 0), entry % share
        )
        entry_id = ((z_of * NX + x) * NC + c_of) * share + offset
        top = jnp.max(logits, axis=0, keepdims=True)
        spread = jnp.sum(jnp.exp(logits - top), axis=0, keepdims=True)
        hit = jnp.sum(jnp.where(wanted == entry_id, logits, 0.0), axis=0, keepdims=True)
        figures = []
        for value in (top + jnp.log(spread), hit):
            column = jnp.sum(jnp.where(same, value, 0.0), axis=1, keepdims=True)
            figures.append(jnp.sum(jnp.where(here, column, 0.0), axis=0, keepdims=True))
        figures = jnp.concatenate(figures)
        for peer in range(out_ref.shape[0]):
            out_ref[peer] = figures


def head(place, targets, rows, tables):
    depth = 1536
    width = rows[0].shape[1]
    share = tables[0].shape[0]
    count = sum(r.shape[0] for r in rows)
    whole = pl.BlockSpec(memory_space=pltpu.SMEM)
    return pl.pallas_call(
        head_kernel,
        grid=(width // depth,),
        in_specs=[whole, pl.BlockSpec(targets.shape, lambda k: (0, 0))]
        + [pl.BlockSpec((rows[0].shape[0], depth), lambda k: (0, k))] * 4
        + [pl.BlockSpec((t.shape[0], depth), lambda k: (0, k)) for t in tables],
        out_specs=pl.BlockSpec((NZ * NX * NC, 2, count), lambda k: (0, 0, 0)),
        out_shape=shape((NZ * NX * NC, 2, count), f32),
        scratch_shapes=[pltpu.VMEM((4 * share, count), f32)],
        compiler_params=params(),
        cost_estimate=cost(8 * count * share * width, 8 * share * width),
    )(place, targets, *rows, *tables)


def hold_kernel(*refs, count):
    sources, kept, sems = refs[:count], refs[count : 2 * count], refs[2 * count]
    copies = [
        pltpu.make_async_copy(source, keep, sems.at[j])
        for j, (source, keep) in enumerate(zip(sources, kept))
    ]
    for copy in copies:
        copy.start()
    for copy in copies:
        copy.wait()


def hold(arrays):
    count = len(arrays)
    return pl.pallas_call(
        functools.partial(hold_kernel, count=count),
        in_specs=[pl.BlockSpec(memory_space=pl.ANY)] * count,
        out_specs=[pl.BlockSpec(memory_space=pltpu.VMEM)] * count,
        out_shape=[pltpu.VMEM(a.shape, a.dtype) for a in arrays],
        scratch_shapes=[pltpu.SemaphoreType.DMA((count,))],
        compiler_params=params(),
        cost_estimate=cost(0, sum(2 * a.size for a in arrays)),
    )(*arrays)


def finish_kernel(place_ref, stats_ref, lengths_ref, questions_ref, logprob_ref, prob_ref):
    z, x, c = place_ref[0], place_ref[1], place_ref[2]
    count = lengths_ref.shape[1]
    local = stats_ref.shape[2]
    lengths = lengths_ref[...].astype(f32)
    questions = questions_ref[...].astype(f32)
    square = (count, count)
    same_place = iota(square, 0) == iota(square, 1)
    ends = jnp.sum(
        jnp.where(iota(square, 1) <= iota(square, 0), lengths, 0.0), axis=1, keepdims=True
    )

    def as_column(line):
        return jnp.sum(jnp.where(same_place, line, 0.0), axis=1, keepdims=True)

    def as_line(column):
        return jnp.sum(jnp.where(same_place, column, 0.0), axis=0, keepdims=True)

    length_column = as_column(lengths)
    starts = ends - length_column
    lane = iota((1, local), 1)
    choice_total = jnp.zeros((count, 1), f32)
    own = jnp.zeros((1, local), f32)
    for parity in range(2):
        for core in range(NC):
            senders = [
                (zz * NX + xx) * NC + core for zz in range(parity, NZ, 2) for xx in range(NX)
            ]
            figures = [stats_ref[j] for j in senders]
            best = functools.reduce(jnp.maximum, [f[0:1] for f in figures])
            summed = sum(jnp.exp(f[0:1] - best) for f in figures)
            logprob = sum(f[1:2] for f in figures) - (best + jnp.log(summed))
            position = (
                (2 * (lane // 32) + parity) * (NX * NC * 8)
                + lane // 8 % 4 * (NC * 8)
                + core * 8
                + lane % 8
            ).astype(f32)
            member = (position >= starts) & (position < ends)
            choice_total += jnp.sum(jnp.where(member, logprob, 0.0), axis=1, keepdims=True)
            mine = (z % 2 == parity) & (c == core)
            own += jnp.where(mine, logprob, 0.0)
    tokens = logprob_ref.shape[1]
    first = (z // 2 * NX + x) * tokens
    column = jnp.sum(
        jnp.where(iota((tokens, local), 1) == first + iota((tokens, local), 0), own, 0.0),
        axis=1,
        keepdims=True,
    )
    eye = iota((tokens, tokens), 0) == iota((tokens, tokens), 1)
    logprob_ref[...] = jnp.sum(jnp.where(eye, column, 0.0), axis=0, keepdims=True)

    average = choice_total / length_column
    same_question = as_column(questions) == questions
    top = jnp.max(
        jnp.where(same_question, as_line(average), -jnp.inf), axis=1, keepdims=True
    )
    raised = jnp.exp(average - top)
    denominator = jnp.sum(
        jnp.where(same_question, as_line(raised), 0.0), axis=1, keepdims=True
    )
    prob_ref[...] = as_line(raised / denominator)


def finish(place, stats, lengths, questions, tokens):
    smem, vmem = (pl.BlockSpec(memory_space=space) for space in (pltpu.SMEM, pltpu.VMEM))
    return pl.pallas_call(
        finish_kernel,
        in_specs=[smem, vmem, vmem, vmem],
        out_shape=(shape((1, tokens), f32), shape(lengths.shape, f32)),
        compiler_params=params(),
    )(place, stats, lengths, questions)


def on_device(
    resid,
    moe_gain,
    final_gain,
    router,
    w_gate,
    w_up,
    w_down,
    lm_head,
    expert_ids,
    target_ids,
    choice_len,
    choice_question,
):
    own_gate, own_up, own_down = w_gate[0], w_up[0], w_down[0]
    z_index = lax.axis_index("expert")
    v_index = lax.axis_index("vocab")
    place = jnp.stack([z_index, v_index // NC, v_index % NC]).astype(i32)

    other_gate = swap_cores(own_gate)
    other_up = swap_cores(own_up)
    other_down = swap_cores(own_down)
    other_head = swap_cores(lm_head)

    buckets = bucket_rows(expert_ids[0], resid[0], moe_gain.reshape(1, -1))
    arrived = lax.all_to_all(buckets, "expert", split_axis=0, concat_axis=0, tiled=True)
    arrived, other_gate, other_up, other_down, other_head, own_head, router = tied(
        arrived, other_gate, other_up, other_down, other_head, lm_head, router
    )
    combine_weights = slot_gates(expert_ids[0], resid[0], moe_gain.reshape(1, -1), router.T)
    head_half = own_head.shape[0] // 2
    low_head = z_shift(own_head[:head_half], 1)
    high_head = z_shift(own_head[head_half:], -1)

    def first(block, shift):
        return plane_shift(block, False, shift)

    def second(block, shift):
        return plane_shift(block, True, shift)

    line = stack(gather_four(arrived, first))
    rows = line.shape[0]
    half = rows // 2
    from_before = second(line, 1)
    from_after = second(line, -1)
    weights = hold(tied(line, own_gate, own_up, other_gate, other_up)[1:])
    from_before, from_after, combine_weights, *weights = tied(
        from_before, from_after, combine_weights, *weights
    )
    far_before = second(from_before[:half], 1)
    far_after = second(from_after[half:], -1)
    downs = (own_down, other_down)
    near_hidden = expand([line, from_before, from_after], weights)
    near_hidden, far_before, far_after = tied(near_hidden, far_before, far_after)
    far_hidden = expand([far_before, far_after], weights)

    hidden = (near_hidden, far_hidden)
    to_before, to_after = down_call(far_kernel, hidden, downs, (), (half, half))
    got_before = first(to_before, -1)
    got_after = first(to_after, 1)
    got_before, low_head, high_head = tied(got_before, low_head, high_head)
    before_part, after_part = down_call(
        near_kernel, hidden, downs, (got_before, got_after), (rows, rows)
    )
    (own_part,) = down_call(own_kernel, hidden, downs, (), (rows,))
    own_part, low_head, high_head = tied(own_part, low_head, high_head)
    low_other = swap_cores(low_head)
    high_other = swap_cores(high_head)
    pieces = line_sum([own_part, first(before_part, -1), first(after_part, 1)])
    back = (second(pieces[1], -1), second(pieces[2], 1), second(pieces[3], 2))
    outgoing = expert_sum([pieces[0], *back])

    returned = lax.all_to_all(outgoing, "expert", split_axis=0, concat_axis=0, tiled=True)
    normed_out = combine(combine_weights, returned, resid[0], final_gain.reshape(1, -1))

    head_line = stack(gather_four(normed_out, lambda b, s: head_shift(b, False, s)))
    head_rows = gather_four(head_line, lambda b, s: head_shift(b, True, s))
    stats = head(place, target_ids, head_rows, hold([lm_head, other_head, low_head, low_other, high_head, high_other]))
    gathered = lax.all_to_all(stats, ("expert", "vocab"), 0, 0, tiled=True)
    return finish(place, gathered, choice_len, choice_question, resid.shape[1])


def solution(mesh):
    return jax.shard_map(
        on_device,
        mesh=mesh,
        in_specs=(
            P("batch", ("expert", "vocab"), None),
            P(),
            P(),
            P(),
            P("expert", None, ("vocab", "batch")),
            P("expert", None, ("vocab", "batch")),
            P("expert", ("vocab", "batch"), None),
            P(("expert", "vocab"), None),
            P("batch", ("expert", "vocab"), None),
            P("batch", None),
            P("batch", None),
            P("batch", None),
        ),
        out_specs=(P("batch", ("expert", "vocab")), P("batch", None)),
        check_vma=False,
    )
```

```python
import functools

import jax
import jax.numpy as jnp
from jax import lax
from jax.experimental import pallas as pl
from jax.experimental.pallas import tpu as pltpu
from jax.sharding import PartitionSpec as P

epsilon = 1e-05
bf16 = jnp.bfloat16
f32 = jnp.float32
i32 = jnp.int32

NZ, NX, NC, NY = 8, 4, 2, 4
SLOTS = 3
VMEM_LIMIT = 16 * 2**20


def two_axis_perm(sizes, coords, axis_of, shift):
    pairs = []
    for index in range(sizes):
        place = coords(index)
        axis, step, size = axis_of(place)
        to = dict(place)
        to[axis] = (place[axis] + shift * step) % size
        pairs.append((index, coords(to)))
    return pairs


def plane_coords(index):
    if isinstance(index, dict):
        return (index["x"] * NC + index["c"]) * NY + index["y"]
    return {"x": index // (NC * NY), "c": index // NY % NC, "y": index % NY}


def head_coords(index):
    if isinstance(index, dict):
        return (index["z"] * NX + index["x"]) * NC + index["c"]
    return {"z": index // (NX * NC), "x": index // NC % NX, "c": index % NC}


def plane_shift(array, second, shift):
    def axis_of(place):
        return ("x", 1, NX) if (place["c"] == 0) != second else ("y", 1, NY)

    perm = two_axis_perm(NX * NC * NY, plane_coords, axis_of, shift)
    return lax.ppermute(array, ("vocab", "batch"), perm)


def head_shift(array, second, shift):
    def axis_of(place):
        return ("x", 1, NX) if second else ("z", 2, NZ)

    perm = two_axis_perm(NZ * NX * NC, head_coords, axis_of, shift)
    return lax.ppermute(array, ("expert", "vocab"), perm)


def swap_cores(array):
    return lax.ppermute(array, "vocab", [(v, v ^ 1) for v in range(NX * NC)])


def z_shift(array, shift):
    return lax.ppermute(array, "expert", [(z, (z + shift) % NZ) for z in range(NZ)])


def gather_four(block, shift_by):
    return [block, shift_by(block, 1), shift_by(block, -1), shift_by(block, 2)]


def rel_step(rel):
    return jnp.where(rel == 1, -1, jnp.where(rel == 2, 1, jnp.where(rel == 3, 2, 0)))


def tied(*arrays):
    return lax.optimization_barrier(arrays)


def shape(dims, dtype):
    return jax.ShapeDtypeStruct(dims, dtype)


def iota(dims, axis):
    return lax.broadcasted_iota(i32, dims, axis)


def params():
    return pltpu.CompilerParams(vmem_limit_bytes=VMEM_LIMIT)


def cost(flops, moved):
    return pl.CostEstimate(flops=flops, bytes_accessed=moved, transcendentals=0)


def normed_rows(resid_ref, gain_ref):
    values = resid_ref[...].astype(f32)
    mean_square = jnp.mean(values * values, axis=-1, keepdims=True)
    return (values * lax.rsqrt(mean_square + epsilon) * gain_ref[...]).astype(bf16)


def slots(ids, width):
    tokens = ids.shape[0]
    earlier = (iota((tokens, tokens), 0) > iota((tokens, tokens), 1)).astype(f32)
    column = iota((tokens, NZ * width), 1)
    owner, slot = column // width, column % width
    match_a, match_b = ids[:, 0:1] == owner, ids[:, 1:2] == owner
    named = (match_a | match_b).astype(f32)
    rank = jnp.dot(earlier, named, preferred_element_type=f32)
    chosen = named * (rank == slot.astype(f32)).astype(f32)
    return chosen, match_a, match_b


def bucket_kernel(ids_ref, resid_ref, gain_ref, buckets_ref):
    chosen, _, _ = slots(ids_ref[...], 8)
    rows = lax.dot_general(
        chosen.astype(bf16),
        normed_rows(resid_ref, gain_ref),
        (((0,), (0,)), ((), ())),
        preferred_element_type=f32,
    )
    for e in range(NZ):
        buckets_ref[e] = rows[8 * e : 8 * e + SLOTS].astype(bf16)


def bucket_rows(ids, resid, gain):
    tokens, width = resid.shape
    return pl.pallas_call(
        bucket_kernel,
        out_shape=shape((NZ, SLOTS, width), bf16),
        compiler_params=params(),
        cost_estimate=cost(2 * 64 * tokens * width, 8 * width),
    )(ids, resid, gain)


def gate_kernel(ids_ref, resid_ref, gain_ref, router_ref, weights_ref):
    logits = lax.dot_general(
        normed_rows(resid_ref, gain_ref),
        router_ref[...],
        (((1,), (1,)), ((), ())),
        preferred_element_type=f32,
    )
    ids = ids_ref[...]
    chosen, match_a, match_b = slots(ids, SLOTS)
    entry = iota(logits.shape, 1)
    pick_a = jnp.sum(jnp.where(ids[:, 0:1] == entry, logits, 0.0), axis=1, keepdims=True)
    pick_b = jnp.sum(jnp.where(ids[:, 1:2] == entry, logits, 0.0), axis=1, keepdims=True)
    gate_a = 1.0 / (1.0 + jnp.exp(pick_b - pick_a))
    gate_b = 1.0 / (jnp.exp(pick_a - pick_b) + 1.0)
    weights_ref[...] = chosen * (
        jnp.where(match_a, gate_a, 0.0) + jnp.where(match_b, gate_b, 0.0)
    )


def slot_gates(ids, resid, gain, router):
    tokens, width = resid.shape
    return pl.pallas_call(
        gate_kernel,
        out_shape=shape((tokens, NZ * SLOTS), f32),
        compiler_params=params(),
        cost_estimate=cost(16 * tokens * width, 8 * width),
    )(ids, resid, gain, router)


def stack_kernel(*refs, chunk):
    *parts, out_ref = refs
    width = out_ref.shape[1]

    @pl.loop(0, width // chunk)
    def _(step):
        columns = pl.ds(pl.multiple_of(step * chunk, chunk), chunk)
        pieces = []
        for part in parts:
            if len(part.shape) == 3:
                pieces += [part[e, :, columns].astype(f32) for e in range(part.shape[0])]
            else:
                pieces.append(part[:, columns].astype(f32))
        out_ref[:, columns] = jnp.concatenate(pieces).astype(bf16)


def stack(parts):
    width = parts[0].shape[-1]
    rows = sum(part.size // width for part in parts)
    return pl.pallas_call(
        functools.partial(stack_kernel, chunk=512),
        out_shape=shape((rows, width), bf16),
        compiler_params=params(),
        cost_estimate=cost(0, 4 * rows * width),
    )(*parts)


def expand_kernel(*refs, count, chunk):
    rows = refs[:count]
    gate_a, up_a, gate_b, up_b, out_ref, total = refs[count:]
    total[...] = jnp.zeros_like(total)

    @pl.loop(0, rows[0].shape[1] // chunk)
    def _(step):
        columns = pl.ds(pl.multiple_of(step * chunk, chunk), chunk)
        block = jnp.concatenate([ref[:, columns] for ref in rows])
        for j, weight in enumerate((gate_a, up_a, gate_b, up_b)):
            total[j] += jnp.dot(block, weight[columns, :], preferred_element_type=f32)

    share = total.shape[2]
    for j in range(2):
        gate = total[2 * j]
        out_ref[:, j * share : (j + 1) * share] = (
            gate / (1.0 + jnp.exp(-gate)) * total[2 * j + 1]
        ).astype(bf16)


def expand(rows, weights):
    count = len(rows)
    each, width = rows[0].shape
    share = weights[0].shape[1]
    return pl.pallas_call(
        functools.partial(expand_kernel, count=count, chunk=width if count == 2 else 1536),
        out_shape=shape((count * each, 2 * share), bf16),
        scratch_shapes=[pltpu.VMEM((4, count * each, share), f32)],
        compiler_params=params(),
        cost_estimate=cost(8 * count * each * width * share, 8 * width * share),
    )(*rows, *weights)


def rows_from(near_ref, far_ref, places):
    near, far = near_ref[...].astype(f32), far_ref[...].astype(f32)
    block = far.shape[0]
    each = block // 4
    pieces = []
    for place in places:
        at = place * each
        pieces += [near[q * block + at : q * block + at + each] for q in range(3)]
        pieces.append(far[at : at + each])
    return jnp.concatenate(pieces).astype(bf16)


def down_kernel(near_ref, far_ref, down_a, down_b, *outs, places, chunk):
    rows = rows_from(near_ref, far_ref, places)
    share, width = down_a.shape

    @pl.loop(0, width // chunk)
    def _(step):
        columns = pl.ds(pl.multiple_of(step * chunk, chunk), chunk)
        part = jnp.dot(rows[:, :share], down_a[:, columns], preferred_element_type=f32)
        part += jnp.dot(rows[:, share:], down_b[:, columns], preferred_element_type=f32)
        at = 0
        for out in outs:
            out[:, columns] = part[at : at + out.shape[0]].astype(bf16)
            at += out.shape[0]


def down_parts(places, hidden, downs, out_rows):
    share, width = downs[0].shape
    return pl.pallas_call(
        functools.partial(down_kernel, places=places, chunk=1536),
        out_shape=[shape((rows, width), bf16) for rows in out_rows],
        compiler_params=params(),
        cost_estimate=cost(4 * sum(out_rows) * share * width, 4 * share * width),
    )(*hidden, *downs)


def join_kernel(before, after, got_before, got_after, before_ref, after_ref, *, chunk):
    half = got_before.shape[0]

    @pl.loop(0, before.shape[1] // chunk)
    def _(step):
        columns = pl.ds(pl.multiple_of(step * chunk, chunk), chunk)
        first_half = before[:half, columns].astype(f32) + got_before[:, columns].astype(f32)
        before_ref[:half, columns] = first_half.astype(bf16)
        before_ref[half:, columns] = before[half:, columns]
        after_ref[:half, columns] = after[:half, columns]
        second_half = after[half:, columns].astype(f32) + got_after[:, columns].astype(f32)
        after_ref[half:, columns] = second_half.astype(bf16)


def join(before, after, got_before, got_after):
    return pl.pallas_call(
        functools.partial(join_kernel, chunk=1024),
        out_shape=[shape(before.shape, bf16)] * 2,
        compiler_params=params(),
        cost_estimate=cost(before.size, 10 * before.size),
    )(before, after, got_before, got_after)


def line_sum_kernel(own_ref, before_ref, after_ref, *outs):
    total = own_ref[...].astype(f32) + before_ref[...].astype(f32) + after_ref[...].astype(f32)
    rows = outs[0].shape[0]
    for j, out in enumerate(outs):
        out[...] = total[j * rows : (j + 1) * rows].astype(bf16)


def line_sum(parts):
    tile = 1536
    rows, width = parts[0].shape
    return pl.pallas_call(
        line_sum_kernel,
        grid=(width // tile,),
        in_specs=[pl.BlockSpec((rows, tile), lambda n: (0, n))] * 3,
        out_specs=[pl.BlockSpec((rows // 4, tile), lambda n: (0, n))] * 4,
        out_shape=[shape((rows // 4, width), bf16)] * 4,
        compiler_params=params(),
        cost_estimate=cost(3 * rows * width, 8 * rows * width),
    )(*parts)


def expert_sum_kernel(a, b, c, d, out_ref, *, chunk):
    @pl.loop(0, out_ref.shape[2] // chunk)
    def _(step):
        columns = pl.ds(pl.multiple_of(step * chunk, chunk), chunk)
        total = (
            a[:, columns].astype(f32)
            + b[:, columns].astype(f32)
            + c[:, columns].astype(f32)
            + d[:, columns].astype(f32)
        )
        for e in range(NZ):
            out_ref[e, :, columns] = total[SLOTS * e : SLOTS * e + SLOTS].astype(bf16)


def expert_sum(parts):
    width = parts[0].shape[1]
    return pl.pallas_call(
        functools.partial(expert_sum_kernel, chunk=512),
        out_shape=shape((NZ, SLOTS, width), bf16),
        compiler_params=params(),
        cost_estimate=cost(96 * width, 240 * width),
    )(*parts)


def combine_kernel(weights_ref, rows_ref, resid_ref, gain_ref, out_ref):
    mixed = resid_ref[...].astype(f32)
    weights = weights_ref[...]
    for e in range(NZ):
        rows = rows_ref[e].astype(f32)
        for s in range(SLOTS):
            slot = SLOTS * e + s
            mixed += weights[:, slot : slot + 1] * rows[s : s + 1]
    mean_square = jnp.mean(mixed * mixed, axis=-1, keepdims=True)
    out_ref[...] = (mixed * lax.rsqrt(mean_square + epsilon) * gain_ref[...]).astype(bf16)


def combine(weights, rows, resid, gain):
    return pl.pallas_call(
        combine_kernel,
        out_shape=shape(resid.shape, bf16),
        compiler_params=params(),
        cost_estimate=cost(48 * resid.size, 8 * resid.size),
    )(weights, rows, resid, gain)


def head_kernel(place_ref, targets_ref, r0, r1, r2, r3, *refs, chunk):
    *tables, out_ref, total = refs
    total[...] = jnp.zeros_like(total)
    share, width = tables[0].shape
    count = total.shape[1]

    @pl.loop(0, width // chunk)
    def _(step):
        columns = pl.ds(pl.multiple_of(step * chunk, chunk), chunk)
        rows = jnp.concatenate([r[:, columns] for r in (r0, r1, r2, r3)])
        at = 0
        for table in tables:
            total[at : at + table.shape[0]] += lax.dot_general(
                table[:, columns], rows, (((1,), (1,)), ((), ())), preferred_element_type=f32
            )
            at += table.shape[0]

    z, x, c = place_ref[0], place_ref[1], place_ref[2]
    row = iota((count, 1), 0)
    outer, inner, token = rel_step(row // 32), rel_step(row // 8 % 4), row % 8
    z_half = (z // 2 + 4 + inner) % 4
    x_seen = (x + 4 + outer) % 4
    place = (z_half * NX + x_seen) * 8 + token
    position = ((2 * z_half + z % 2) * NX + x_seen) * (NC * 8) + c * 8 + token
    targets = targets_ref[...]
    wanted = jnp.sum(
        jnp.where(position == iota((count, targets.shape[1]), 1), targets, 0),
        axis=1,
        keepdims=True,
    )
    same = iota((count, count), 0) == iota((count, count), 1)
    here = place == iota((count, count), 1)
    wanted = jnp.sum(jnp.where(same, wanted, 0), axis=0, keepdims=True)
    logits = total[...]
    half = share // 2
    entry = iota((4 * share, 1), 0)
    part = entry // half
    shared, upper = part >= 4, part >= 6
    z_of = jnp.where(shared, (z + NZ + jnp.where(upper, 1, -1)) % NZ, z)
    other = jnp.where(shared, part % 2, jnp.where(part >= 2, 1, 0))
    c_of = c + other * (1 - 2 * c)
    offset = jnp.where(
        shared, entry % half + jnp.where(upper, half, 0), entry % share
    )
    entry_id = ((z_of * NX + x) * NC + c_of) * share + offset
    top = jnp.max(logits, axis=0, keepdims=True)
    spread = jnp.sum(jnp.exp(logits - top), axis=0, keepdims=True)
    hit = jnp.sum(jnp.where(wanted == entry_id, logits, 0.0), axis=0, keepdims=True)
    figures = []
    for value in (top + jnp.log(spread), hit):
        column = jnp.sum(jnp.where(same, value, 0.0), axis=1, keepdims=True)
        figures.append(jnp.sum(jnp.where(here, column, 0.0), axis=0, keepdims=True))
    figures = jnp.concatenate(figures)
    for peer in range(out_ref.shape[0]):
        out_ref[peer] = figures


def head(place, targets, rows, tables):
    width = rows[0].shape[1]
    entries = sum(t.shape[0] for t in tables)
    count = sum(r.shape[0] for r in rows)
    smem, vmem = (pl.BlockSpec(memory_space=space) for space in (pltpu.SMEM, pltpu.VMEM))
    return pl.pallas_call(
        functools.partial(head_kernel, chunk=3072),
        in_specs=[smem] + [vmem] * (1 + len(rows) + len(tables)),
        out_shape=shape((NZ * NX * NC, 2, count), f32),
        scratch_shapes=[pltpu.VMEM((entries, count), f32)],
        compiler_params=params(),
        cost_estimate=cost(2 * count * entries * width, 2 * entries * width),
    )(place, targets, *rows, *tables)


def hold_kernel(*refs, count):
    sources, kept, sems = refs[:count], refs[count : 2 * count], refs[2 * count]
    copies = [
        pltpu.make_async_copy(source, keep, sems.at[j])
        for j, (source, keep) in enumerate(zip(sources, kept))
    ]
    for copy in copies:
        copy.start()
    for copy in copies:
        copy.wait()


def hold(arrays):
    count = len(arrays)
    return pl.pallas_call(
        functools.partial(hold_kernel, count=count),
        in_specs=[pl.BlockSpec(memory_space=pl.ANY)] * count,
        out_specs=[pl.BlockSpec(memory_space=pltpu.VMEM)] * count,
        out_shape=[pltpu.VMEM(a.shape, a.dtype) for a in arrays],
        scratch_shapes=[pltpu.SemaphoreType.DMA((count,))],
        compiler_params=params(),
        cost_estimate=cost(0, sum(2 * a.size for a in arrays)),
    )(*arrays)


def finish_kernel(place_ref, stats_ref, lengths_ref, questions_ref, logprob_ref, prob_ref):
    z, x, c = place_ref[0], place_ref[1], place_ref[2]
    count = lengths_ref.shape[1]
    local = stats_ref.shape[2]
    lengths = lengths_ref[...].astype(f32)
    questions = questions_ref[...].astype(f32)
    square = (count, count)
    same_place = iota(square, 0) == iota(square, 1)
    ends = jnp.sum(
        jnp.where(iota(square, 1) <= iota(square, 0), lengths, 0.0), axis=1, keepdims=True
    )

    def as_column(line):
        return jnp.sum(jnp.where(same_place, line, 0.0), axis=1, keepdims=True)

    def as_line(column):
        return jnp.sum(jnp.where(same_place, column, 0.0), axis=0, keepdims=True)

    length_column = as_column(lengths)
    starts = ends - length_column
    lane = iota((1, local), 1)
    choice_total = jnp.zeros((count, 1), f32)
    own = jnp.zeros((1, local), f32)
    for parity in range(2):
        for core in range(NC):
            senders = [
                (zz * NX + xx) * NC + core for zz in range(parity, NZ, 2) for xx in range(NX)
            ]
            figures = [stats_ref[j] for j in senders]
            best = functools.reduce(jnp.maximum, [f[0:1] for f in figures])
            summed = sum(jnp.exp(f[0:1] - best) for f in figures)
            logprob = sum(f[1:2] for f in figures) - (best + jnp.log(summed))
            position = (
                (2 * (lane // 32) + parity) * (NX * NC * 8)
                + lane // 8 % 4 * (NC * 8)
                + core * 8
                + lane % 8
            ).astype(f32)
            member = (position >= starts) & (position < ends)
            choice_total += jnp.sum(jnp.where(member, logprob, 0.0), axis=1, keepdims=True)
            mine = (z % 2 == parity) & (c == core)
            own += jnp.where(mine, logprob, 0.0)
    tokens = logprob_ref.shape[1]
    first = (z // 2 * NX + x) * tokens
    column = jnp.sum(
        jnp.where(iota((tokens, local), 1) == first + iota((tokens, local), 0), own, 0.0),
        axis=1,
        keepdims=True,
    )
    eye = iota((tokens, tokens), 0) == iota((tokens, tokens), 1)
    logprob_ref[...] = jnp.sum(jnp.where(eye, column, 0.0), axis=0, keepdims=True)

    average = choice_total / length_column
    same_question = as_column(questions) == questions
    top = jnp.max(
        jnp.where(same_question, as_line(average), -jnp.inf), axis=1, keepdims=True
    )
    raised = jnp.exp(average - top)
    denominator = jnp.sum(
        jnp.where(same_question, as_line(raised), 0.0), axis=1, keepdims=True
    )
    prob_ref[...] = as_line(raised / denominator)


def finish(place, stats, lengths, questions, tokens):
    smem, vmem = (pl.BlockSpec(memory_space=space) for space in (pltpu.SMEM, pltpu.VMEM))
    return pl.pallas_call(
        finish_kernel,
        in_specs=[smem, vmem, vmem, vmem],
        out_shape=(shape((1, tokens), f32), shape(lengths.shape, f32)),
        compiler_params=params(),
    )(place, stats, lengths, questions)


def on_device(
    resid,
    moe_gain,
    final_gain,
    router,
    w_gate,
    w_up,
    w_down,
    lm_head,
    expert_ids,
    target_ids,
    choice_len,
    choice_question,
):
    own_gate, own_up, own_down = w_gate[0], w_up[0], w_down[0]
    z_index = lax.axis_index("expert")
    v_index = lax.axis_index("vocab")
    place = jnp.stack([z_index, v_index // NC, v_index % NC]).astype(i32)

    other_gate = swap_cores(own_gate)
    other_up = swap_cores(own_up)
    other_down = swap_cores(own_down)
    other_head = swap_cores(lm_head)

    buckets = bucket_rows(expert_ids[0], resid[0], moe_gain.reshape(1, -1))
    arrived = lax.all_to_all(buckets, "expert", split_axis=0, concat_axis=0, tiled=True)
    arrived, other_gate, other_up, other_down, other_head, own_head, router = tied(
        arrived, other_gate, other_up, other_down, other_head, lm_head, router
    )
    combine_weights = slot_gates(expert_ids[0], resid[0], moe_gain.reshape(1, -1), router.T)
    head_half = own_head.shape[0] // 2
    low_head = z_shift(own_head[:head_half], 1)
    high_head = z_shift(own_head[head_half:], -1)

    def first(block, shift):
        return plane_shift(block, False, shift)

    def second(block, shift):
        return plane_shift(block, True, shift)

    line = stack(gather_four(arrived, first))
    rows = line.shape[0]
    half = rows // 2
    from_before = second(line, 1)
    from_after = second(line, -1)
    weights = hold(tied(line, own_gate, own_up, other_gate, other_up)[1:])
    from_before, from_after, combine_weights, *weights = tied(
        from_before, from_after, combine_weights, *weights
    )
    far_before = second(from_before[:half], 1)
    far_after = second(from_after[half:], -1)
    near_hidden = expand([line, from_before, from_after], weights)
    downs = hold(tied(near_hidden, own_down, other_down)[1:])
    near_hidden, far_before, far_after, *downs = tied(
        near_hidden, far_before, far_after, *downs
    )
    far_hidden = expand([far_before, far_after], weights)

    hidden = (near_hidden, far_hidden)
    to_before, to_after = down_parts((3,), hidden, downs, (half, half))
    before_part, after_part = down_parts((1, 2), hidden, downs, (rows, rows))
    got_before = first(to_before, -1)
    got_after = first(to_after, 1)
    got_before, low_head, high_head = tied(got_before, low_head, high_head)
    before_part, after_part = join(before_part, after_part, got_before, got_after)
    (own_part,) = down_parts((0,), hidden, downs, (rows,))
    own_part, low_head, high_head = tied(own_part, low_head, high_head)
    low_other = swap_cores(low_head)
    high_other = swap_cores(high_head)
    pieces = line_sum([own_part, first(before_part, -1), first(after_part, 1)])
    back = (second(pieces[1], -1), second(pieces[2], 1), second(pieces[3], 2))
    outgoing = expert_sum([pieces[0], *back])

    returned = lax.all_to_all(outgoing, "expert", split_axis=0, concat_axis=0, tiled=True)
    normed_out = combine(combine_weights, returned, resid[0], final_gain.reshape(1, -1))

    head_line = stack(gather_four(normed_out, lambda b, s: head_shift(b, False, s)))
    head_rows = gather_four(head_line, lambda b, s: head_shift(b, True, s))
    stats = head(place, target_ids, head_rows, hold([lm_head, other_head, low_head, low_other, high_head, high_other]))
    gathered = lax.all_to_all(stats, ("expert", "vocab"), 0, 0, tiled=True)
    return finish(place, gathered, choice_len, choice_question, resid.shape[1])


def solution(mesh):
    return jax.shard_map(
        on_device,
        mesh=mesh,
        in_specs=(
            P("batch", ("expert", "vocab"), None),
            P(),
            P(),
            P(),
            P("expert", None, ("vocab", "batch")),
            P("expert", None, ("vocab", "batch")),
            P("expert", ("vocab", "batch"), None),
            P(("expert", "vocab"), None),
            P("batch", ("expert", "vocab"), None),
            P("batch", None),
            P("batch", None),
            P("batch", None),
        ),
        out_specs=(P("batch", ("expert", "vocab")), P("batch", None)),
        check_vma=False,
    )
```

```python
import functools

import jax
import jax.numpy as jnp
from jax import lax
from jax.experimental import pallas as pl
from jax.experimental.pallas import tpu as pltpu
from jax.sharding import PartitionSpec as P

epsilon = 1e-05
bf16 = jnp.bfloat16
f32 = jnp.float32
i32 = jnp.int32

NZ, NX, NC, NY = 8, 4, 2, 4
SLOTS = 3
VMEM_LIMIT = 16 * 2**20


def two_axis_perm(sizes, coords, axis_of, shift):
    pairs = []
    for index in range(sizes):
        place = coords(index)
        axis, step, size = axis_of(place)
        to = dict(place)
        to[axis] = (place[axis] + shift * step) % size
        pairs.append((index, coords(to)))
    return pairs


def plane_coords(index):
    if isinstance(index, dict):
        return (index["x"] * NC + index["c"]) * NY + index["y"]
    return {"x": index // (NC * NY), "c": index // NY % NC, "y": index % NY}


def head_coords(index):
    if isinstance(index, dict):
        return (index["z"] * NX + index["x"]) * NC + index["c"]
    return {"z": index // (NX * NC), "x": index // NC % NX, "c": index % NC}


def plane_shift(array, second, shift):
    def axis_of(place):
        return ("x", 1, NX) if (place["c"] == 0) != second else ("y", 1, NY)

    perm = two_axis_perm(NX * NC * NY, plane_coords, axis_of, shift)
    return lax.ppermute(array, ("vocab", "batch"), perm)


def head_shift(array, second, shift):
    def axis_of(place):
        return ("x", 1, NX) if second else ("z", 2, NZ)

    perm = two_axis_perm(NZ * NX * NC, head_coords, axis_of, shift)
    return lax.ppermute(array, ("expert", "vocab"), perm)


def swap_cores(array):
    return lax.ppermute(array, "vocab", [(v, v ^ 1) for v in range(NX * NC)])


def z_shift(array, shift):
    return lax.ppermute(array, "expert", [(z, (z + shift) % NZ) for z in range(NZ)])


def gather_four(block, shift_by):
    return [block, shift_by(block, 1), shift_by(block, -1), shift_by(block, 2)]


def rel_step(rel):
    return jnp.where(rel == 1, -1, jnp.where(rel == 2, 1, jnp.where(rel == 3, 2, 0)))


def tied(*arrays):
    return lax.optimization_barrier(arrays)


def shape(dims, dtype):
    return jax.ShapeDtypeStruct(dims, dtype)


def iota(dims, axis):
    return lax.broadcasted_iota(i32, dims, axis)


def params():
    return pltpu.CompilerParams(vmem_limit_bytes=VMEM_LIMIT)


def cost(flops, moved):
    return pl.CostEstimate(flops=flops, bytes_accessed=moved, transcendentals=0)


def normed_rows(resid_ref, gain_ref):
    values = resid_ref[...].astype(f32)
    mean_square = jnp.mean(values * values, axis=-1, keepdims=True)
    return (values * lax.rsqrt(mean_square + epsilon) * gain_ref[...]).astype(bf16)


def slots(ids, width):
    tokens = ids.shape[0]
    earlier = (iota((tokens, tokens), 0) > iota((tokens, tokens), 1)).astype(f32)
    column = iota((tokens, NZ * width), 1)
    owner, slot = column // width, column % width
    match_a, match_b = ids[:, 0:1] == owner, ids[:, 1:2] == owner
    named = (match_a | match_b).astype(f32)
    rank = jnp.dot(earlier, named, preferred_element_type=f32)
    chosen = named * (rank == slot.astype(f32)).astype(f32)
    return chosen, match_a, match_b


def bucket_kernel(ids_ref, resid_ref, gain_ref, buckets_ref):
    chosen, _, _ = slots(ids_ref[...], 8)
    rows = lax.dot_general(
        chosen.astype(bf16),
        normed_rows(resid_ref, gain_ref),
        (((0,), (0,)), ((), ())),
        preferred_element_type=f32,
    )
    for e in range(NZ):
        buckets_ref[e] = rows[8 * e : 8 * e + SLOTS].astype(bf16)


def bucket_rows(ids, resid, gain):
    tokens, width = resid.shape
    return pl.pallas_call(
        bucket_kernel,
        out_shape=shape((NZ, SLOTS, width), bf16),
        compiler_params=params(),
        cost_estimate=cost(2 * 64 * tokens * width, 8 * width),
    )(ids, resid, gain)


def gate_kernel(ids_ref, resid_ref, gain_ref, router_ref, weights_ref):
    logits = lax.dot_general(
        normed_rows(resid_ref, gain_ref),
        router_ref[...],
        (((1,), (1,)), ((), ())),
        preferred_element_type=f32,
    )
    ids = ids_ref[...]
    chosen, match_a, match_b = slots(ids, SLOTS)
    entry = iota(logits.shape, 1)
    pick_a = jnp.sum(jnp.where(ids[:, 0:1] == entry, logits, 0.0), axis=1, keepdims=True)
    pick_b = jnp.sum(jnp.where(ids[:, 1:2] == entry, logits, 0.0), axis=1, keepdims=True)
    gate_a = 1.0 / (1.0 + jnp.exp(pick_b - pick_a))
    gate_b = 1.0 / (jnp.exp(pick_a - pick_b) + 1.0)
    weights_ref[...] = chosen * (
        jnp.where(match_a, gate_a, 0.0) + jnp.where(match_b, gate_b, 0.0)
    )


def slot_gates(ids, resid, gain, router):
    tokens, width = resid.shape
    return pl.pallas_call(
        gate_kernel,
        out_shape=shape((tokens, NZ * SLOTS), f32),
        compiler_params=params(),
        cost_estimate=cost(16 * tokens * width, 8 * width),
    )(ids, resid, gain, router)


def stack_kernel(*refs, chunk):
    *parts, out_ref = refs
    width = out_ref.shape[1]

    @pl.loop(0, width // chunk)
    def _(step):
        columns = pl.ds(pl.multiple_of(step * chunk, chunk), chunk)
        pieces = []
        for part in parts:
            if len(part.shape) == 3:
                pieces += [part[e, :, columns].astype(f32) for e in range(part.shape[0])]
            else:
                pieces.append(part[:, columns].astype(f32))
        out_ref[:, columns] = jnp.concatenate(pieces).astype(bf16)


def stack(parts):
    width = parts[0].shape[-1]
    rows = sum(part.size // width for part in parts)
    return pl.pallas_call(
        functools.partial(stack_kernel, chunk=512),
        out_shape=shape((rows, width), bf16),
        compiler_params=params(),
        cost_estimate=cost(0, 4 * rows * width),
    )(*parts)


def expand_kernel(*refs, count, chunk):
    rows = refs[:count]
    gate_a, up_a, gate_b, up_b, out_ref, total = refs[count:]
    total[...] = jnp.zeros_like(total)

    @pl.loop(0, rows[0].shape[1] // chunk)
    def _(step):
        columns = pl.ds(pl.multiple_of(step * chunk, chunk), chunk)
        block = jnp.concatenate([ref[:, columns] for ref in rows])
        for j, weight in enumerate((gate_a, up_a, gate_b, up_b)):
            total[j] += jnp.dot(block, weight[columns, :], preferred_element_type=f32)

    share = total.shape[2]
    for j in range(2):
        gate = total[2 * j]
        out_ref[:, j * share : (j + 1) * share] = (
            gate / (1.0 + jnp.exp(-gate)) * total[2 * j + 1]
        ).astype(bf16)


def expand(rows, weights):
    count = len(rows)
    each, width = rows[0].shape
    share = weights[0].shape[1]
    return pl.pallas_call(
        functools.partial(expand_kernel, count=count, chunk=width if count == 2 else 1536),
        out_shape=shape((count * each, 2 * share), bf16),
        scratch_shapes=[pltpu.VMEM((4, count * each, share), f32)],
        compiler_params=params(),
        cost_estimate=cost(8 * count * each * width * share, 8 * width * share),
    )(*rows, *weights)


def rows_from(near_ref, far_ref, places):
    near, far = near_ref[...].astype(f32), far_ref[...].astype(f32)
    block = far.shape[0]
    each = block // 4
    pieces = []
    for place in places:
        at = place * each
        pieces += [near[q * block + at : q * block + at + each] for q in range(3)]
        pieces.append(far[at : at + each])
    return jnp.concatenate(pieces).astype(bf16)


def down_kernel(near_ref, far_ref, down_a, down_b, *outs, places, chunk):
    rows = rows_from(near_ref, far_ref, places)
    share, width = down_a.shape

    @pl.loop(0, width // chunk)
    def _(step):
        columns = pl.ds(pl.multiple_of(step * chunk, chunk), chunk)
        part = jnp.dot(rows[:, :share], down_a[:, columns], preferred_element_type=f32)
        part += jnp.dot(rows[:, share:], down_b[:, columns], preferred_element_type=f32)
        at = 0
        for out in outs:
            out[:, columns] = part[at : at + out.shape[0]].astype(out.dtype)
            at += out.shape[0]


def down_parts(places, hidden, downs, out_rows, dtype):
    share, width = downs[0].shape
    return pl.pallas_call(
        functools.partial(down_kernel, places=places, chunk=1536),
        out_shape=[shape((rows, width), dtype) for rows in out_rows],
        compiler_params=params(),
        cost_estimate=cost(4 * sum(out_rows) * share * width, 4 * share * width),
    )(*hidden, *downs)


def join_kernel(before, after, got_before, got_after, before_ref, after_ref, *, chunk):
    half = got_before.shape[0]

    @pl.loop(0, before.shape[1] // chunk)
    def _(step):
        columns = pl.ds(pl.multiple_of(step * chunk, chunk), chunk)
        first_half = before[:half, columns] + got_before[:, columns].astype(f32)
        before_ref[:half, columns] = first_half.astype(bf16)
        before_ref[half:, columns] = before[half:, columns].astype(bf16)
        after_ref[:half, columns] = after[:half, columns].astype(bf16)
        second_half = after[half:, columns] + got_after[:, columns].astype(f32)
        after_ref[half:, columns] = second_half.astype(bf16)


def join(before, after, got_before, got_after):
    return pl.pallas_call(
        functools.partial(join_kernel, chunk=1024),
        out_shape=[shape(before.shape, bf16)] * 2,
        compiler_params=params(),
        cost_estimate=cost(before.size, 10 * before.size),
    )(before, after, got_before, got_after)


def line_sum_kernel(own_ref, before_ref, after_ref, *outs):
    total = own_ref[...].astype(f32) + before_ref[...].astype(f32) + after_ref[...].astype(f32)
    rows = outs[0].shape[0]
    for j, out in enumerate(outs):
        out[...] = total[j * rows : (j + 1) * rows].astype(bf16)


def line_sum(parts):
    tile = 1536
    rows, width = parts[0].shape
    return pl.pallas_call(
        line_sum_kernel,
        grid=(width // tile,),
        in_specs=[pl.BlockSpec((rows, tile), lambda n: (0, n))] * 3,
        out_specs=[pl.BlockSpec((rows // 4, tile), lambda n: (0, n))] * 4,
        out_shape=[shape((rows // 4, width), bf16)] * 4,
        compiler_params=params(),
        cost_estimate=cost(3 * rows * width, 8 * rows * width),
    )(*parts)


def expert_sum_kernel(a, b, c, d, out_ref, *, chunk):
    @pl.loop(0, out_ref.shape[2] // chunk)
    def _(step):
        columns = pl.ds(pl.multiple_of(step * chunk, chunk), chunk)
        total = (
            a[:, columns].astype(f32)
            + b[:, columns].astype(f32)
            + c[:, columns].astype(f32)
            + d[:, columns].astype(f32)
        )
        for e in range(NZ):
            out_ref[e, :, columns] = total[SLOTS * e : SLOTS * e + SLOTS].astype(bf16)


def expert_sum(parts):
    width = parts[0].shape[1]
    return pl.pallas_call(
        functools.partial(expert_sum_kernel, chunk=512),
        out_shape=shape((NZ, SLOTS, width), bf16),
        compiler_params=params(),
        cost_estimate=cost(96 * width, 240 * width),
    )(*parts)


def combine_kernel(weights_ref, rows_ref, resid_ref, gain_ref, out_ref):
    mixed = resid_ref[...].astype(f32)
    weights = weights_ref[...]
    for e in range(NZ):
        rows = rows_ref[e].astype(f32)
        for s in range(SLOTS):
            slot = SLOTS * e + s
            mixed += weights[:, slot : slot + 1] * rows[s : s + 1]
    mean_square = jnp.mean(mixed * mixed, axis=-1, keepdims=True)
    out_ref[...] = (mixed * lax.rsqrt(mean_square + epsilon) * gain_ref[...]).astype(bf16)


def combine(weights, rows, resid, gain):
    return pl.pallas_call(
        combine_kernel,
        out_shape=shape(resid.shape, bf16),
        compiler_params=params(),
        cost_estimate=cost(48 * resid.size, 8 * resid.size),
    )(weights, rows, resid, gain)


def head_kernel(place_ref, targets_ref, r0, r1, r2, r3, *refs, chunk):
    *tables, out_ref, total = refs
    total[...] = jnp.zeros_like(total)
    share, width = tables[0].shape
    count = total.shape[1]

    @pl.loop(0, width // chunk)
    def _(step):
        columns = pl.ds(pl.multiple_of(step * chunk, chunk), chunk)
        rows = jnp.concatenate([r[:, columns] for r in (r0, r1, r2, r3)])
        at = 0
        for table in tables:
            total[at : at + table.shape[0]] += lax.dot_general(
                table[:, columns], rows, (((1,), (1,)), ((), ())), preferred_element_type=f32
            )
            at += table.shape[0]

    z, x, c = place_ref[0], place_ref[1], place_ref[2]
    row = iota((count, 1), 0)
    outer, inner, token = rel_step(row // 32), rel_step(row // 8 % 4), row % 8
    z_half = (z // 2 + 4 + inner) % 4
    x_seen = (x + 4 + outer) % 4
    place = (z_half * NX + x_seen) * 8 + token
    position = ((2 * z_half + z % 2) * NX + x_seen) * (NC * 8) + c * 8 + token
    targets = targets_ref[...]
    wanted = jnp.sum(
        jnp.where(position == iota((count, targets.shape[1]), 1), targets, 0),
        axis=1,
        keepdims=True,
    )
    same = iota((count, count), 0) == iota((count, count), 1)
    here = place == iota((count, count), 1)
    wanted = jnp.sum(jnp.where(same, wanted, 0), axis=0, keepdims=True)
    logits = total[...]
    half = share // 2
    entry = iota((4 * share, 1), 0)
    part = entry // half
    shared, upper = part >= 4, part >= 6
    z_of = jnp.where(shared, (z + NZ + jnp.where(upper, 1, -1)) % NZ, z)
    other = jnp.where(shared, part % 2, jnp.where(part >= 2, 1, 0))
    c_of = c + other * (1 - 2 * c)
    offset = jnp.where(
        shared, entry % half + jnp.where(upper, half, 0), entry % share
    )
    entry_id = ((z_of * NX + x) * NC + c_of) * share + offset
    top = jnp.max(logits, axis=0, keepdims=True)
    spread = jnp.sum(jnp.exp(logits - top), axis=0, keepdims=True)
    hit = jnp.sum(jnp.where(wanted == entry_id, logits, 0.0), axis=0, keepdims=True)
    figures = []
    for value in (top + jnp.log(spread), hit):
        column = jnp.sum(jnp.where(same, value, 0.0), axis=1, keepdims=True)
        figures.append(jnp.sum(jnp.where(here, column, 0.0), axis=0, keepdims=True))
    figures = jnp.concatenate(figures)
    for peer in range(out_ref.shape[0]):
        out_ref[peer] = figures


def head(place, targets, rows, tables):
    width = rows[0].shape[1]
    entries = sum(t.shape[0] for t in tables)
    count = sum(r.shape[0] for r in rows)
    smem, vmem = (pl.BlockSpec(memory_space=space) for space in (pltpu.SMEM, pltpu.VMEM))
    return pl.pallas_call(
        functools.partial(head_kernel, chunk=3072),
        in_specs=[smem] + [vmem] * (1 + len(rows) + len(tables)),
        out_shape=shape((NZ * NX * NC, 2, count), f32),
        scratch_shapes=[pltpu.VMEM((entries, count), f32)],
        compiler_params=params(),
        cost_estimate=cost(2 * count * entries * width, 2 * entries * width),
    )(place, targets, *rows, *tables)


def hold_kernel(*refs, count):
    sources, kept, sems = refs[:count], refs[count : 2 * count], refs[2 * count]
    copies = [
        pltpu.make_async_copy(source, keep, sems.at[j])
        for j, (source, keep) in enumerate(zip(sources, kept))
    ]
    for copy in copies:
        copy.start()
    for copy in copies:
        copy.wait()


def hold(arrays):
    count = len(arrays)
    return pl.pallas_call(
        functools.partial(hold_kernel, count=count),
        in_specs=[pl.BlockSpec(memory_space=pl.ANY)] * count,
        out_specs=[pl.BlockSpec(memory_space=pltpu.VMEM)] * count,
        out_shape=[pltpu.VMEM(a.shape, a.dtype) for a in arrays],
        scratch_shapes=[pltpu.SemaphoreType.DMA((count,))],
        compiler_params=params(),
        cost_estimate=cost(0, sum(2 * a.size for a in arrays)),
    )(*arrays)


def finish_kernel(place_ref, stats_ref, lengths_ref, questions_ref, logprob_ref, prob_ref):
    z, x, c = place_ref[0], place_ref[1], place_ref[2]
    count = lengths_ref.shape[1]
    local = stats_ref.shape[2]
    lengths = lengths_ref[...].astype(f32)
    questions = questions_ref[...].astype(f32)
    square = (count, count)
    same_place = iota(square, 0) == iota(square, 1)
    ends = jnp.sum(
        jnp.where(iota(square, 1) <= iota(square, 0), lengths, 0.0), axis=1, keepdims=True
    )

    def as_column(line):
        return jnp.sum(jnp.where(same_place, line, 0.0), axis=1, keepdims=True)

    def as_line(column):
        return jnp.sum(jnp.where(same_place, column, 0.0), axis=0, keepdims=True)

    length_column = as_column(lengths)
    starts = ends - length_column
    lane = iota((1, local), 1)
    choice_total = jnp.zeros((count, 1), f32)
    own = jnp.zeros((1, local), f32)
    for parity in range(2):
        for core in range(NC):
            senders = [
                (zz * NX + xx) * NC + core for zz in range(parity, NZ, 2) for xx in range(NX)
            ]
            figures = [stats_ref[j] for j in senders]
            best = functools.reduce(jnp.maximum, [f[0:1] for f in figures])
            summed = sum(jnp.exp(f[0:1] - best) for f in figures)
            logprob = sum(f[1:2] for f in figures) - (best + jnp.log(summed))
            position = (
                (2 * (lane // 32) + parity) * (NX * NC * 8)
                + lane // 8 % 4 * (NC * 8)
                + core * 8
                + lane % 8
            ).astype(f32)
            member = (position >= starts) & (position < ends)
            choice_total += jnp.sum(jnp.where(member, logprob, 0.0), axis=1, keepdims=True)
            mine = (z % 2 == parity) & (c == core)
            own += jnp.where(mine, logprob, 0.0)
    tokens = logprob_ref.shape[1]
    first = (z // 2 * NX + x) * tokens
    column = jnp.sum(
        jnp.where(iota((tokens, local), 1) == first + iota((tokens, local), 0), own, 0.0),
        axis=1,
        keepdims=True,
    )
    eye = iota((tokens, tokens), 0) == iota((tokens, tokens), 1)
    logprob_ref[...] = jnp.sum(jnp.where(eye, column, 0.0), axis=0, keepdims=True)

    average = choice_total / length_column
    same_question = as_column(questions) == questions
    top = jnp.max(
        jnp.where(same_question, as_line(average), -jnp.inf), axis=1, keepdims=True
    )
    raised = jnp.exp(average - top)
    denominator = jnp.sum(
        jnp.where(same_question, as_line(raised), 0.0), axis=1, keepdims=True
    )
    prob_ref[...] = as_line(raised / denominator)


def finish(place, stats, lengths, questions, tokens):
    smem, vmem = (pl.BlockSpec(memory_space=space) for space in (pltpu.SMEM, pltpu.VMEM))
    return pl.pallas_call(
        finish_kernel,
        in_specs=[smem, vmem, vmem, vmem],
        out_shape=(shape((1, tokens), f32), shape(lengths.shape, f32)),
        compiler_params=params(),
    )(place, stats, lengths, questions)


def on_device(
    resid,
    moe_gain,
    final_gain,
    router,
    w_gate,
    w_up,
    w_down,
    lm_head,
    expert_ids,
    target_ids,
    choice_len,
    choice_question,
):
    own_gate, own_up, own_down = w_gate[0], w_up[0], w_down[0]
    z_index = lax.axis_index("expert")
    v_index = lax.axis_index("vocab")
    place = jnp.stack([z_index, v_index // NC, v_index % NC]).astype(i32)

    other_gate = swap_cores(own_gate)
    other_up = swap_cores(own_up)
    other_down = swap_cores(own_down)
    other_head = swap_cores(lm_head)

    buckets = bucket_rows(expert_ids[0], resid[0], moe_gain.reshape(1, -1))
    arrived = lax.all_to_all(buckets, "expert", split_axis=0, concat_axis=0, tiled=True)
    arrived, other_gate, other_up, other_down, other_head, own_head, router = tied(
        arrived, other_gate, other_up, other_down, other_head, lm_head, router
    )
    combine_weights = slot_gates(expert_ids[0], resid[0], moe_gain.reshape(1, -1), router.T)
    head_half = own_head.shape[0] // 2
    low_head = z_shift(own_head[:head_half], 1)
    high_head = z_shift(own_head[head_half:], -1)

    def first(block, shift):
        return plane_shift(block, False, shift)

    def second(block, shift):
        return plane_shift(block, True, shift)

    line = stack(gather_four(arrived, first))
    rows = line.shape[0]
    half = rows // 2
    from_before = second(line, 1)
    from_after = second(line, -1)
    weights = hold(tied(line, own_gate, own_up, other_gate, other_up)[1:])
    from_before, from_after, combine_weights, *weights = tied(
        from_before, from_after, combine_weights, *weights
    )
    far_before = second(from_before[:half], 1)
    far_after = second(from_after[half:], -1)
    near_hidden = expand([line, from_before, from_after], weights)
    downs = hold(tied(near_hidden, own_down, other_down)[1:])
    near_hidden, far_before, far_after, *downs = tied(
        near_hidden, far_before, far_after, *downs
    )
    far_hidden = expand([far_before, far_after], weights)

    hidden = (near_hidden, far_hidden)
    to_before, to_after = down_parts((3,), hidden, downs, (half, half), bf16)
    before_part, after_part = down_parts((1, 2), hidden, downs, (rows, rows), f32)
    got_before = first(to_before, -1)
    got_after = first(to_after, 1)
    got_before, low_head, high_head = tied(got_before, low_head, high_head)
    before_part, after_part = join(before_part, after_part, got_before, got_after)
    (own_part,) = down_parts((0,), hidden, downs, (rows,), f32)
    own_part, low_head, high_head = tied(own_part, low_head, high_head)
    low_other = swap_cores(low_head)
    high_other = swap_cores(high_head)
    pieces = line_sum([own_part, first(before_part, -1), first(after_part, 1)])
    back = (second(pieces[1], -1), second(pieces[2], 1), second(pieces[3], 2))
    outgoing = expert_sum([pieces[0], *back])

    returned = lax.all_to_all(outgoing, "expert", split_axis=0, concat_axis=0, tiled=True)
    normed_out = combine(combine_weights, returned, resid[0], final_gain.reshape(1, -1))

    head_line = stack(gather_four(normed_out, lambda b, s: head_shift(b, False, s)))
    head_rows = gather_four(head_line, lambda b, s: head_shift(b, True, s))
    stats = head(place, target_ids, head_rows, hold([lm_head, other_head, low_head, low_other, high_head, high_other]))
    gathered = lax.all_to_all(stats, ("expert", "vocab"), 0, 0, tiled=True)
    return finish(place, gathered, choice_len, choice_question, resid.shape[1])


def solution(mesh):
    return jax.shard_map(
        on_device,
        mesh=mesh,
        in_specs=(
            P("batch", ("expert", "vocab"), None),
            P(),
            P(),
            P(),
            P("expert", None, ("vocab", "batch")),
            P("expert", None, ("vocab", "batch")),
            P("expert", ("vocab", "batch"), None),
            P(("expert", "vocab"), None),
            P("batch", ("expert", "vocab"), None),
            P("batch", None),
            P("batch", None),
            P("batch", None),
        ),
        out_specs=(P("batch", ("expert", "vocab")), P("batch", None)),
        check_vma=False,
    )
```
